32 devices in a mesh: rows: 16 (over z, x, core), field: 2 (over y).
Axes of the slice: x: 2, y: 2, z: 4, core: 2. Of those that a mesh axis runs over, the one named last changes fastest.
Arguments:
- inputs: bfloat16 [4, 8192, 512], P(None, 'rows', 'field'), may hold values from -6 to 6
- valid_mask: int32 [4, 8192], P(None, 'rows'), may hold values from 0 to 1, as said below
- labels: int32 [4, 8192], P(None, 'rows'), may hold values from 0 to 1
- domains: int32 [4, 8192], P(None, 'rows'), may hold values from 0 to 1
- expert_in: float32 [512, 2048], P(('field', 'rows')), may hold values from -0.25 to 0.25
- gate_in: float32 [512, 16], P(('field', 'rows')), may hold values from -0.1875 to 0.1875
- expert_out: float32 [8, 256, 256], P(None, ('rows', 'field')), may hold values from -0.375 to 0.375
- tower_in: float32 [2, 256, 128], P(None, ('rows', 'field')), may hold values from -0.375 to 0.375
- tower_out: float32 [2, 128], replicated, may hold values from -0.5 to 0.5
- velocity_expert_in: float32 [512, 2048], P(('field', 'rows')), may hold values from -5.340576e-05 to 5.340576e-05
- velocity_gate_in: float32 [512, 16], P(('field', 'rows')), may hold values from -0.00061035156 to 0.00061035156
- velocity_expert_out: float32 [8, 256, 256], P(None, ('rows', 'field')), may hold values from -5.340576e-05 to 5.340576e-05
- velocity_tower_in: float32 [2, 256, 128], P(None, ('rows', 'field')), may hold values from -0.00030517578 to 0.00030517578
- velocity_tower_out: float32 [2, 128], replicated, may hold values from -0.0068359375 to 0.0068359375
- average_expert_in: float32 [512, 2048], P(('field', 'rows')), may hold values from -0.25 to 0.25
- average_gate_in: float32 [512, 16], P(('field', 'rows')), may hold values from -0.1875 to 0.1875
- average_expert_out: float32 [8, 256, 256], P(None, ('rows', 'field')), may hold values from -0.375 to 0.375
- average_tower_in: float32 [2, 256, 128], P(None, ('rows', 'field')), may hold values from -0.375 to 0.375
- average_tower_out: float32 [2, 128], replicated, may hold values from -0.5 to 0.5
Outputs:
- loss_mean: float32 [], replicated
- input_grad: float32 [4, 8192, 512], P(None, 'rows', 'field')
- expert_in_new: float32 [512, 2048], P(('field', 'rows'))
- velocity_expert_in_new: float32 [512, 2048], P(('field', 'rows'))
- average_expert_in_new: float32 [512, 2048], P(('field', 'rows'))
- gate_in_new: float32 [512, 16], P(('field', 'rows'))
- velocity_gate_in_new: float32 [512, 16], P(('field', 'rows'))
- average_gate_in_new: float32 [512, 16], P(('field', 'rows'))
- expert_out_new: float32 [8, 256, 256], P(None, ('rows', 'field'))
- velocity_expert_out_new: float32 [8, 256, 256], P(None, ('rows', 'field'))
- average_expert_out_new: float32 [8, 256, 256], P(None, ('rows', 'field'))
- tower_in_new: float32 [2, 256, 128], P(None, ('rows', 'field'))
- velocity_tower_in_new: float32 [2, 256, 128], P(None, ('rows', 'field'))
- average_tower_in_new: float32 [2, 256, 128], P(None, ('rows', 'field'))
- tower_out_new: float32 [2, 128], replicated
- velocity_tower_out_new: float32 [2, 128], replicated
- average_tower_out_new: float32 [2, 128], replicated
The draws below stay inside these ranges and needn't reach their ends.
Inputs may be any that keep to these rules, and one draw needn't show every extreme that they name: `valid_mask`: in the first micro-batch the first row of each block of 512 rows is real.
All inputs are finite; a program needn't handle non-finite values.
Results may differ from the reference program's by a relative error of at most 0.014.
Values may be sent and summed in bfloat16 or wider, within the bound.
No kernel may reach another device: no remote copies, remote signals or barrier semaphores. Data moves between devices by JAX's collectives and lax.ppermute only.
A program may use at most 128 MiB of HBM per device.

```python
import math
import jax
import jax.numpy as jnp
from jax import lax

D_IN = 512
E = 8
H = 256
EO = 256
TASKS = 2
TH = 128
MB = 4
ROW_DEV = 512
ROWS = 8192


def draw_valid_mask(key, part):
    key = jax.random.fold_in(key, 11)
    places = jnp.arange(ROWS, dtype=jnp.int32)
    owners = places // ROW_DEV
    final_owner = max(ROWS // ROW_DEV - 1, 1)
    bound_limit = 300 + 600 * owners // final_owner
    tickets = jax.random.randint(key, (MB, ROWS), 0, 1000)
    kept_rows = (tickets < bound_limit[None, :]).astype(jnp.int32)
    leading = (jnp.arange(MB, dtype=jnp.int32)[:, None] == 0) & (places[None, :] % ROW_DEV == 0)
    return jnp.where(leading, 1, kept_rows).astype(jnp.int32)


def plant(drawn, own_key, low, high):
    spot = [jax.random.randint(jax.random.fold_in(own_key, axis), (), 0, length) for axis, length in enumerate(drawn.shape)]
    widest = drawn.shape.index(max(drawn.shape))
    neighbour = spot[:widest] + [(spot[widest] + 1) % drawn.shape[widest]] + spot[widest + 1:]
    return drawn.at[tuple(spot)].set(low).at[tuple(neighbour)].set(high)


def level_of(own_key, extent, split, low, high):
    gain = 1.0
    for axis_at, parts in split:
        draws = jax.random.uniform(jax.random.fold_in(jax.random.fold_in(own_key, 6), axis_at), (parts,), jnp.float32, low / len(split), high / len(split))
        gain = gain * jnp.repeat(jnp.exp(draws), extent[axis_at] // parts).reshape((-1,) + (1,) * (len(extent) - 1 - axis_at))
    return gain


def noise(rng, shape, deviation, most, shards=(), held_as=jnp.bfloat16):
    entries = deviation * jax.random.normal(rng, shape, jnp.float32)
    if shards:
        entries = entries * level_of(rng, shape, shards, -0.22, 0.18)
    return jnp.clip(entries, -most, most).astype(held_as)


def setup_inputs(seed: int = 0) -> dict:
    streams_of = jax.random.split(jax.random.key(seed), 20)
    inputs = noise(streams_of[0], (MB, ROWS, D_IN), 1.0, 6.0, ((1, 16), (2, 2)))
    valid_mask = draw_valid_mask(jax.random.fold_in(streams_of[19], 71), 0)
    labels = plant(jax.random.randint(streams_of[2], (MB, ROWS), 0, 2), jax.random.fold_in(streams_of[2], 1), 0, 1).astype(jnp.int32)
    domains = plant(jax.random.randint(streams_of[3], (MB, ROWS), 0, TASKS), jax.random.fold_in(streams_of[3], 1), 0, TASKS - 1).astype(jnp.int32)
    expert_in = noise(streams_of[4], (D_IN, E * H), D_IN ** -0.5, 0.25, ((0, 32),), jnp.float32)
    gate_in = noise(streams_of[5], (D_IN, TASKS * E), (2 * D_IN) ** -0.5, 0.1875, ((0, 32),), jnp.float32)
    expert_out = noise(streams_of[6], (E, H, EO), H ** -0.5, 0.375, ((1, 32),), jnp.float32)
    tower_in = noise(streams_of[7], (TASKS, EO, TH), EO ** -0.5, 0.375, ((1, 32),), jnp.float32)
    tower_out = noise(streams_of[8], (TASKS, TH), TH ** -0.5, 0.5, (), jnp.float32)
    velocity_expert_in = noise(streams_of[9], (D_IN, E * H), (0.0015 * (MB * ROWS) ** -0.5), 5.340576171875e-05, ((0, 32),), jnp.float32)
    velocity_gate_in = noise(streams_of[10], (D_IN, TASKS * E), (0.018 * (MB * ROWS) ** -0.5), 0.00061035156, ((0, 32),), jnp.float32)
    velocity_expert_out = noise(streams_of[11], (E, H, EO), (0.0015 * (MB * ROWS) ** -0.5), 5.340576171875e-05, ((1, 32),), jnp.float32)
    velocity_tower_in = noise(streams_of[12], (TASKS, EO, TH), (0.009 * (MB * ROWS) ** -0.5), 0.00030517578, ((1, 32),), jnp.float32)
    velocity_tower_out = noise(streams_of[13], (TASKS, TH), (0.2 * (MB * ROWS) ** -0.5), 0.0068359375, (), jnp.float32)
    average_expert_in = noise(streams_of[14], (D_IN, E * H), D_IN ** -0.5, 0.25, ((0, 32),), jnp.float32)
    average_gate_in = noise(streams_of[15], (D_IN, TASKS * E), (2 * D_IN) ** -0.5, 0.1875, ((0, 32),), jnp.float32)
    average_expert_out = noise(streams_of[16], (E, H, EO), H ** -0.5, 0.375, ((1, 32),), jnp.float32)
    average_tower_in = noise(streams_of[17], (TASKS, EO, TH), EO ** -0.5, 0.375, ((1, 32),), jnp.float32)
    average_tower_out = noise(streams_of[18], (TASKS, TH), TH ** -0.5, 0.5, (), jnp.float32)
    return {"inputs": inputs, "valid_mask": valid_mask, "labels": labels, "domains": domains, "expert_in": expert_in, "gate_in": gate_in, "expert_out": expert_out, "tower_in": tower_in, "tower_out": tower_out, "velocity_expert_in": velocity_expert_in, "velocity_gate_in": velocity_gate_in, "velocity_expert_out": velocity_expert_out, "velocity_tower_in": velocity_tower_in, "velocity_tower_out": velocity_tower_out, "average_expert_in": average_expert_in, "average_gate_in": average_gate_in, "average_expert_out": average_expert_out, "average_tower_in": average_tower_in, "average_tower_out": average_tower_out}


highest = lax.Precision.HIGHEST
momentum_mu = 0.5
average_keep = 0.5
rate_bases = (17.0, 1.0, 24.0, 4.0, 0.25)

@jax.custom_vjp
def low(v):
    return lax.optimization_barrier(v.astype(jnp.bfloat16)).astype(jnp.float32)

@jax.custom_vjp
def low_back(v):
    return v

def low_keep(v):
    return (low(v), None)

def low_pass(kept, grad):
    return (grad,)

def back_keep(v):
    return (v, None)

def back_low(kept, grad):
    return (low(grad),)
low.defvjp(low_keep, low_pass)
low_back.defvjp(back_keep, back_low)

def mixture_loss(rows_x, row_valid, row_label, row_pick, valid_total, expert_in, gate_in, expert_out, tower_in, tower_out):
    block_rows = rows_x.shape[0]
    expert_pre = low_back(jnp.dot(rows_x, low(expert_in), precision=highest, preferred_element_type=jnp.float32))
    gate_pre = low_back(jnp.dot(rows_x, low(gate_in), precision=highest, preferred_element_type=jnp.float32))
    gate_prob = jax.nn.softmax(gate_pre.reshape(block_rows, TASKS, E), axis=-1)
    expert_cube = expert_pre.reshape(block_rows, E, H)
    expert_act = low(jax.nn.silu(expert_cube))
    expert_res = low_back(jnp.einsum('rkh,kho->rko', expert_act, low(expert_out), precision=highest))
    mixed_rows = low(jnp.einsum('rtk,rko->rto', gate_prob, expert_res, precision=highest))
    tower_pre = low_back(jnp.einsum('rto,tom->rtm', mixed_rows, low(tower_in), precision=highest))
    tower_act = low(jax.nn.silu(tower_pre))
    logit_rows = low_back(jnp.einsum('rtm,tm->rt', tower_act, low(tower_out), precision=highest))
    chosen = lax.optimization_barrier(jnp.sum(row_pick * logit_rows, axis=1))
    per_row = row_valid * (jax.nn.softplus(chosen) - row_label * chosen)
    return jnp.sum(per_row) / valid_total

def renew(weight, velocity, average, gradient, rate):
    velocity_new = momentum_mu * velocity + gradient
    weight_new = weight - rate * (gradient + momentum_mu * velocity_new)
    average_new = average_keep * average + (1.0 - average_keep) * weight_new
    return (weight_new, velocity_new, average_new)

def reference(inputs, valid_mask, labels, domains, expert_in, gate_in, expert_out, tower_in, tower_out, velocity_expert_in, velocity_gate_in, velocity_expert_out, velocity_tower_in, velocity_tower_out, average_expert_in, average_gate_in, average_expert_out, average_tower_in, average_tower_out):
    weights = (expert_in, gate_in, expert_out, tower_in, tower_out)
    velocities = (velocity_expert_in, velocity_gate_in, velocity_expert_out, velocity_tower_in, velocity_tower_out)
    averages = (average_expert_in, average_gate_in, average_expert_out, average_tower_in, average_tower_out)
    valid_total = jnp.sum(valid_mask.astype(jnp.float32))
    blocks = MB * ROWS // ROW_DEV
    flat_x = inputs.astype(jnp.float32).reshape(blocks, ROW_DEV, D_IN)
    flat_valid = valid_mask.reshape(blocks, ROW_DEV)
    flat_label = labels.reshape(blocks, ROW_DEV)
    flat_domain = domains.reshape(blocks, ROW_DEV)
    task_ids = jnp.arange(TASKS, dtype=jnp.int32)

    def block_step(carry, block):
        rows_x, own_valid, own_label, own_domain = block
        row_pick = (own_domain[:, None] == task_ids[None, :]).astype(jnp.float32)

        def block_loss(xb, w_one, w_two, w_three, w_four, w_five):
            return mixture_loss(xb, own_valid.astype(jnp.float32), own_label.astype(jnp.float32), row_pick, valid_total, w_one, w_two, w_three, w_four, w_five)
        loss_part, pullback = jax.vjp(block_loss, rows_x, *weights)
        grads = pullback(jnp.float32(1.0))
        new_carry = (carry[0] + loss_part,) + tuple((c + g for c, g in zip(carry[1:], grads[1:])))
        return (new_carry, grads[0])
    start_carry = (jnp.float32(0.0),) + tuple((jnp.zeros_like(w) for w in weights))
    totals, input_blocks = lax.scan(block_step, start_carry, (flat_x, flat_valid, flat_label, flat_domain))
    input_grad = input_blocks.reshape(MB, ROWS, D_IN)
    scale_root = math.sqrt(MB * ROWS)
    results = [totals[0], input_grad]
    for index_w in range(5):
        results.extend(renew(weights[index_w], velocities[index_w], averages[index_w], totals[index_w + 1], rate_bases[index_w] * scale_root))
    return tuple(results)
```

```python
import math

import jax
import jax.numpy as jnp
import numpy as np
from jax import lax
from jax.experimental import pallas as pl
from jax.experimental.pallas import tpu as pltpu
from jax.sharding import PartitionSpec as P

momentum_mu = 0.5
average_keep = 0.5
rate_bases = (17.0, 1.0, 24.0, 4.0, 0.25)
both = ("rows", "field")
f32 = jnp.float32
bf16 = jnp.bfloat16
BLOCK = 16
LANES = 128


def dot(a, b):
    return lax.dot_general(a, b, (((1,), (0,)), ((), ())), preferred_element_type=f32)


def dot_t(a, b):
    return lax.dot_general(a, b, (((1,), (1,)), ((), ())), preferred_element_type=f32)


def t_dot(a, b):
    return lax.dot_general(a, b, (((0,), (0,)), ((), ())), preferred_element_type=f32)


def sigmoid(v):
    return 0.5 + 0.5 * jnp.tanh(0.5 * v)


def rows16(start):
    return pl.ds(pl.multiple_of(start, BLOCK), BLOCK)


def each_block(tab, pairs, body):
    def step(j, carry):
        for side in range(2):
            core = tab[2 * pairs] if side == 0 else 1 - tab[2 * pairs]
            body(side, tab[side * pairs + j], 2 * (j // 2) + core, j % 2)
        return carry

    lax.fori_loop(0, pairs, step, 0, unroll=True)


def first_kernel(
    tab, own_ref, oth_ref, xo_ref, xr_ref, meta_ref, ga_ref, gs_ref, gate_ref, w_ref, cnt_ref, xt_ref
):
    pairs = own_ref.shape[0] // BLOCK
    half = xo_ref.shape[-1]
    wide = ga_ref.shape[1]
    hidden = 256 if wide % 256 == 0 else LANES
    experts = tab_experts(wide, hidden)

    @pl.when(pl.program_id(0) == 0)
    def _():
        def put(side, place, rr, ff):
            src = own_ref if side == 0 else oth_ref
            row = (ff ^ tab[2 * pairs + 1]) * half + rr * BLOCK
            w_ref[rows16(row), :] = src[rows16(place * BLOCK), :]

        each_block(tab, pairs, put)
        side_cols = w_ref[:, wide:].astype(f32)
        lane = lax.broadcasted_iota(jnp.int32, side_cols.shape, 1)
        base = 2 * experts
        scale = jnp.where(
            lane == base, 1.0, jnp.where(lane == base + 1, 256.0, jnp.where(lane == base + 2, 65536.0, 0.0))
        )
        total = jnp.sum(jnp.sum(side_cols * scale, axis=1, keepdims=True), axis=0, keepdims=True)
        cnt_ref[...] = jnp.broadcast_to(total, cnt_ref.shape)

    x = jnp.concatenate([xo_ref[0], xr_ref[...]], axis=1)
    xt_ref[...] = x.T
    meta = meta_ref[0].T
    domain = meta[:, 2:3]
    logits = dot(x, w_ref[:, wide:])
    lane = lax.broadcasted_iota(jnp.int32, logits.shape, 1)
    picked = (lane // experts).astype(f32) == domain
    top = jnp.max(jnp.where(picked, logits, -jnp.inf), axis=1, keepdims=True)
    raised = jnp.where(picked, jnp.exp(jnp.where(picked, logits, top) - top), 0.0)
    gate = raised / jnp.sum(raised, axis=1, keepdims=True)
    gate_ref[...] = gate
    gate = gate + pltpu.roll(gate, LANES - experts, axis=1)
    for k in range(experts):
        cols = pl.ds(k * hidden, hidden)
        pre = dot(x, w_ref[:, cols])
        s = sigmoid(pre)
        a = pre * s
        g = gate[:, k : k + 1]
        ga_ref[:, cols] = (g * a).astype(bf16)
        gs_ref[:, cols] = (g * (s + a * (1.0 - s))).astype(bf16)


def tab_experts(wide, hidden):
    return wide // hidden


def second_kernel(
    tab,
    own_ref,
    oth_ref,
    ga_ref,
    meta_ref,
    cnt_ref,
    to_ref,
    w_ref,
    dm_ref,
    keep_ref,
    send_ref,
    side_ref,
    ti_ref,
    gwo_ref,
    gti_ref,
):
    pairs = own_ref.shape[0] // BLOCK
    step = pl.program_id(0)
    out_cols = dm_ref.shape[1]
    hidden = pairs * BLOCK
    experts = w_ref.shape[0] // hidden
    part = experts // 2

    @pl.when(step == 0)
    def _():
        def put(side, j):
            src = own_ref if side == 0 else oth_ref
            core = tab[2 * pairs] if side == 0 else 1 - tab[2 * pairs]
            a0 = src[rows16(tab[side * pairs + 2 * j] * BLOCK), :].astype(f32)
            a1 = src[rows16(tab[side * pairs + 2 * j + 1] * BLOCK), :].astype(f32)
            row = (2 * j + core) * BLOCK
            upper = jnp.concatenate([a0[:8], a1[:8]], axis=0).astype(bf16)
            lower = jnp.concatenate([a0[8:], a1[8:]], axis=0).astype(bf16)
            for k in range(part):
                cols = slice(k * out_cols, (k + 1) * out_cols)
                w_ref[rows16(k * hidden + row), :] = upper[:, cols]
                w_ref[rows16((k + part) * hidden + row), :] = lower[:, cols]
            ti_ref[rows16(row), 0:LANES] = upper[:, part * out_cols :]
            ti_ref[rows16(row), LANES : 2 * LANES] = lower[:, part * out_cols :]

        for j in range(pairs // 2):
            put(0, j)
            put(1, j)
        gwo_ref[...] = jnp.zeros_like(gwo_ref)
        gti_ref[...] = jnp.zeros_like(gti_ref)
        side_ref[...] = jnp.zeros_like(side_ref)

    meta = meta_ref[0].T
    valid, label, domain = meta[:, 0:1], meta[:, 1:2], meta[:, 2:3]
    count = cnt_ref[0:1, 0:1]
    head = to_ref[0:1, :]
    mixed = dot(ga_ref[...], w_ref[...]).astype(bf16)
    tpre = dot(mixed, ti_ref[...])
    lane = lax.broadcasted_iota(jnp.int32, tpre.shape, 1)
    picked = (lane // LANES).astype(f32) == domain
    s = sigmoid(tpre)
    act = (tpre * s).astype(bf16).astype(f32)
    act = jnp.where(picked, act, 0.0)
    chosen = jnp.sum(act * head, axis=1, keepdims=True)
    soft = jnp.maximum(chosen, 0.0) + jnp.log1p(jnp.exp(-jnp.abs(chosen)))
    loss = jnp.sum(valid * (soft - label * chosen), axis=0, keepdims=True)
    dlogit = (valid * (sigmoid(chosen) - label) / count).astype(bf16).astype(f32)
    slope = s * (1.0 + tpre * (1.0 - s))
    dtpre = jnp.where(picked, dlogit * head * slope, 0.0).astype(bf16)
    side_ref[0:1, :] += jnp.sum(dlogit * act, axis=0, keepdims=True)
    side_ref[1:2, :] += jnp.broadcast_to(loss, (1, side_ref.shape[1]))
    gti_ref[...] += t_dot(mixed, dtpre)
    dmixed = dot_t(dtpre, ti_ref[...]).astype(bf16)
    dm_ref[...] = dmixed
    for k in range(experts):
        gwo_ref[k] += t_dot(ga_ref[:, pl.ds(k * hidden, hidden)], dmixed)

    @pl.when(step == pl.num_programs(0) - 1)
    def _():
        def put(side, place, rr, ff):
            dst = keep_ref if side == 0 else send_ref
            row = pl.ds(pl.multiple_of(rr * BLOCK + ff * 8, 8), 8)
            for k in range(part):
                cols = slice(k * out_cols, (k + 1) * out_cols)
                tile = jnp.concatenate([gwo_ref[k, row, :], gwo_ref[k + part, row, :]], axis=0)
                dst[rows16(place * BLOCK), cols] = tile.astype(dst.dtype)
            tile = gti_ref[row, :]
            tile = jnp.concatenate([tile[:, :LANES], tile[:, LANES:]], axis=0)
            dst[rows16(place * BLOCK), part * out_cols :] = tile.astype(dst.dtype)

        each_block(tab, pairs, put)


def back_kernel(
    tab,
    dm_ref,
    w_ref,
    ga_ref,
    gs_ref,
    xt_ref,
    gate_ref,
    dp_ref,
    dg_ref,
    keep_ref,
    send_ref,
    q_ref,
    gwi_ref,
):
    k = pl.program_id(0)
    experts = pl.num_programs(0)
    pairs = keep_ref.shape[0] // BLOCK
    half = keep_ref.shape[0]
    hidden = ga_ref.shape[1]
    wide = keep_ref.shape[1] - LANES

    def pack(start, width):
        def put(side, place, rr, ff):
            dst = keep_ref if side == 0 else send_ref
            row = (ff ^ tab[2 * pairs + 1]) * half + rr * BLOCK
            dst[rows16(place * BLOCK), pl.ds(start, width)] = gwi_ref[rows16(row), 0:width].astype(dst.dtype)

        each_block(tab, pairs, put)

    u = dot_t(dm_ref[...], w_ref[...])
    dpre = (u * gs_ref[...].astype(f32)).astype(bf16)
    dp_ref[...] = dpre
    q = jnp.sum(u * ga_ref[...].astype(f32), axis=1, keepdims=True)
    lane = lax.broadcasted_iota(jnp.int32, q_ref.shape, 1)
    mine = (lane == k) | (lane == k + experts)
    q_ref[...] = jnp.where(mine, q, jnp.where(k == 0, 0.0, q_ref[...]))
    gwi_ref[...] = dot(xt_ref[...], dpre)
    pack(pl.multiple_of(k * hidden, hidden), hidden)

    @pl.when(k == experts - 1)
    def _():
        q = q_ref[...]
        gate = gate_ref[...]
        total = jnp.sum(jnp.where(lane < experts, q, 0.0), axis=1, keepdims=True)
        dgate = jnp.where(gate_ref[...] != 0.0, q, 0.0) - gate * total
        dgate = dgate.astype(bf16)
        dg_ref[...] = dgate
        gwi_ref[:, 0:LANES] = dot(xt_ref[...], dgate)
        pack(wide, LANES)


def input_kernel(tab, dp_ref, dg_ref, w_ref, keep_ref, send_ref):
    wide = dp_ref.shape[1]
    grad = dot_t(dp_ref[...], w_ref[:, 0:wide]) + dot_t(dg_ref[...], w_ref[:, wide:])
    half = grad.shape[1] // 2
    keep_ref[0] = grad[:, :half]
    send_ref[...] = grad[:, half:].astype(bf16)


class Cube:
    def __init__(self):
        self.rows = lax.axis_size("rows")
        self.fields = lax.axis_size("field")
        self.bits = int(math.log2(self.rows))
        assert 1 << self.bits == self.rows and self.fields == 2
        self.outer = self.bits - 2
        steps = [self.flip_row(b) for b in range(self.bits - 1, 1, -1)]
        steps += [self.flip_mixed(0), self.flip_mixed(1)]
        self.steps = steps
        self.core = self.flip_row(0)

    def table(self, partner):
        pairs = []
        for r in range(self.rows):
            for f in range(self.fields):
                rr, ff = partner(r, f)
                pairs.append((r * self.fields + f, rr * self.fields + ff))
        return pairs

    def flip_row(self, bit):
        return self.table(lambda r, f: (r ^ (1 << bit), f))

    def flip_mixed(self, turn):
        return self.table(lambda r, f: (r ^ 2, f) if (r & 1) == turn else (r, f ^ 1))

    def place(self, rr, ff, r, f):
        dr, df, core = rr ^ r, ff ^ f, r & 1
        out = jnp.zeros_like(dr)
        for s in range(self.outer):
            out = out + (((dr >> (self.bits - 1 - s)) & 1) << s)
        xbit = (dr >> 1) & 1
        low = jnp.where(core == 0, xbit, df)
        high = jnp.where(core == 0, df, xbit)
        return out + (low << self.outer) + (high << (self.outer + 1))


def gather(cube, block):
    for pairs in cube.steps:
        block = jnp.concatenate([block, lax.ppermute(block, both, pairs)], axis=0)
    return block, lax.ppermute(block, both, cube.core)


def scatter(cube, keep, send):
    total = keep + lax.ppermute(send, both, cube.core).astype(f32)
    for pairs in reversed(cube.steps):
        half = total.shape[0] // 2
        got = lax.ppermute(total[half:].astype(bf16), both, pairs)
        total = total[:half] + got.astype(f32)
    return total


def sum_all(cube, part):
    for pairs in [cube.core] + cube.steps:
        part = part + lax.ppermute(part, both, pairs)
    return part


def renew(weight, velocity, average, gradient, rate):
    velocity_new = momentum_mu * velocity + gradient
    weight_new = weight - rate * (gradient + momentum_mu * velocity_new)
    average_new = average_keep * average + (1.0 - average_keep) * weight_new
    return (weight_new, velocity_new, average_new)


def shape(dims, dtype):
    return jax.ShapeDtypeStruct(dims, dtype)


def whole(dims):
    return pl.BlockSpec(dims, lambda i, tab: (0,) * len(dims))


def params(limit=48):
    return pltpu.CompilerParams(vmem_limit_bytes=limit << 20)


def on_device(
    inputs,
    valid_mask,
    labels,
    domains,
    expert_in,
    gate_in,
    expert_out,
    tower_in,
    tower_out,
    velocity_expert_in,
    velocity_gate_in,
    velocity_expert_out,
    velocity_tower_in,
    velocity_tower_out,
    average_expert_in,
    average_gate_in,
    average_expert_out,
    average_tower_in,
    average_tower_out,
):
    cube = Cube()
    micro, rows_dev, width = inputs.shape
    fields = cube.fields
    tile = rows_dev // fields
    rows_own = micro * tile
    experts, second_rows, out_cols = expert_out.shape
    tasks, tower_cols = tower_out.shape
    wide = expert_in.shape[1]
    hidden = wide // experts
    first_rows = expert_in.shape[0]
    part = experts // 2
    total_rows = micro * rows_dev * cube.rows
    r, f = lax.axis_index("rows"), lax.axis_index("field")

    def own_half(values, which):
        return lax.dynamic_slice_in_dim(values, which * tile, tile, 1)

    own_valid = own_half(valid_mask, f)
    ones = jnp.sum(own_valid)
    digits = jnp.stack([ones % 256, (ones // 256) % 256, ones // 65536]).astype(bf16)
    extra = jnp.zeros((first_rows, LANES - tasks * experts), bf16).at[0, :3].set(digits)
    block_a = jnp.concatenate([expert_in.astype(bf16), gate_in.astype(bf16), extra], axis=1)
    block_b = jnp.concatenate(
        [
            expert_out.astype(bf16)
            .reshape(2, part, second_rows, out_cols)
            .transpose(0, 2, 1, 3)
            .reshape(2 * second_rows, part * out_cols),
            tower_in.astype(bf16).reshape(2 * second_rows, tower_cols),
        ],
        axis=1,
    )
    x_send = own_half(inputs, 1 - f).reshape(rows_own, width)
    x_got = lax.ppermute(x_send, "field", [(0, 1), (1, 0)])
    own_a, oth_a = gather(cube, block_a)
    own_b, oth_b = gather(cube, block_b)

    pairs = 2 * width // BLOCK // 2
    fit = first_rows == BLOCK
    j = jnp.arange(pairs // 2, dtype=jnp.int32)[:, None]
    ff = jnp.arange(2, dtype=jnp.int32)[None, :]
    if fit:
        core = r & 1
        places = [
            cube.place(2 * j + core, ff, r, f).reshape(-1),
            cube.place(2 * j + 1 - core, ff, r ^ 1, f).reshape(-1),
        ]
    else:
        core = jnp.int32(0)
        places = [(2 * j + ff).reshape(-1)] * 2
        rows_a, rows_b = sorted_rows(cube, r, f, width, first_rows, second_rows)
        all_a, all_b = jnp.concatenate([own_a, oth_a]), jnp.concatenate([own_b, oth_b])
        own_a, oth_a = jnp.split(jnp.take(all_a, rows_a, axis=0), 2)
        own_b, oth_b = jnp.split(jnp.take(all_b, rows_b, axis=0), 2)
    tab = jnp.concatenate(places + [jnp.stack([core, f])]).astype(jnp.int32)
    sent = bf16 if fit else f32

    meta = jnp.stack(
        [own_valid.astype(f32), own_half(labels, f).astype(f32), own_half(domains, f).astype(f32)]
        + [jnp.zeros((micro, tile), f32)] * 5,
        axis=1,
    )
    a_cols, b_cols = wide + LANES, part * out_cols + LANES
    half = width

    ga, gs, gate, first_w, count, x_t = pl.pallas_call(
        first_kernel,
        grid_spec=pltpu.PrefetchScalarGridSpec(
            num_scalar_prefetch=1,
            grid=(micro,),
            in_specs=[
                whole((half, a_cols)),
                whole((half, a_cols)),
                pl.BlockSpec((1, tile, width), lambda i, tab: (i, tab[2 * pairs + 1], 0)),
                pl.BlockSpec((tile, width), lambda i, tab: (i, 0)),
                pl.BlockSpec((1, 8, tile), lambda i, tab: (i, 0, 0)),
            ],
            out_specs=[
                pl.BlockSpec((tile, wide), lambda i, tab: (i, 0)),
                pl.BlockSpec((tile, wide), lambda i, tab: (i, 0)),
                pl.BlockSpec((tile, LANES), lambda i, tab: (i, 0)),
                whole((2 * half, a_cols)),
                whole((8, LANES)),
                pl.BlockSpec((2 * width, tile), lambda i, tab: (0, i)),
            ],
        ),
        out_shape=[
            shape((rows_own, wide), bf16),
            shape((rows_own, wide), bf16),
            shape((rows_own, LANES), f32),
            shape((2 * half, a_cols), bf16),
            shape((8, LANES), f32),
            shape((2 * width, rows_own), bf16),
        ],
        compiler_params=params(),
        name="first",
    )(tab, own_a, oth_a, inputs, x_got, meta)

    head = jnp.broadcast_to(
        tower_out.astype(bf16).astype(f32).reshape(1, tasks * tower_cols), (8, tasks * tower_cols)
    )
    second_w, dmixed, keep_b, send_b, side = pl.pallas_call(
        second_kernel,
        grid_spec=pltpu.PrefetchScalarGridSpec(
            num_scalar_prefetch=1,
            grid=(micro,),
            in_specs=[
                whole((half, b_cols)),
                whole((half, b_cols)),
                pl.BlockSpec((tile, wide), lambda i, tab: (i, 0)),
                pl.BlockSpec((1, 8, tile), lambda i, tab: (i, 0, 0)),
                whole((8, LANES)),
                whole((8, tasks * tower_cols)),
            ],
            out_specs=[
                whole((wide, out_cols)),
                pl.BlockSpec((tile, out_cols), lambda i, tab: (i, 0)),
                whole((half, b_cols)),
                whole((half, b_cols)),
                whole((8, tasks * tower_cols)),
            ],
            scratch_shapes=[
                pltpu.VMEM((out_cols, tasks * tower_cols), bf16),
                pltpu.VMEM((experts, hidden, out_cols), f32),
                pltpu.VMEM((out_cols, tasks * tower_cols), f32),
            ],
        ),
        out_shape=[
            shape((wide, out_cols), bf16),
            shape((rows_own, out_cols), bf16),
            shape((half, b_cols), f32),
            shape((half, b_cols), sent),
            shape((8, tasks * tower_cols), f32),
        ],
        compiler_params=params(),
        name="second",
    )(tab, own_b, oth_b, ga, meta, count, head)

    dpre, dgate, keep_a, send_a = pl.pallas_call(
        back_kernel,
        grid_spec=pltpu.PrefetchScalarGridSpec(
            num_scalar_prefetch=1,
            grid=(experts,),
            in_specs=[
                whole((rows_own, out_cols)),
                pl.BlockSpec((hidden, out_cols), lambda i, tab: (i, 0)),
                pl.BlockSpec((rows_own, hidden), lambda i, tab: (0, i)),
                pl.BlockSpec((rows_own, hidden), lambda i, tab: (0, i)),
                whole((2 * width, rows_own)),
                whole((rows_own, LANES)),
            ],
            out_specs=[
                pl.BlockSpec((rows_own, hidden), lambda i, tab: (0, i)),
                whole((rows_own, LANES)),
                whole((half, a_cols)),
                whole((half, a_cols)),
            ],
            scratch_shapes=[
                pltpu.VMEM((rows_own, LANES), f32),
                pltpu.VMEM((2 * width, hidden), f32),
            ],
        ),
        out_shape=[
            shape((rows_own, wide), bf16),
            shape((rows_own, LANES), bf16),
            shape((half, a_cols), f32),
            shape((half, a_cols), sent),
        ],
        compiler_params=params(),
        name="back",
    )(tab, dmixed, second_w, ga, gs, x_t, gate)

    grad_keep, grad_send = pl.pallas_call(
        input_kernel,
        grid_spec=pltpu.PrefetchScalarGridSpec(
            num_scalar_prefetch=1,
            grid=(micro,),
            in_specs=[
                pl.BlockSpec((tile, wide), lambda i, tab: (i, 0)),
                pl.BlockSpec((tile, LANES), lambda i, tab: (i, 0)),
                whole((2 * half, a_cols)),
            ],
            out_specs=[
                pl.BlockSpec((1, tile, width), lambda i, tab: (i, tab[2 * pairs + 1], 0)),
                pl.BlockSpec((tile, width), lambda i, tab: (i, 0)),
            ],
        ),
        out_shape=[
            shape((micro, rows_dev, width), f32),
            shape((rows_own, width), bf16),
        ],
        compiler_params=params(),
        name="input",
    )(tab, dpre, dgate, first_w)
    grad_got = lax.ppermute(grad_send, "field", [(0, 1), (1, 0)])
    input_grad = lax.dynamic_update_slice_in_dim(
        grad_keep, grad_got.astype(f32).reshape(micro, tile, width), (1 - f) * tile, 1
    )

    if not fit:
        keep_b, send_b = unsorted(keep_b, send_b, rows_b)
        keep_a, send_a = unsorted(keep_a, send_a, rows_a)
    sum_b = scatter(cube, keep_b, send_b)
    sum_a = scatter(cube, keep_a, send_a)
    side = sum_all(cube, side)

    second_sum = (
        sum_b[:, : part * out_cols]
        .reshape(2, second_rows, part, out_cols)
        .transpose(0, 2, 1, 3)
        .reshape(experts, second_rows, out_cols)
    )
    gradients = (
        sum_a[:, :wide],
        sum_a[:, wide : wide + tasks * experts],
        second_sum,
        sum_b[:, part * out_cols :].reshape(tasks, second_rows, tower_cols),
        side[0].reshape(tasks, tower_cols),
    )
    weights = (expert_in, gate_in, expert_out, tower_in, tower_out)
    velocities = (
        velocity_expert_in,
        velocity_gate_in,
        velocity_expert_out,
        velocity_tower_in,
        velocity_tower_out,
    )
    averages = (
        average_expert_in,
        average_gate_in,
        average_expert_out,
        average_tower_in,
        average_tower_out,
    )
    scale_root = math.sqrt(total_rows)
    results = [side[1, 0] / count[0, 0], input_grad]
    for at in range(5):
        results.extend(
            renew(weights[at], velocities[at], averages[at], gradients[at], rate_bases[at] * scale_root)
        )
    return tuple(results)


def sorted_rows(cube, r, f, width, first_rows, second_rows):
    core = r & 1
    held = cube.rows * cube.fields // 2

    def row_of(rr, ff, inner, size):
        same = (rr & 1) == core
        here = cube.place(rr, ff, r, f)
        there = cube.place(rr, ff, r ^ 1, f)
        return jnp.where(same, here, held + there) * size + inner

    side = np.arange(2)[:, None, None, None]
    j = np.arange(width // (2 * BLOCK))[None, :, None, None]
    ff = np.arange(2)[None, None, :, None]
    inner = np.arange(BLOCK)[None, None, None, :]
    at = ((2 * j + side) * BLOCK + inner + 0 * ff).astype(np.int32)
    rows_a = row_of(jnp.asarray(at // first_rows), jnp.asarray(ff + 0 * at), jnp.asarray(at % first_rows), first_rows)
    upper = inner // 8
    at = ((2 * j + side) * BLOCK + ff * 8 + inner % 8).astype(np.int32)
    owner = at // second_rows
    rows_b = row_of(
        jnp.asarray(owner // 2),
        jnp.asarray(owner % 2),
        jnp.asarray(at % second_rows + second_rows * upper),
        2 * second_rows,
    )
    return rows_a.reshape(-1), rows_b.reshape(-1)


def unsorted(keep, send, rows):
    every = jnp.concatenate([keep, send])
    back = jnp.zeros_like(rows).at[rows].set(jnp.arange(rows.shape[0], dtype=rows.dtype))
    keep, send = jnp.split(jnp.take(every, back, axis=0), 2)
    return keep, send.astype(bf16)


def solution(mesh):
    first = P(("field", "rows"), None)
    second = P(None, ("rows", "field"), None)
    by_row = P(None, "rows")
    inputs = P(None, "rows", "field")
    weights = (first, first, second, second, P())
    return jax.shard_map(
        on_device,
        mesh=mesh,
        in_specs=(inputs, by_row, by_row, by_row) + weights * 3,
        out_specs=(P(), inputs) + tuple(spec for spec in weights for _ in range(3)),
        check_vma=False,
    )
```

```python
import math

import jax
import jax.numpy as jnp
import numpy as np
from jax import lax
from jax.experimental import pallas as pl
from jax.experimental.pallas import tpu as pltpu
from jax.sharding import PartitionSpec as P

momentum_mu = 0.5
average_keep = 0.5
rate_bases = (17.0, 1.0, 24.0, 4.0, 0.25)
both = ("rows", "field")
f32 = jnp.float32
bf16 = jnp.bfloat16
BLOCK = 16
LANES = 128


def dot(a, b):
    return lax.dot_general(a, b, (((1,), (0,)), ((), ())), preferred_element_type=f32)


def dot_t(a, b):
    return lax.dot_general(a, b, (((1,), (1,)), ((), ())), preferred_element_type=f32)


def t_dot(a, b):
    return lax.dot_general(a, b, (((0,), (0,)), ((), ())), preferred_element_type=f32)


def sigmoid(v):
    return 0.5 + 0.5 * jnp.tanh(0.5 * v)


def rows16(start):
    return pl.ds(pl.multiple_of(start, BLOCK), BLOCK)


def each_block(tab, pairs, body):
    def step(j, carry):
        for side in range(2):
            core = tab[2 * pairs] if side == 0 else 1 - tab[2 * pairs]
            body(side, tab[side * pairs + j], 2 * (j // 2) + core, j % 2)
        return carry

    lax.fori_loop(0, pairs, step, 0, unroll=True)


def first_kernel(
    tab, own_ref, oth_ref, xo_ref, xr_ref, meta_ref, ga_ref, gs_ref, gate_ref, w_ref, xt_ref
):
    pairs = own_ref.shape[0] // BLOCK
    half = xo_ref.shape[-1]
    wide = ga_ref.shape[1]
    hidden = 256 if wide % 256 == 0 else LANES
    experts = tab_experts(wide, hidden)

    @pl.when(pl.program_id(0) == 0)
    def _():
        def put(side, place, rr, ff):
            src = own_ref if side == 0 else oth_ref
            row = (ff ^ tab[2 * pairs + 1]) * half + rr * BLOCK
            w_ref[rows16(row), :] = src[rows16(place * BLOCK), :]

        each_block(tab, pairs, put)

    x = jnp.concatenate([xo_ref[0], xr_ref[...]], axis=1)
    xt_ref[...] = x.T
    meta = meta_ref[0].T
    domain = meta[:, 2:3]
    logits = dot(x, w_ref[:, wide:])
    lane = lax.broadcasted_iota(jnp.int32, logits.shape, 1)
    picked = (lane // experts).astype(f32) == domain
    top = jnp.max(jnp.where(picked, logits, -jnp.inf), axis=1, keepdims=True)
    raised = jnp.where(picked, jnp.exp(jnp.where(picked, logits, top) - top), 0.0)
    gate = raised / jnp.sum(raised, axis=1, keepdims=True)
    gate_ref[...] = gate
    gate = gate + pltpu.roll(gate, LANES - experts, axis=1)
    for k in range(experts):
        cols = pl.ds(k * hidden, hidden)
        pre = dot(x, w_ref[:, cols])
        low = 0.5 * pre
        up = 1.0 + jnp.tanh(low)
        scaled = (0.5 * gate[:, k : k + 1]) * up
        ga_ref[:, cols] = (scaled * pre).astype(bf16)
        gs_ref[:, cols] = (scaled * (1.0 + pre - low * up)).astype(bf16)


def tab_experts(wide, hidden):
    return wide // hidden


def second_kernel(
    tab, own_ref, oth_ref, ga_ref, meta_ref, to_ref, w_ref, dm_ref, gti_ref, side_ref, ti_ref, cnt_ref
):
    pairs = own_ref.shape[0] // BLOCK
    step = pl.program_id(0)
    out_cols = dm_ref.shape[1]
    hidden = pairs * BLOCK
    part = w_ref.shape[0] // hidden // 2

    @pl.when(step == 0)
    def _():
        def put(side, j):
            src = own_ref if side == 0 else oth_ref
            core = tab[2 * pairs] if side == 0 else 1 - tab[2 * pairs]
            a0 = src[rows16(tab[side * pairs + 2 * j] * BLOCK), :].astype(f32)
            a1 = src[rows16(tab[side * pairs + 2 * j + 1] * BLOCK), :].astype(f32)
            row = (2 * j + core) * BLOCK
            upper = jnp.concatenate([a0[:8], a1[:8]], axis=0).astype(bf16)
            lower = jnp.concatenate([a0[8:], a1[8:]], axis=0).astype(bf16)
            at = part * out_cols
            for k in range(part):
                cols = slice(k * out_cols, (k + 1) * out_cols)
                w_ref[rows16(k * hidden + row), :] = upper[:, cols]
                w_ref[rows16((k + part) * hidden + row), :] = lower[:, cols]
            ti_ref[rows16(row), 0:LANES] = upper[:, at : at + LANES]
            ti_ref[rows16(row), LANES : 2 * LANES] = lower[:, at : at + LANES]
            return (a0 + a1)[:, at + LANES :]

        digits = jnp.zeros((BLOCK, LANES), f32)
        for j in range(pairs // 2):
            digits = digits + put(0, j) + put(1, j)
        lane = lax.broadcasted_iota(jnp.int32, digits.shape, 1)
        scale = jnp.where(lane == 0, 1.0, jnp.where(lane == 1, 256.0, jnp.where(lane == 2, 65536.0, 0.0)))
        total = jnp.sum(jnp.sum(digits * scale, axis=1, keepdims=True), axis=0, keepdims=True)
        cnt_ref[...] = jnp.broadcast_to(total, cnt_ref.shape)
        gti_ref[...] = jnp.zeros_like(gti_ref)
        side_ref[...] = jnp.zeros_like(side_ref)

    meta = meta_ref[0].T
    valid, label, domain = meta[:, 0:1], meta[:, 1:2], meta[:, 2:3]
    count = cnt_ref[0:1, 0:1]
    head = to_ref[0:1, :]
    mixed = dot(ga_ref[...], w_ref[...]).astype(bf16)
    tpre = dot(mixed, ti_ref[...])
    lane = lax.broadcasted_iota(jnp.int32, tpre.shape, 1)
    picked = (lane // LANES).astype(f32) == domain
    s = sigmoid(tpre)
    act = (tpre * s).astype(bf16).astype(f32)
    act = jnp.where(picked, act, 0.0)
    chosen = jnp.sum(act * head, axis=1, keepdims=True)
    soft = jnp.maximum(chosen, 0.0) + jnp.log1p(jnp.exp(-jnp.abs(chosen)))
    loss = jnp.sum(valid * (soft - label * chosen), axis=0, keepdims=True) / count
    dlogit = (valid * (sigmoid(chosen) - label) / count).astype(bf16).astype(f32)
    slope = s * (1.0 + tpre * (1.0 - s))
    dtpre = jnp.where(picked, dlogit * head * slope, 0.0).astype(bf16)
    width = head.shape[1]
    side_ref[0:1, 0:width] += jnp.sum(dlogit * act, axis=0, keepdims=True)
    side_ref[0:1, width : width + LANES] += jnp.broadcast_to(loss, (1, LANES))
    gti_ref[...] += t_dot(mixed, dtpre)
    dm_ref[...] = dot_t(dtpre, ti_ref[...]).astype(bf16)


def outer_kernel(tab, dm_ref, ga_ref, gb_ref, gti_ref, side_ref, keep_ref, send_ref, gwo_ref):
    pairs = keep_ref.shape[0] // BLOCK
    step = pl.program_id(0)
    out_cols = dm_ref.shape[1]
    gwo_ref[0] = t_dot(ga_ref[...], dm_ref[...])
    gwo_ref[1] = t_dot(gb_ref[...], dm_ref[...])

    def pack(above, below, cols):
        def put(side, place, rr, ff):
            dst = keep_ref if side == 0 else send_ref
            row = pl.ds(pl.multiple_of(rr * BLOCK + ff * 8, 8), 8)
            tile = jnp.concatenate([above(row), below(row)], axis=0)
            dst[rows16(place * BLOCK), cols] = tile.astype(dst.dtype)

        each_block(tab, pairs, put)

    pack(
        lambda row: gwo_ref[0, row, :],
        lambda row: gwo_ref[1, row, :],
        pl.ds(pl.multiple_of(step * out_cols, out_cols), out_cols),
    )

    @pl.when(step == 0)
    def _():
        at = keep_ref.shape[1] - LANES
        pack(
            lambda row: gti_ref[row, 0:LANES],
            lambda row: gti_ref[row, LANES : 2 * LANES],
            slice(at, at + LANES),
        )


def back_kernel(
    tab,
    dm_ref,
    w_ref,
    ga_ref,
    gs_ref,
    xt_ref,
    gate_ref,
    dp_ref,
    dg_ref,
    keep_ref,
    send_ref,
    q_ref,
    gwi_ref,
):
    k = pl.program_id(0)
    experts = pl.num_programs(0)
    pairs = keep_ref.shape[0] // BLOCK
    half = keep_ref.shape[0]
    hidden = ga_ref.shape[1]
    wide = keep_ref.shape[1] - LANES

    def pack(start, width):
        def put(side, place, rr, ff):
            dst = keep_ref if side == 0 else send_ref
            row = (ff ^ tab[2 * pairs + 1]) * half + rr * BLOCK
            dst[rows16(place * BLOCK), pl.ds(start, width)] = gwi_ref[rows16(row), 0:width].astype(dst.dtype)

        each_block(tab, pairs, put)

    u = dot_t(dm_ref[...], w_ref[...])
    dpre = (u * gs_ref[...].astype(f32)).astype(bf16)
    dp_ref[...] = dpre
    q = jnp.sum(u * ga_ref[...].astype(f32), axis=1, keepdims=True)
    lane = lax.broadcasted_iota(jnp.int32, q_ref.shape, 1)
    mine = (lane == k) | (lane == k + experts)
    q_ref[...] = jnp.where(mine, q, jnp.where(k == 0, 0.0, q_ref[...]))
    gwi_ref[...] = dot(xt_ref[...], dpre)
    pack(pl.multiple_of(k * hidden, hidden), hidden)

    @pl.when(k == experts - 1)
    def _():
        q = q_ref[...]
        gate = gate_ref[...]
        total = jnp.sum(jnp.where(lane < experts, q, 0.0), axis=1, keepdims=True)
        dgate = jnp.where(gate_ref[...] != 0.0, q, 0.0) - gate * total
        dgate = dgate.astype(bf16)
        dg_ref[...] = dgate
        gwi_ref[:, 0:LANES] = dot(xt_ref[...], dgate)
        pack(wide, LANES)


def input_kernel(tab, dp_ref, dg_ref, w_ref, keep_ref, send_ref):
    wide = dp_ref.shape[1]
    grad = dot_t(dp_ref[...], w_ref[:, 0:wide]) + dot_t(dg_ref[...], w_ref[:, wide:])
    half = grad.shape[1] // 2
    keep_ref[0] = grad[:, :half]
    send_ref[...] = grad[:, half:].astype(bf16)


class Cube:
    def __init__(self):
        self.rows = lax.axis_size("rows")
        self.fields = lax.axis_size("field")
        self.bits = int(math.log2(self.rows))
        assert 1 << self.bits == self.rows and self.fields == 2
        self.outer = self.bits - 2
        steps = [self.flip_row(b) for b in range(self.bits - 1, 1, -1)]
        steps += [self.flip_mixed(0), self.flip_mixed(1)]
        self.steps = steps
        self.core = self.flip_row(0)

    def table(self, partner):
        pairs = []
        for r in range(self.rows):
            for f in range(self.fields):
                rr, ff = partner(r, f)
                pairs.append((r * self.fields + f, rr * self.fields + ff))
        return pairs

    def flip_row(self, bit):
        return self.table(lambda r, f: (r ^ (1 << bit), f))

    def flip_mixed(self, turn):
        return self.table(lambda r, f: (r ^ 2, f) if (r & 1) == turn else (r, f ^ 1))

    def place(self, rr, ff, r, f):
        dr, df, core = rr ^ r, ff ^ f, r & 1
        out = jnp.zeros_like(dr)
        for s in range(self.outer):
            out = out + (((dr >> (self.bits - 1 - s)) & 1) << s)
        xbit = (dr >> 1) & 1
        low = jnp.where(core == 0, xbit, df)
        high = jnp.where(core == 0, df, xbit)
        return out + (low << self.outer) + (high << (self.outer + 1))


def gather_two(cube, block_a, block_b):
    for pairs in cube.steps:
        got = lax.ppermute(block_a, both, pairs)
        block_a = jnp.concatenate([block_a, got], axis=0)
        got = lax.ppermute(after(block_b, got), both, pairs)
        block_b = jnp.concatenate([block_b, got], axis=0)
    oth_a = lax.ppermute(block_a, both, cube.core)
    return block_a, oth_a, block_b, lax.ppermute(block_b, both, cube.core)


def after(values, *earlier):
    return lax.optimization_barrier((values,) + earlier)[0]


def fold(total, got):
    rows = got.shape[0]
    total = total[:rows] + got.astype(f32)
    half = rows // 2
    return total, total[half:].astype(bf16)


def split_two(values):
    high = lax.reduce_precision(values, 8, 7)
    low = lax.reduce_precision(values - high, 8, 7)
    return jnp.concatenate([high, low], axis=0).astype(bf16)


def join_two(rows):
    rows = rows.astype(f32)
    half = rows.shape[0] // 2
    return rows[:half] + rows[half:]


def beside(part, side):
    mine = split_two(side)
    return jnp.concatenate([part, mine], axis=0), join_two(mine)


def fold_beside(total, side, got):
    rows = got.shape[0] - 8
    total, part = fold(total, got[:rows])
    message, side = beside(part, side + join_two(got[rows:]))
    return total, message, side


def renew(weight, velocity, average, gradient, rate):
    velocity_new = momentum_mu * velocity + gradient
    weight_new = weight - rate * (gradient + momentum_mu * velocity_new)
    average_new = average_keep * average + (1.0 - average_keep) * weight_new
    return (weight_new, velocity_new, average_new)


def shape(dims, dtype):
    return jax.ShapeDtypeStruct(dims, dtype)


def whole(dims):
    return pl.BlockSpec(dims, lambda i, tab: (0,) * len(dims), pipeline_mode=pl.Buffered(1))


def whole_out(dims):
    return pl.BlockSpec(dims, lambda i, tab: (0,) * len(dims))


def params(limit):
    return pltpu.CompilerParams(vmem_limit_bytes=limit << 20)


def cost(flops):
    return pl.CostEstimate(flops=flops, bytes_accessed=8 << 20, transcendentals=0)


def on_device(
    inputs,
    valid_mask,
    labels,
    domains,
    expert_in,
    gate_in,
    expert_out,
    tower_in,
    tower_out,
    velocity_expert_in,
    velocity_gate_in,
    velocity_expert_out,
    velocity_tower_in,
    velocity_tower_out,
    average_expert_in,
    average_gate_in,
    average_expert_out,
    average_tower_in,
    average_tower_out,
):
    cube = Cube()
    micro, rows_dev, width = inputs.shape
    fields = cube.fields
    tile = rows_dev // fields
    rows_own = micro * tile
    experts, second_rows, out_cols = expert_out.shape
    tasks, tower_cols = tower_out.shape
    wide = expert_in.shape[1]
    hidden = wide // experts
    first_rows = expert_in.shape[0]
    part = experts // 2
    total_rows = micro * rows_dev * cube.rows
    r, f = lax.axis_index("rows"), lax.axis_index("field")

    def own_half(values, which):
        return lax.dynamic_slice_in_dim(values, which * tile, tile, 1)

    own_valid = own_half(valid_mask, f)
    ones = jnp.sum(own_valid)
    digits = jnp.stack([ones % 256, (ones // 256) % 256, ones // 65536]).astype(bf16)
    extra = jnp.zeros((2 * second_rows, LANES), bf16).at[0, :3].set(digits)
    empty = jnp.zeros((first_rows, LANES - tasks * experts), bf16)
    block_a = jnp.concatenate([expert_in.astype(bf16), gate_in.astype(bf16), empty], axis=1)
    block_b = jnp.concatenate(
        [
            expert_out.astype(bf16)
            .reshape(2, part, second_rows, out_cols)
            .transpose(0, 2, 1, 3)
            .reshape(2 * second_rows, part * out_cols),
            tower_in.astype(bf16).reshape(2 * second_rows, tower_cols),
            extra,
        ],
        axis=1,
    )
    x_send = own_half(after(inputs, block_a), 1 - f).reshape(rows_own, width)
    x_got = lax.ppermute(x_send, "field", [(0, 1), (1, 0)])
    own_a, oth_a, own_b, oth_b = gather_two(cube, block_a, block_b)

    pairs = 2 * width // BLOCK // 2
    fit = first_rows == BLOCK
    j = jnp.arange(pairs // 2, dtype=jnp.int32)[:, None]
    ff = jnp.arange(2, dtype=jnp.int32)[None, :]
    if fit:
        core = r & 1
        places = [
            cube.place(2 * j + core, ff, r, f).reshape(-1),
            cube.place(2 * j + 1 - core, ff, r ^ 1, f).reshape(-1),
        ]
    else:
        core = jnp.int32(0)
        places = [(2 * j + ff).reshape(-1)] * 2
        rows_a, rows_b = sorted_rows(cube, r, f, width, first_rows, second_rows)
        all_a, all_b = jnp.concatenate([own_a, oth_a]), jnp.concatenate([own_b, oth_b])
        own_a, oth_a = jnp.split(jnp.take(all_a, rows_a, axis=0), 2)
        own_b, oth_b = jnp.split(jnp.take(all_b, rows_b, axis=0), 2)
    tab = jnp.concatenate(places + [jnp.stack([core, f])]).astype(jnp.int32)
    sent = bf16 if fit else f32

    meta = jnp.stack(
        [own_valid.astype(f32), own_half(labels, f).astype(f32), own_half(domains, f).astype(f32)]
        + [jnp.zeros((micro, tile), f32)] * 5,
        axis=1,
    )
    a_cols, b_cols = wide + LANES, part * out_cols + LANES
    half = width
    heads = tasks * tower_cols

    ga, gs, gate, first_w, x_t = pl.pallas_call(
        first_kernel,
        grid_spec=pltpu.PrefetchScalarGridSpec(
            num_scalar_prefetch=1,
            grid=(micro,),
            in_specs=[
                whole((half, a_cols)),
                whole((half, a_cols)),
                pl.BlockSpec((1, tile, width), lambda i, tab: (i, tab[2 * pairs + 1], 0)),
                pl.BlockSpec((tile, width), lambda i, tab: (i, 0)),
                pl.BlockSpec((1, 8, tile), lambda i, tab: (i, 0, 0)),
            ],
            out_specs=[
                pl.BlockSpec((tile, wide), lambda i, tab: (i, 0)),
                pl.BlockSpec((tile, wide), lambda i, tab: (i, 0)),
                pl.BlockSpec((tile, LANES), lambda i, tab: (i, 0)),
                whole_out((2 * half, a_cols)),
                pl.BlockSpec((2 * width, tile), lambda i, tab: (0, i)),
            ],
        ),
        out_shape=[
            shape((rows_own, wide), bf16),
            shape((rows_own, wide), bf16),
            shape((rows_own, LANES), f32),
            shape((2 * half, a_cols), bf16),
            shape((2 * width, rows_own), bf16),
        ],
        compiler_params=params(24),
        cost_estimate=cost(4 * rows_own * 2 * width * a_cols),
        name="first",
    )(tab, own_a, oth_a, inputs, x_got, meta)

    head = jnp.broadcast_to(tower_out.astype(bf16).astype(f32).reshape(1, heads), (8, heads))
    second_w, dmixed, grad_ti, side = pl.pallas_call(
        second_kernel,
        grid_spec=pltpu.PrefetchScalarGridSpec(
            num_scalar_prefetch=1,
            grid=(micro,),
            in_specs=[
                whole((half, b_cols + LANES)),
                whole((half, b_cols + LANES)),
                pl.BlockSpec((tile, wide), lambda i, tab: (i, 0)),
                pl.BlockSpec((1, 8, tile), lambda i, tab: (i, 0, 0)),
                whole((8, heads)),
            ],
            out_specs=[
                whole_out((wide, out_cols)),
                pl.BlockSpec((tile, out_cols), lambda i, tab: (i, 0)),
                whole_out((out_cols, heads)),
                whole_out((8, b_cols)),
            ],
            scratch_shapes=[
                pltpu.VMEM((out_cols, heads), bf16),
                pltpu.VMEM((8, LANES), f32),
            ],
        ),
        out_shape=[
            shape((wide, out_cols), bf16),
            shape((rows_own, out_cols), bf16),
            shape((out_cols, heads), f32),
            shape((8, b_cols), f32),
        ],
        compiler_params=params(24),
        cost_estimate=cost(4 * rows_own * wide * out_cols),
        name="second",
    )(tab, own_b, oth_b, ga, meta, head)

    dpre, dgate, keep_a, send_a = pl.pallas_call(
        back_kernel,
        grid_spec=pltpu.PrefetchScalarGridSpec(
            num_scalar_prefetch=1,
            grid=(experts,),
            in_specs=[
                whole((rows_own, out_cols)),
                pl.BlockSpec((hidden, out_cols), lambda i, tab: (i, 0)),
                pl.BlockSpec((rows_own, hidden), lambda i, tab: (0, i)),
                pl.BlockSpec((rows_own, hidden), lambda i, tab: (0, i)),
                whole((2 * width, rows_own)),
                whole((rows_own, LANES)),
            ],
            out_specs=[
                pl.BlockSpec((rows_own, hidden), lambda i, tab: (0, i)),
                whole_out((rows_own, LANES)),
                whole_out((half, a_cols)),
                whole_out((half, a_cols)),
            ],
            scratch_shapes=[
                pltpu.VMEM((rows_own, LANES), f32),
                pltpu.VMEM((2 * width, hidden), f32),
            ],
        ),
        out_shape=[
            shape((rows_own, wide), bf16),
            shape((rows_own, LANES), bf16),
            shape((half, a_cols), f32),
            shape((half, a_cols), sent),
        ],
        compiler_params=params(24),
        cost_estimate=cost(6 * rows_own * 2 * width * a_cols),
        name="back",
    )(tab, dmixed, second_w, ga, gs, x_t, gate)

    order = [cube.core] + cube.steps[::-1]
    if not fit:
        keep_a, send_a = unsorted(keep_a, send_a, rows_a)
    got_a = lax.ppermute(send_a, both, order[0])
    keep_b, send_b = pl.pallas_call(
        outer_kernel,
        grid_spec=pltpu.PrefetchScalarGridSpec(
            num_scalar_prefetch=1,
            grid=(part,),
            in_specs=[
                whole((rows_own, out_cols)),
                pl.BlockSpec((rows_own, hidden), lambda i, tab: (0, i)),
                pl.BlockSpec((rows_own, hidden), lambda i, tab: (0, i + part)),
                whole((out_cols, heads)),
                whole((8, b_cols)),
            ],
            out_specs=[whole_out((half, b_cols)), whole_out((half, b_cols))],
            scratch_shapes=[pltpu.VMEM((2, hidden, out_cols), f32)],
        ),
        out_shape=[shape((half, b_cols), f32), shape((half, b_cols), sent)],
        compiler_params=params(16),
        cost_estimate=cost(4 * rows_own * wide * out_cols),
        name="outer",
    )(tab, after(dmixed, dgate), ga, ga, grad_ti, side)

    if not fit:
        keep_b, send_b = unsorted(keep_b, send_b, rows_b)
    side = side[:4]
    message, side = beside(after(send_b, got_a), side)
    sum_a, next_a = fold(keep_a, after(got_a, keep_b))
    got_a = lax.ppermute(next_a, both, order[1])
    got_b = lax.ppermute(message, both, order[0])
    grad_keep, grad_send = pl.pallas_call(
        input_kernel,
        grid_spec=pltpu.PrefetchScalarGridSpec(
            num_scalar_prefetch=1,
            grid=(micro,),
            in_specs=[
                pl.BlockSpec((tile, wide), lambda i, tab: (i, 0)),
                pl.BlockSpec((tile, LANES), lambda i, tab: (i, 0)),
                whole((2 * half, a_cols)),
            ],
            out_specs=[
                pl.BlockSpec((1, tile, width), lambda i, tab: (i, tab[2 * pairs + 1], 0)),
                pl.BlockSpec((tile, width), lambda i, tab: (i, 0)),
            ],
        ),
        out_shape=[
            shape((micro, rows_dev, width), f32),
            shape((rows_own, width), bf16),
        ],
        compiler_params=params(16),
        cost_estimate=cost(4 * rows_own * 2 * width * a_cols),
        name="input",
    )(tab, dpre, after(dgate, next_a), first_w)
    sum_b, message, side = fold_beside(keep_b, side, after(got_b, grad_send))
    for at in range(1, len(order)):
        if at == 2:
            grad_got = lax.ppermute(after(grad_send, got_a), "field", [(0, 1), (1, 0)])
        sum_a, next_a = fold(sum_a, got_a)
        got_b = lax.ppermute(after(message, got_a), both, order[at])
        if at + 1 < len(order):
            got_a = lax.ppermute(next_a, both, order[at + 1])
            sum_b, message, side = fold_beside(sum_b, side, got_b)
    rows = got_b.shape[0] - 8
    sum_b = sum_b[:rows] + got_b[:rows].astype(f32)
    side = side + join_two(got_b[rows:])
    input_grad = lax.dynamic_update_slice_in_dim(
        grad_keep, grad_got.astype(f32).reshape(micro, tile, width), (1 - f) * tile, 1
    )

    second_sum = (
        sum_b[:, : part * out_cols]
        .reshape(2, second_rows, part, out_cols)
        .transpose(0, 2, 1, 3)
        .reshape(experts, second_rows, out_cols)
    )
    gradients = (
        sum_a[:, :wide],
        sum_a[:, wide : wide + tasks * experts],
        second_sum,
        sum_b[:, part * out_cols :].reshape(tasks, second_rows, tower_cols),
        side[0, :heads].reshape(tasks, tower_cols),
    )
    weights = (expert_in, gate_in, expert_out, tower_in, tower_out)
    velocities = (
        velocity_expert_in,
        velocity_gate_in,
        velocity_expert_out,
        velocity_tower_in,
        velocity_tower_out,
    )
    averages = (
        average_expert_in,
        average_gate_in,
        average_expert_out,
        average_tower_in,
        average_tower_out,
    )
    scale_root = math.sqrt(total_rows)
    results = [side[0, heads], input_grad]
    for at in range(5):
        results.extend(
            renew(weights[at], velocities[at], averages[at], gradients[at], rate_bases[at] * scale_root)
        )
    return tuple(results)


def sorted_rows(cube, r, f, width, first_rows, second_rows):
    core = r & 1
    held = cube.rows * cube.fields // 2

    def row_of(rr, ff, inner, size):
        same = (rr & 1) == core
        here = cube.place(rr, ff, r, f)
        there = cube.place(rr, ff, r ^ 1, f)
        return jnp.where(same, here, held + there) * size + inner

    side = np.arange(2)[:, None, None, None]
    j = np.arange(width // (2 * BLOCK))[None, :, None, None]
    ff = np.arange(2)[None, None, :, None]
    inner = np.arange(BLOCK)[None, None, None, :]
    at = ((2 * j + side) * BLOCK + inner + 0 * ff).astype(np.int32)
    rows_a = row_of(jnp.asarray(at // first_rows), jnp.asarray(ff + 0 * at), jnp.asarray(at % first_rows), first_rows)
    upper = inner // 8
    at = ((2 * j + side) * BLOCK + ff * 8 + inner % 8).astype(np.int32)
    owner = at // second_rows
    rows_b = row_of(
        jnp.asarray(owner // 2),
        jnp.asarray(owner % 2),
        jnp.asarray(at % second_rows + second_rows * upper),
        2 * second_rows,
    )
    return rows_a.reshape(-1), rows_b.reshape(-1)


def unsorted(keep, send, rows):
    every = jnp.concatenate([keep, send])
    back = jnp.zeros_like(rows).at[rows].set(jnp.arange(rows.shape[0], dtype=rows.dtype))
    keep, send = jnp.split(jnp.take(every, back, axis=0), 2)
    return keep, send.astype(bf16)


def solution(mesh):
    first = P(("field", "rows"), None)
    second = P(None, ("rows", "field"), None)
    by_row = P(None, "rows")
    inputs = P(None, "rows", "field")
    weights = (first, first, second, second, P())
    return jax.shard_map(
        on_device,
        mesh=mesh,
        in_specs=(inputs, by_row, by_row, by_row) + weights * 3,
        out_specs=(P(), inputs) + tuple(spec for spec in weights for _ in range(3)),
        check_vma=False,
    )
```

```python
import functools
import math

import jax
import jax.numpy as jnp
import numpy as np
from jax import lax
from jax.experimental import pallas as pl
from jax.experimental.pallas import tpu as pltpu
from jax.sharding import PartitionSpec as P

momentum_mu = 0.5
average_keep = 0.5
rate_bases = (17.0, 1.0, 24.0, 4.0, 0.25)
both = ("rows", "field")
f32 = jnp.float32
bf16 = jnp.bfloat16
BLOCK = 16
LANES = 128


def dot(a, b):
    return lax.dot_general(a, b, (((1,), (0,)), ((), ())), preferred_element_type=f32)


def dot_t(a, b):
    return lax.dot_general(a, b, (((1,), (1,)), ((), ())), preferred_element_type=f32)


def t_dot(a, b):
    return lax.dot_general(a, b, (((0,), (0,)), ((), ())), preferred_element_type=f32)


def sigmoid(v):
    return 0.5 + 0.5 * jnp.tanh(0.5 * v)


def rows16(start):
    return pl.ds(pl.multiple_of(start, BLOCK), BLOCK)


def each_block(tab, pairs, body):
    for j in range(pairs):
        for side in range(2):
            core = tab[2 * pairs] if side == 0 else 1 - tab[2 * pairs]
            body(side, tab[side * pairs + j], 2 * (j // 2) + core, j % 2)


def pack_a_kernel(expert_ref, gate_ref, out_ref):
    wide, gates = expert_ref.shape[1], gate_ref.shape[1]
    out_ref[:, 0:wide] = expert_ref[...].astype(bf16)
    out_ref[:, wide:] = jnp.zeros((out_ref.shape[0], LANES), bf16)
    out_ref[:, wide : wide + gates] = gate_ref[...].astype(bf16)


def pack_b_kernel(expert_ref, tower_ref, digits_ref, out_ref):
    experts, rows, out_cols = expert_ref.shape
    part = experts // 2
    for k in range(part):
        both_k = jnp.concatenate([expert_ref[k], expert_ref[k + part]], axis=0)
        out_ref[:, k * out_cols : (k + 1) * out_cols] = both_k.astype(bf16)
    at = part * out_cols
    towers = jnp.concatenate([tower_ref[0], tower_ref[1]], axis=0)
    out_ref[:, at : at + LANES] = towers.astype(bf16)
    out_ref[:, at + LANES :] = digits_ref[0 : 2 * rows, :].astype(bf16)


def rows_kernel(tab, in_ref, got_ref, meta_ref, x_ref, xt_ref, by_row_ref):
    micro, rows_dev, width = in_ref.shape
    tile = rows_dev // 2
    start = pl.multiple_of(tab[tab.shape[0] - 1] * tile, tile)
    for m in range(micro):
        rows = slice(m * tile, (m + 1) * tile)
        x = jnp.concatenate([in_ref[m, pl.ds(start, tile), :], got_ref[rows, :]], axis=1)
        x_ref[rows, :] = x
        xt_ref[:, rows] = x.T
        by_row_ref[rows, :] = meta_ref[m].T


def first_kernel(tab, own_ref, oth_ref, x_ref, by_row_ref, ga_ref, gs_ref, gate_ref, w_ref):
    half = own_ref.shape[0]
    pairs = half // BLOCK
    count, wide = ga_ref.shape
    experts = wide // half
    tile = count // 2

    def put(side, place, rr, ff):
        src = own_ref if side == 0 else oth_ref
        row = (ff ^ tab[2 * pairs + 1]) * half + rr * BLOCK
        w_ref[rows16(row), :] = src[rows16(place * BLOCK), :]

    each_block(tab, pairs, put)

    def step(i, carry):
        rows = pl.ds(pl.multiple_of(i * tile, tile), tile)
        x = x_ref[rows, :]
        domain = by_row_ref[rows, 2:3]
        logits = dot(x, w_ref[:, wide:])
        lane = lax.broadcasted_iota(jnp.int32, logits.shape, 1)
        picked = (lane // experts).astype(f32) == domain
        masked = jnp.where(picked, logits, -jnp.inf)
        raised = jnp.exp(masked - jnp.max(masked, axis=1, keepdims=True))
        gate = raised / jnp.sum(raised, axis=1, keepdims=True)
        gate_ref[rows, :] = gate
        gate = 0.5 * (gate + pltpu.roll(gate, LANES - experts, axis=1))
        for k in range(experts):
            cols = slice(k * half, (k + 1) * half)
            pre = dot(x, w_ref[:, cols])
            low = 0.5 * pre
            up = 1.0 + jnp.tanh(low)
            scaled = gate[:, k : k + 1] * up
            ga_ref[rows, cols] = (scaled * pre).astype(bf16)
            gs_ref[rows, cols] = (scaled * (1.0 + pre - low * up)).astype(bf16)
        return carry

    lax.fori_loop(0, 2, step, 0)


def rest_kernel(
    tab,
    own_ref,
    oth_ref,
    ga_ref,
    gs_ref,
    gate_ref,
    by_row_ref,
    to_ref,
    xt_ref,
    dm_ref,
    gti_ref,
    side_ref,
    dp_ref,
    dg_ref,
    keep_ref,
    send_ref,
    w_ref,
    ti_ref,
    q_ref,
    g_ref,
):
    half = own_ref.shape[0]
    pairs = half // BLOCK
    count, out_cols = dm_ref.shape
    hidden = half
    wide = ga_ref.shape[1]
    experts = wide // hidden
    part = experts // 2

    digits = jnp.zeros((BLOCK, LANES), f32)
    for side in range(2):
        for j in range(pairs // 2):
            src = own_ref if side == 0 else oth_ref
            core = tab[2 * pairs] if side == 0 else 1 - tab[2 * pairs]
            a0 = src[rows16(tab[side * pairs + 2 * j] * BLOCK), :].astype(f32)
            a1 = src[rows16(tab[side * pairs + 2 * j + 1] * BLOCK), :].astype(f32)
            row = (2 * j + core) * BLOCK
            upper = jnp.concatenate([a0[:8], a1[:8]], axis=0).astype(bf16)
            lower = jnp.concatenate([a0[8:], a1[8:]], axis=0).astype(bf16)
            at = part * out_cols
            for k in range(part):
                cols = slice(k * out_cols, (k + 1) * out_cols)
                w_ref[rows16(k * hidden + row), :] = upper[:, cols]
                w_ref[rows16((k + part) * hidden + row), :] = lower[:, cols]
            ti_ref[rows16(row), 0:LANES] = upper[:, at : at + LANES]
            ti_ref[rows16(row), LANES : 2 * LANES] = lower[:, at : at + LANES]
            digits = digits + (a0 + a1)[:, at + LANES :]
    lane = lax.broadcasted_iota(jnp.int32, digits.shape, 1)
    scale = jnp.where(lane == 0, 1.0, jnp.where(lane == 1, 256.0, jnp.where(lane == 2, 65536.0, 0.0)))
    real = jnp.sum(jnp.sum(digits * scale, axis=1, keepdims=True), axis=0, keepdims=True)

    valid, label, domain = by_row_ref[:, 0:1], by_row_ref[:, 1:2], by_row_ref[:, 2:3]
    head = to_ref[0:1, :]
    mixed = dot(ga_ref[...], w_ref[...]).astype(bf16)
    tpre = dot(mixed, ti_ref[...])
    lane = lax.broadcasted_iota(jnp.int32, tpre.shape, 1)
    picked = (lane // LANES).astype(f32) == domain
    s = sigmoid(tpre)
    act = (tpre * s).astype(bf16).astype(f32)
    act = jnp.where(picked, act, 0.0)
    chosen = jnp.sum(act * head, axis=1, keepdims=True)
    soft = jnp.maximum(chosen, 0.0) + jnp.log1p(jnp.exp(-jnp.abs(chosen)))
    loss = jnp.sum(valid * (soft - label * chosen), axis=0, keepdims=True) / real
    dlogit = (valid * (sigmoid(chosen) - label) / real).astype(bf16).astype(f32)
    slope = s * (1.0 + tpre * (1.0 - s))
    dtpre = jnp.where(picked, dlogit * head * slope, 0.0).astype(bf16)
    heads = head.shape[1]
    side_ref[...] = jnp.zeros_like(side_ref)
    side_ref[0:1, 0:heads] = jnp.sum(dlogit * act, axis=0, keepdims=True)
    side_ref[0:1, heads : heads + LANES] = jnp.broadcast_to(loss, (1, LANES))
    dm_ref[...] = dot_t(dtpre, ti_ref[...]).astype(bf16)

    def pack(start, width):
        def put(side, place, rr, ff):
            dst = keep_ref if side == 0 else send_ref
            row = (ff ^ tab[2 * pairs + 1]) * half + rr * BLOCK
            tile = g_ref[rows16(row), start : start + width]
            dst[rows16(place * BLOCK), start : start + width] = tile.astype(dst.dtype)

        each_block(tab, pairs, put)

    tile = count // 4
    lane = lax.broadcasted_iota(jnp.int32, (tile, LANES), 1)
    q_ref[...] = jnp.zeros_like(q_ref)
    for k in range(experts):
        cols = slice(k * hidden, (k + 1) * hidden)
        for i in range(4):
            rows = slice(i * tile, (i + 1) * tile)
            u = dot_t(dm_ref[rows, :], w_ref[cols, :])
            dp_ref[rows, cols] = (u * gs_ref[rows, cols].astype(f32)).astype(bf16)
            q = jnp.sum(u * ga_ref[rows, cols].astype(f32), axis=1, keepdims=True)
            q_ref[rows, :] = jnp.where((lane == k) | (lane == k + experts), q, q_ref[rows, :])
        g_ref[:, cols] = dot(xt_ref[...], dp_ref[:, cols])
        pack(k * hidden, hidden)
    q = q_ref[...]
    lane = lax.broadcasted_iota(jnp.int32, q.shape, 1)
    total = jnp.sum(jnp.where(lane < experts, q, 0.0), axis=1, keepdims=True)
    mine = (lane // experts).astype(f32) == domain
    dg_ref[...] = (jnp.where(mine, q, 0.0) - gate_ref[...] * total).astype(bf16)
    g_ref[:, wide:] = dot(xt_ref[...], dg_ref[...])
    pack(wide, LANES)
    gti_ref[...] = t_dot(mixed, dtpre)


def outer_kernel(tab, dm_ref, ga_ref, gti_ref, keep_ref, send_ref, g_ref):
    half = keep_ref.shape[0]
    pairs = half // BLOCK
    out_cols = dm_ref.shape[1]
    part = ga_ref.shape[1] // half // 2

    def pack(above, below, cols):
        def put(side, place, rr, ff):
            dst = keep_ref if side == 0 else send_ref
            row = pl.ds(pl.multiple_of(rr * BLOCK + ff * 8, 8), 8)
            tile = jnp.concatenate([above(row), below(row)], axis=0)
            dst[rows16(place * BLOCK), cols] = tile.astype(dst.dtype)

        each_block(tab, pairs, put)

    for k in range(part):
        g_ref[k] = t_dot(ga_ref[:, k * half : (k + 1) * half], dm_ref[...])
        g_ref[k + part] = t_dot(ga_ref[:, (k + part) * half : (k + part + 1) * half], dm_ref[...])
        pack(
            lambda row: g_ref[k, row, :],
            lambda row: g_ref[k + part, row, :],
            slice(k * out_cols, (k + 1) * out_cols),
        )
    at = part * out_cols
    pack(lambda row: gti_ref[row, 0:LANES], lambda row: gti_ref[row, LANES : 2 * LANES], slice(at, at + LANES))


def input_kernel(tab, dp_ref, dg_ref, w_ref, keep_ref, send_ref):
    wide = dp_ref.shape[1]
    grad = dot_t(dp_ref[...], w_ref[:, 0:wide]) + dot_t(dg_ref[...], w_ref[:, wide:])
    half = grad.shape[1] // 2
    keep_ref[0] = grad[:, :half]
    send_ref[...] = grad[:, half:].astype(bf16)


def place_kernel(tab, got_ref, held_ref, out_ref):
    out_ref[0] = got_ref[...].astype(f32)


def update_kernel(rates, sum_a, got_a, sum_b, got_b, side, *refs):
    weights, velocities, averages, outs = refs[0:5], refs[5:10], refs[10:15], refs[15:]
    wide = weights[0].shape[1]
    gates = weights[1].shape[1]
    experts, rows, out_cols = weights[2].shape
    tasks = weights[3].shape[0]
    part = experts // 2

    def renew(at, place, gradient):
        velocity = momentum_mu * velocities[at][place] + gradient
        weight = weights[at][place] - rates[at] * (gradient + momentum_mu * velocity)
        outs[3 * at][place] = weight
        outs[3 * at + 1][place] = velocity
        outs[3 * at + 2][place] = average_keep * averages[at][place] + (1.0 - average_keep) * weight

    first = sum_a[0 : got_a.shape[0], :] + got_a[...].astype(f32)
    renew(0, (slice(None), slice(None)), first[:, :wide])
    renew(1, (slice(None), slice(None)), first[:, wide : wide + gates])
    second = sum_b[0 : got_b.shape[0], :] + got_b[...].astype(f32)
    for k in range(experts):
        top = (k // part) * rows
        renew(2, k, second[top : top + rows, (k % part) * out_cols : (k % part + 1) * out_cols])
    for t in range(tasks):
        renew(3, t, second[t * rows : (t + 1) * rows, part * out_cols :])
        renew(4, (slice(t, t + 1), slice(None)), side[0:1, t * LANES : (t + 1) * LANES])


class Cube:
    def __init__(self):
        self.rows = lax.axis_size("rows")
        self.fields = lax.axis_size("field")
        bits = int(math.log2(self.rows))
        assert 1 << bits == self.rows and self.fields == 2
        outer = [("row", b) for b in range(bits - 1, 1, -1)]
        mixed = [("mixed", 0), ("mixed", 1)]
        self.order = outer + mixed
        self.core = ("row", 0)

    def pairs(self, step):
        kind, which = step
        pairs = []
        for r in range(self.rows):
            for f in range(self.fields):
                if kind == "row":
                    to = (r ^ (1 << which), f)
                else:
                    to = (r ^ 2, f) if (r & 1) == which else (r, f ^ 1)
                pairs.append((r * self.fields + f, to[0] * self.fields + to[1]))
        return pairs

    def swap(self, values, step):
        return lax.ppermute(values, both, self.pairs(step))

    def place(self, order, rr, ff, r, f):
        dr, df, core = rr ^ r, ff ^ f, r & 1
        out = jnp.zeros_like(dr + df)
        for s, (kind, which) in enumerate(order):
            if kind == "row":
                bit = (dr >> which) & 1
            else:
                bit = jnp.where(core == which, (dr >> 1) & 1, df)
            out = out + (bit << s)
        return out


def gather_two(cube, block_a, block_b, x):
    got_b = None
    for at, step in enumerate(cube.order):
        got_a = cube.swap(block_a, step)
        if at:
            block_b = jnp.concatenate([block_b, after(got_b, block_a)], axis=0)
        else:
            block_b = after(block_b, block_a)
        got_b = cube.swap(block_b, step)
        if at + 1 == len(cube.order):
            got_a = after(got_a, x)
        block_a = jnp.concatenate([block_a, after(got_a, block_b)], axis=0)
    return block_a, cube.swap(block_a, cube.core), block_b, got_b


def after(values, *earlier):
    return lax.optimization_barrier((values,) + earlier)[0]


def fold(total, got):
    rows = got.shape[0]
    total = total[:rows] + got.astype(f32)
    half = rows // 2
    return total, total[half:].astype(bf16)


def split_two(values):
    high = lax.reduce_precision(values, 8, 7)
    low = lax.reduce_precision(values - high, 8, 7)
    return jnp.concatenate([high, low], axis=0).astype(bf16)


def join_two(rows):
    rows = rows.astype(f32)
    half = rows.shape[0] // 2
    return rows[:half] + rows[half:]


def beside(part, side):
    mine = split_two(side)
    return jnp.concatenate([part, mine], axis=0), join_two(mine)


def fold_beside(total, side, got):
    rows = got.shape[0] - 8
    total, part = fold(total, got[:rows])
    message, side = beside(part, side + join_two(got[rows:]))
    return total, message, side


def shape(dims, dtype):
    return jax.ShapeDtypeStruct(dims, dtype)


def params(limit):
    return pltpu.CompilerParams(vmem_limit_bytes=limit << 20)


vmem = pl.BlockSpec()
smem = pl.BlockSpec(memory_space=pltpu.SMEM)


def cost(flops):
    return pl.CostEstimate(flops=flops, bytes_accessed=8 << 20, transcendentals=0)


def on_device(
    inputs,
    valid_mask,
    labels,
    domains,
    expert_in,
    gate_in,
    expert_out,
    tower_in,
    tower_out,
    velocity_expert_in,
    velocity_gate_in,
    velocity_expert_out,
    velocity_tower_in,
    velocity_tower_out,
    average_expert_in,
    average_gate_in,
    average_expert_out,
    average_tower_in,
    average_tower_out,
):
    cube = Cube()
    micro, rows_dev, width = inputs.shape
    fields = cube.fields
    tile = rows_dev // fields
    rows_own = micro * tile
    experts, second_rows, out_cols = expert_out.shape
    tasks, tower_cols = tower_out.shape
    wide = expert_in.shape[1]
    hidden = wide // experts
    first_rows = expert_in.shape[0]
    part = experts // 2
    total_rows = micro * rows_dev * cube.rows
    r, f = lax.axis_index("rows"), lax.axis_index("field")

    def own_half(values, which):
        return lax.dynamic_slice_in_dim(values, which * tile, tile, 1)

    block_a = pl.pallas_call(
        pack_a_kernel,
        out_shape=shape((first_rows, wide + LANES), bf16),
        compiler_params=params(4),
        name="pack_a",
    )(expert_in, gate_in)
    own_valid = own_half(after(valid_mask, block_a), f)
    ones = jnp.broadcast_to(jnp.sum(own_valid), (2 * second_rows, LANES))
    row, lane = (lax.broadcasted_iota(jnp.int32, ones.shape, d) for d in range(2))
    digits = jnp.where(lane == 2, ones >> 16, jnp.where(lane == 1, ones >> 8, ones) & 255)
    digits = jnp.where((row == 0) & (lane < 3), digits, 0).astype(f32)
    block_b = pl.pallas_call(
        pack_b_kernel,
        out_shape=shape((2 * second_rows, part * out_cols + 2 * LANES), bf16),
        compiler_params=params(4),
        name="pack_b",
    )(expert_out, tower_in, digits)
    x_send = own_half(after(inputs, block_a), 1 - f).reshape(rows_own, width)
    x_got = lax.ppermute(x_send, "field", [(0, 1), (1, 0)])

    pairs = width // BLOCK
    fit = first_rows == BLOCK
    j = jnp.arange(pairs // 2, dtype=jnp.int32)[:, None]
    ff = jnp.arange(2, dtype=jnp.int32)[None, :]
    if fit:
        core = r & 1
        places = [
            cube.place(cube.order, 2 * j + core, ff, r, f).reshape(-1),
            cube.place(cube.order, 2 * j + 1 - core, ff, r ^ 1, f).reshape(-1),
        ]
    else:
        core = jnp.int32(0)
        places = [(2 * j + ff).reshape(-1)] * 2
    tab = jnp.concatenate(places + [jnp.stack([core, f])]).astype(jnp.int32)
    sent = bf16 if fit else f32

    meta = jnp.stack(
        [own_valid.astype(f32), own_half(labels, f).astype(f32), own_half(domains, f).astype(f32)]
        + [jnp.zeros((micro, tile), f32)] * 5,
        axis=1,
    )
    a_cols, b_cols = wide + LANES, part * out_cols + LANES
    heads = tasks * tower_cols

    x, x_t, by_row = pl.pallas_call(
        rows_kernel,
        in_specs=[smem, vmem, vmem, vmem],
        out_specs=[vmem] * 3,
        out_shape=[
            shape((rows_own, 2 * width), bf16),
            shape((2 * width, rows_own), bf16),
            shape((rows_own, 8), f32),
        ],
        compiler_params=params(8),
        cost_estimate=cost(1 << 20),
        name="rows",
    )(tab, inputs, x_got, meta)

    own_a, oth_a, own_b, got_b = gather_two(cube, block_a, block_b, x)
    if not fit:
        rows_a = first_sorted(cube, cube.order, r, f, width, first_rows)
        own_a, oth_a = jnp.split(jnp.take(jnp.concatenate([own_a, oth_a]), rows_a, axis=0), 2)
    ga, gs, gate, first_w = pl.pallas_call(
        first_kernel,
        in_specs=[smem] + [vmem] * 4,
        out_specs=[vmem] * 4,
        out_shape=[
            shape((rows_own, wide), bf16),
            shape((rows_own, wide), bf16),
            shape((rows_own, LANES), f32),
            shape((2 * width, a_cols), bf16),
        ],
        compiler_params=params(12),
        cost_estimate=cost(4 * rows_own * 2 * width * a_cols),
        name="first",
    )(tab, own_a, oth_a, x, by_row)

    own_b = jnp.concatenate([own_b, after(got_b, gate)], axis=0)
    oth_b = cube.swap(own_b, cube.core)
    if not fit:
        rows_b = second_sorted(cube, cube.order, r, f, width, second_rows)
        own_b, oth_b = jnp.split(jnp.take(jnp.concatenate([own_b, oth_b]), rows_b, axis=0), 2)
    head = jnp.broadcast_to(tower_out.astype(bf16).astype(f32).reshape(1, heads), (8, heads))
    dmixed, grad_ti, side, dpre, dgate, keep_a, send_a = pl.pallas_call(
        rest_kernel,
        in_specs=[smem] + [vmem] * 8,
        out_specs=[vmem] * 7,
        out_shape=[
            shape((rows_own, out_cols), bf16),
            shape((out_cols, heads), f32),
            shape((8, b_cols), f32),
            shape((rows_own, wide), bf16),
            shape((rows_own, LANES), bf16),
            shape((width, a_cols), f32),
            shape((width, a_cols), sent),
        ],
        scratch_shapes=[
            pltpu.VMEM((wide, out_cols), bf16),
            pltpu.VMEM((out_cols, heads), bf16),
            pltpu.VMEM((rows_own, LANES), f32),
            pltpu.VMEM((2 * width, a_cols), f32),
        ],
        compiler_params=params(24),
        cost_estimate=cost(6 * rows_own * 2 * width * a_cols),
        name="rest",
    )(tab, own_b, oth_b, ga, gs, gate, by_row, head, x_t)

    steps = [cube.core] + cube.order[::-1]
    if not fit:
        keep_a, send_a = unsorted(keep_a, send_a, rows_a)
    got_a = cube.swap(send_a, steps[0])
    keep_b, send_b = pl.pallas_call(
        outer_kernel,
        in_specs=[smem] + [vmem] * 3,
        out_specs=[vmem] * 2,
        out_shape=[shape((width, b_cols), f32), shape((width, b_cols), sent)],
        scratch_shapes=[pltpu.VMEM((experts, hidden, out_cols), f32)],
        compiler_params=params(8),
        cost_estimate=cost(4 * rows_own * wide * out_cols),
        name="outer",
    )(tab, dmixed, ga, grad_ti)
    if not fit:
        keep_b, send_b = unsorted(keep_b, send_b, rows_b)

    message, side = beside(send_b, side[:4])
    got_b = cube.swap(message, steps[0])
    sum_a, next_a = fold(keep_a, after(got_a, message))
    sum_b = keep_b
    for at in range(1, len(steps)):
        got_a = cube.swap(next_a, steps[at])
        sum_b, message, side = fold_beside(sum_b, side, after(got_b, next_a))
        got_b = cube.swap(message, steps[at])
        if at == 1:
            grad_keep, grad_send = pl.pallas_call(
                input_kernel,
                grid_spec=pltpu.PrefetchScalarGridSpec(
                    num_scalar_prefetch=1,
                    grid=(micro,),
                    in_specs=[
                        pl.BlockSpec((tile, wide), lambda i, tab: (i, 0)),
                        pl.BlockSpec((tile, LANES), lambda i, tab: (i, 0)),
                        pl.BlockSpec((2 * width, a_cols), lambda i, tab: (0, 0)),
                    ],
                    out_specs=[
                        pl.BlockSpec((1, tile, width), lambda i, tab: (i, tab[2 * pairs + 1], 0)),
                        pl.BlockSpec((tile, width), lambda i, tab: (i, 0)),
                    ],
                ),
                out_shape=[
                    shape((micro, rows_dev, width), f32),
                    shape((rows_own, width), bf16),
                ],
                compiler_params=params(12),
                cost_estimate=cost(4 * rows_own * 2 * width * a_cols),
                name="input",
            )(tab, dpre, after(dgate, message), first_w)
        if at == 3:
            grad_got = lax.ppermute(after(grad_send, next_a), "field", [(0, 1), (1, 0)])
        if at + 1 < len(steps):
            sum_a, next_a = fold(sum_a, after(got_a, message))
    side = side + join_two(got_b[got_b.shape[0] - 8 :])
    input_grad = pl.pallas_call(
        place_kernel,
        grid_spec=pltpu.PrefetchScalarGridSpec(
            num_scalar_prefetch=1,
            grid=(micro,),
            in_specs=[
                pl.BlockSpec((tile, width), lambda i, tab: (i, 0)),
                pl.BlockSpec(memory_space=pl.ANY),
            ],
            out_specs=pl.BlockSpec((1, tile, width), lambda i, tab: (i, 1 - tab[2 * pairs + 1], 0)),
        ),
        out_shape=shape((micro, rows_dev, width), f32),
        input_output_aliases={2: 0},
        compiler_params=params(8),
        cost_estimate=cost(1 << 20),
        name="place",
    )(tab, grad_got, grad_keep)

    weights = (expert_in, gate_in, expert_out, tower_in, tower_out)
    velocities = (
        velocity_expert_in,
        velocity_gate_in,
        velocity_expert_out,
        velocity_tower_in,
        velocity_tower_out,
    )
    averages = (
        average_expert_in,
        average_gate_in,
        average_expert_out,
        average_tower_in,
        average_tower_out,
    )
    rates = [base * math.sqrt(total_rows) for base in rate_bases]
    updated = pl.pallas_call(
        functools.partial(update_kernel, rates),
        out_shape=[shape(w.shape, f32) for w in weights for _ in range(3)],
        compiler_params=params(8),
        cost_estimate=cost(1 << 20),
        name="update",
    )(
        sum_a,
        after(got_a, input_grad),
        sum_b,
        got_b[: got_b.shape[0] - 8],
        side,
        *weights,
        *velocities,
        *averages,
    )
    return (side[0, heads], input_grad, *updated)


def owner_rows(cube, order, r, f, rr, ff, inner, size):
    held = cube.rows * cube.fields // 2
    same = (rr & 1) == (r & 1)
    here = cube.place(order, rr, ff, r, f)
    there = cube.place(order, rr, ff, r ^ 1, f)
    return (jnp.where(same, here, held + there) * size + inner).reshape(-1)


def block_grid(width):
    side = np.arange(2)[:, None, None, None]
    j = np.arange(width // (2 * BLOCK))[None, :, None, None]
    ff = np.arange(2)[None, None, :, None]
    inner = np.arange(BLOCK)[None, None, None, :]
    ahead = (2 * j + side) * BLOCK + 0 * ff + 0 * inner
    full = np.zeros(ahead.shape, np.int32)
    return ahead.astype(np.int32), full + ff.astype(np.int32), full + inner.astype(np.int32)


def first_sorted(cube, order, r, f, width, size):
    ahead, ff, inner = block_grid(width)
    at = ahead + inner
    return owner_rows(
        cube, order, r, f, jnp.asarray(at // size), jnp.asarray(ff), jnp.asarray(at % size), size
    )


def second_sorted(cube, order, r, f, width, size):
    ahead, ff, inner = block_grid(width)
    at = ahead + ff * 8 + inner % 8
    owner = at // size
    held = at % size + size * (inner // 8)
    return owner_rows(
        cube, order, r, f, jnp.asarray(owner // 2), jnp.asarray(owner % 2), jnp.asarray(held), 2 * size
    )


def unsorted(keep, send, rows):
    every = jnp.concatenate([keep, send])
    back = jnp.zeros_like(rows).at[rows].set(jnp.arange(rows.shape[0], dtype=rows.dtype))
    keep, send = jnp.split(jnp.take(every, back, axis=0), 2)
    return keep, send.astype(bf16)


def solution(mesh):
    first = P(("field", "rows"), None)
    second = P(None, ("rows", "field"), None)
    by_row = P(None, "rows")
    inputs = P(None, "rows", "field")
    weights = (first, first, second, second, P())
    return jax.shard_map(
        on_device,
        mesh=mesh,
        in_specs=(inputs, by_row, by_row, by_row) + weights * 3,
        out_specs=(P(), inputs) + tuple(spec for spec in weights for _ in range(3)),
        check_vma=False,
    )
```

```python
import functools
import math

import jax
import jax.numpy as jnp
import numpy as np
from jax import lax
from jax.experimental import pallas as pl
from jax.experimental.pallas import tpu as pltpu
from jax.sharding import PartitionSpec as P

momentum_mu = 0.5
average_keep = 0.5
rate_bases = (17.0, 1.0, 24.0, 4.0, 0.25)
both = ("rows", "field")
f32 = jnp.float32
bf16 = jnp.bfloat16
BLOCK = 16
LANES = 128


def dot(a, b):
    return lax.dot_general(a, b, (((1,), (0,)), ((), ())), preferred_element_type=f32)


def dot_t(a, b):
    return lax.dot_general(a, b, (((1,), (1,)), ((), ())), preferred_element_type=f32)


def t_dot(a, b):
    return lax.dot_general(a, b, (((0,), (0,)), ((), ())), preferred_element_type=f32)


def sigmoid(v):
    return 0.5 + 0.5 * jnp.tanh(0.5 * v)


def rows16(start):
    return pl.ds(pl.multiple_of(start, BLOCK), BLOCK)


class Places:
    def __init__(self, fit, order):
        self.fit, self.order = fit, order

    def bits(self, core, rr, ff):
        out = 0
        for s, (kind, which) in enumerate(self.order):
            if kind == "row":
                bit = (rr >> which) & 1
            else:
                bit = (rr >> 1) & 1 if core == which else ff
            out = out | (bit << s)
        return out

    def start(self):
        r, self.field = lax.axis_index("rows"), lax.axis_index("field")
        self.core = r & 1 if self.fit else jnp.int32(0)
        self.bases = [self.bits(core, r, self.field) for core in range(2)]

    def block(self, side, j):
        core = self.core if side == 0 else 1 - self.core
        pair, ff = j // 2, j % 2
        if not self.fit:
            return j, 2 * pair + side, ff
        ways = [base ^ self.bits(c, 2 * pair, ff) for c, base in enumerate(self.bases)]
        return jnp.where(core == 0, ways[0], ways[1]), 2 * pair + core, ff

    def each(self, pairs, body):
        for j in range(pairs):
            for side in range(2):
                body(side, *self.block(side, j))


def pack_a_kernel(expert_ref, gate_ref, out_ref):
    wide, gates = expert_ref.shape[1], gate_ref.shape[1]
    out_ref[:, 0:wide] = expert_ref[...].astype(bf16)
    out_ref[:, wide:] = jnp.zeros((out_ref.shape[0], LANES), bf16)
    out_ref[:, wide : wide + gates] = gate_ref[...].astype(bf16)


def pack_b_kernel(expert_ref, tower_ref, valid_ref, out_ref):
    experts, rows, out_cols = expert_ref.shape
    part = experts // 2
    for k in range(part):
        both_k = jnp.concatenate([expert_ref[k], expert_ref[k + part]], axis=0)
        out_ref[:, k * out_cols : (k + 1) * out_cols] = both_k.astype(bf16)
    at = part * out_cols
    towers = jnp.concatenate([tower_ref[0], tower_ref[1]], axis=0)
    out_ref[:, at : at + LANES] = towers.astype(bf16)
    tile = valid_ref.shape[1] // 2
    own = valid_ref[:, pl.ds(pl.multiple_of(lax.axis_index("field") * tile, tile), tile)].astype(f32)
    ones = jnp.sum(jnp.sum(own, axis=1, keepdims=True), axis=0, keepdims=True).astype(jnp.int32)
    ones = jnp.broadcast_to(ones, (2 * rows, LANES))
    row, lane = (lax.broadcasted_iota(jnp.int32, ones.shape, d) for d in range(2))
    digits = jnp.where(lane == 2, ones >> 16, jnp.where(lane == 1, ones >> 8, ones) & 255)
    digits = jnp.where((row == 0) & (lane < 3), digits, 0).astype(f32)
    out_ref[:, at + LANES :] = digits.astype(bf16)


def rows_kernel(in_ref, got_ref, valid_ref, label_ref, domain_ref, x_ref, xt_ref, flags_ref, by_row_ref):
    micro, rows_dev, width = in_ref.shape
    tile = rows_dev // 2
    start = pl.multiple_of(lax.axis_index("field") * tile, tile)
    for m in range(micro):
        rows = slice(m * tile, (m + 1) * tile)
        x = jnp.concatenate([in_ref[m, pl.ds(start, tile), :], got_ref[rows, :]], axis=1)
        x_ref[rows, :] = x
        xt_ref[:, rows] = x.T
        kinds = [ref[m : m + 1, pl.ds(start, tile)].astype(f32) for ref in (valid_ref, label_ref, domain_ref)]
        flags = jnp.concatenate(kinds + [jnp.zeros((5, tile), f32)], axis=0)
        flags_ref[:, rows] = flags
        by_row_ref[rows, :] = flags.T


def first_kernel(places, own_ref, oth_ref, x_ref, xt_ref, flags_ref, ga_ref, gs_ref, gate_ref, w_ref):
    half = own_ref.shape[0]
    count, wide = ga_ref.shape
    experts = wide // half
    tile = count // 2
    places.start()

    def put(side, place, rr, ff):
        src = own_ref if side == 0 else oth_ref
        row = (ff ^ places.field) * half + rr * BLOCK
        w_ref[rows16(row), :] = src[rows16(place * BLOCK), :]

    places.each(half // BLOCK, put)
    logits = dot(w_ref[:, wide:].T, xt_ref[...])
    logits = jnp.where(flags_ref[2:3, :] == 0.0, logits[0:experts], logits[experts : 2 * experts])
    raised = jnp.exp(logits - jnp.max(logits, axis=0, keepdims=True))
    gate = raised / jnp.sum(raised, axis=0, keepdims=True)
    gate_ref[...] = jnp.concatenate([gate, gate], axis=0).T

    def step(i, carry):
        rows = pl.ds(pl.multiple_of(i * tile, tile), tile)
        x = x_ref[rows, :]
        gate = 0.5 * gate_ref[rows, :]
        for k in range(experts):
            cols = slice(k * half, (k + 1) * half)
            pre = dot(x, w_ref[:, cols])
            low = 0.5 * pre
            up = 1.0 + jnp.tanh(low)
            scaled = gate[:, k : k + 1] * up
            ga_ref[rows, cols] = (scaled * pre).astype(bf16)
            gs_ref[rows, cols] = (scaled * (1.0 + pre - low * up)).astype(bf16)
        return carry

    lax.fori_loop(0, 2, step, 0)


def second_kernel(
    places,
    own_ref,
    oth_ref,
    ga_ref,
    flags_ref,
    by_row_ref,
    to_ref,
    w_ref,
    dm_ref,
    side_ref,
    keep_ref,
    send_ref,
    ti_ref,
    mix_ref,
    g_ref,
    gti_ref,
):
    half = own_ref.shape[0]
    pairs = half // BLOCK
    count, out_cols = dm_ref.shape
    hidden = half
    wide = ga_ref.shape[1]
    experts = wide // hidden
    part = experts // 2

    places.start()

    digits = jnp.zeros((BLOCK, LANES), f32)
    for side in range(2):
        for j in range(pairs // 2):
            src = own_ref if side == 0 else oth_ref
            (place0, rr, _), (place1, _, _) = places.block(side, 2 * j), places.block(side, 2 * j + 1)
            a0 = src[rows16(place0 * BLOCK), :].astype(f32)
            a1 = src[rows16(place1 * BLOCK), :].astype(f32)
            row = rr * BLOCK
            upper = jnp.concatenate([a0[:8], a1[:8]], axis=0).astype(bf16)
            lower = jnp.concatenate([a0[8:], a1[8:]], axis=0).astype(bf16)
            at = part * out_cols
            for k in range(part):
                cols = slice(k * out_cols, (k + 1) * out_cols)
                w_ref[rows16(k * hidden + row), :] = upper[:, cols]
                w_ref[rows16((k + part) * hidden + row), :] = lower[:, cols]
            ti_ref[rows16(row), 0:LANES] = upper[:, at : at + LANES]
            ti_ref[rows16(row), LANES : 2 * LANES] = lower[:, at : at + LANES]
            digits = digits + (a0 + a1)[:, at + LANES :]
    lane = lax.broadcasted_iota(jnp.int32, digits.shape, 1)
    scale = jnp.where(lane == 0, 1.0, jnp.where(lane == 1, 256.0, jnp.where(lane == 2, 65536.0, 0.0)))
    real = jnp.sum(jnp.sum(digits * scale, axis=1, keepdims=True), axis=0, keepdims=True)

    domain = by_row_ref[:, 2:3]
    heads = to_ref[...].astype(bf16).astype(f32)
    empty = jnp.zeros((6, LANES), f32)
    tile = count // 4
    for i in range(4):
        rows = slice(i * tile, (i + 1) * tile)
        mix_ref[rows, :] = dot(ga_ref[rows, :], w_ref[...]).astype(bf16)
    mixed = mix_ref[...]
    tpre = dot(mixed, ti_ref[...])
    tpre = jnp.where(domain == 0.0, tpre[:, :LANES], tpre[:, LANES:])
    s = sigmoid(tpre)
    act = (tpre * s).astype(bf16)
    logits = dot_t(jnp.concatenate([heads, empty], axis=0).astype(bf16), act)
    valid, label, first = flags_ref[0:1, :], flags_ref[1:2, :], flags_ref[2:3, :] == 0.0
    chosen = jnp.where(first, logits[0:1, :], logits[1:2, :])
    soft = jnp.maximum(chosen, 0.0) + jnp.log1p(jnp.exp(-jnp.abs(chosen)))
    loss = jnp.sum(valid * (soft - label * chosen), axis=1, keepdims=True) / real
    dlogit = valid * (sigmoid(chosen) - label) / real
    dlogit = jnp.concatenate(
        [jnp.where(first, dlogit, 0.0), jnp.where(first, 0.0, dlogit), jnp.zeros((6, count), f32)], axis=0
    ).astype(bf16)
    apart = jnp.concatenate(
        [
            jnp.concatenate([heads[0:1], jnp.zeros((1, LANES), f32)], axis=1),
            jnp.concatenate([jnp.zeros((1, LANES), f32), heads[1:2]], axis=1),
            jnp.concatenate([empty, empty], axis=1),
        ],
        axis=0,
    ).astype(bf16)
    slope = s * (1.0 + tpre * (1.0 - s))
    dtpre = (t_dot(dlogit, apart) * jnp.concatenate([slope, slope], axis=1)).astype(bf16)
    dm_ref[...] = dot_t(dtpre, ti_ref[...]).astype(bf16)
    head_grad = dot(dlogit, act)
    side_ref[...] = jnp.zeros_like(side_ref)
    side_ref[0:1, 0:LANES] = head_grad[0:1]
    side_ref[0:1, LANES : 2 * LANES] = head_grad[1:2]
    side_ref[0:1, 2 * LANES : 3 * LANES] = jnp.broadcast_to(loss, (1, LANES))
    gti_ref[...] = t_dot(mixed, dtpre)

    def pack(above, below, cols):
        def put(side, place, rr, ff):
            dst = keep_ref if side == 0 else send_ref
            row = pl.ds(pl.multiple_of(rr * BLOCK + ff * 8, 8), 8)
            tile = jnp.concatenate([above(row), below(row)], axis=0)
            dst[rows16(place * BLOCK), cols] = tile.astype(dst.dtype)

        places.each(pairs, put)

    for k in range(part):
        g_ref[k] = t_dot(ga_ref[:, k * hidden : (k + 1) * hidden], dm_ref[...])
        g_ref[k + part] = t_dot(ga_ref[:, (k + part) * hidden : (k + part + 1) * hidden], dm_ref[...])
        pack(
            lambda row: g_ref[k, row, :],
            lambda row: g_ref[k + part, row, :],
            slice(k * out_cols, (k + 1) * out_cols),
        )
    at = part * out_cols
    pack(lambda row: gti_ref[row, 0:LANES], lambda row: gti_ref[row, LANES : 2 * LANES], slice(at, at + LANES))


def back_part(places, ks, w_ref, dm_ref, ga_ref, gs_ref, xt_ref, dp_ref, keep_ref, send_ref, g_ref):
    half = keep_ref.shape[0]
    tile = dm_ref.shape[0] // 4
    places.start()
    terms = []
    for at, k in enumerate(ks):
        cols, here = slice(k * half, (k + 1) * half), slice(at * half, (at + 1) * half)
        sums = []
        for i in range(4):
            rows = slice(i * tile, (i + 1) * tile)
            u = dot_t(dm_ref[rows, :], w_ref[cols, :])
            dp_ref[rows, here] = (u * gs_ref[rows, cols].astype(f32)).astype(bf16)
            sums.append(jnp.sum(u * ga_ref[rows, cols].astype(f32), axis=1, keepdims=True))
        terms.append(sums)
        g_ref[:, here] = dot(xt_ref[...], dp_ref[:, here])
        back_pack(places, here, keep_ref, send_ref, g_ref)
    return terms


def back_pack(places, cols, keep_ref, send_ref, g_ref):
    half = keep_ref.shape[0]

    def put(side, place, rr, ff):
        dst = keep_ref if side == 0 else send_ref
        row = (ff ^ places.field) * half + rr * BLOCK
        dst[rows16(place * BLOCK), cols] = g_ref[rows16(row), cols].astype(dst.dtype)

    places.each(half // BLOCK, put)


def set_terms(q_ref, terms, ks):
    tile = q_ref.shape[0] // 4
    experts = q_ref.shape[1] // 2
    lane = lax.broadcasted_iota(jnp.int32, (tile, 2 * experts), 1)
    for i in range(4):
        rows = slice(i * tile, (i + 1) * tile)
        q = q_ref[rows, :]
        for k, sums in zip(ks, terms):
            q = jnp.where((lane == k) | (lane == k + experts), sums[i], q)
        q_ref[rows, :] = q


def back_first_kernel(
    places, ks, w_ref, dm_ref, ga_ref, gs_ref, xt_ref, dp_ref, keep_ref, send_ref, q_ref, g_ref
):
    terms = back_part(places, ks, w_ref, dm_ref, ga_ref, gs_ref, xt_ref, dp_ref, keep_ref, send_ref, g_ref)
    q_ref[...] = jnp.zeros_like(q_ref)
    set_terms(q_ref, terms, ks)


def back_last_kernel(
    places,
    ks,
    w_ref,
    dm_ref,
    ga_ref,
    gs_ref,
    xt_ref,
    before_ref,
    gate_ref,
    by_row_ref,
    dp_ref,
    keep_ref,
    send_ref,
    dg_ref,
    g_ref,
    q_ref,
):
    terms = back_part(places, ks, w_ref, dm_ref, ga_ref, gs_ref, xt_ref, dp_ref, keep_ref, send_ref, g_ref)
    q_ref[...] = before_ref[...]
    set_terms(q_ref, terms, ks)
    q = q_ref[...]
    experts = q.shape[1] // 2
    lane = lax.broadcasted_iota(jnp.int32, q.shape, 1)
    total = 0.5 * jnp.sum(q, axis=1, keepdims=True)
    mine = (lane // experts).astype(f32) == by_row_ref[:, 2:3]
    dg_ref[...] = jnp.zeros_like(dg_ref)
    dg_ref[:, 0 : 2 * experts] = jnp.where(mine, q - gate_ref[...] * total, 0.0).astype(bf16)
    cols = slice(dp_ref.shape[1], dp_ref.shape[1] + LANES)
    g_ref[:, cols] = dot(xt_ref[...], dg_ref[...])
    back_pack(places, cols, keep_ref, send_ref, g_ref)


def input_kernel(at, low_ref, high_ref, dg_ref, w_ref, keep_ref, send_ref):
    part = low_ref.shape[1]
    wide = part + high_ref.shape[1]
    grad = dot_t(low_ref[...], w_ref[:, 0:part]) + dot_t(high_ref[...], w_ref[:, part:wide])
    grad = grad + dot_t(dg_ref[...], w_ref[:, wide:])
    half = grad.shape[1] // 2
    keep_ref[0] = grad[:, :half]
    send_ref[...] = grad[:, half:].astype(bf16)


def update_kernel(rates, sum_a, got_a, sum_b, got_b, side, dx_ref, held_ref, *refs):
    weights, velocities, averages = refs[0:5], refs[5:10], refs[10:15]
    grad_ref, outs, (wide_ref, sems) = refs[15], refs[16:31], refs[31:]
    micro, tile, _ = wide_ref.shape
    start = pl.multiple_of((1 - lax.axis_index("field")) * tile, tile)
    copies = []
    for m in range(micro):
        wide_ref[m] = dx_ref[m * tile : (m + 1) * tile, :].astype(f32)
        copy = pltpu.make_async_copy(wide_ref.at[m], grad_ref.at[m, pl.ds(start, tile), :], sems.at[m])
        copy.start()
        copies.append(copy)
    wide = weights[0].shape[1]
    gates = weights[1].shape[1]
    experts, rows, out_cols = weights[2].shape
    tasks = weights[3].shape[0]
    part = experts // 2

    def renew(at, place, gradient):
        velocity = momentum_mu * velocities[at][place] + gradient
        weight = weights[at][place] - rates[at] * (gradient + momentum_mu * velocity)
        outs[3 * at][place] = weight
        outs[3 * at + 1][place] = velocity
        outs[3 * at + 2][place] = average_keep * averages[at][place] + (1.0 - average_keep) * weight

    first = sum_a[0 : got_a.shape[0], :] + got_a[...].astype(f32)
    renew(0, (slice(None), slice(None)), first[:, :wide])
    renew(1, (slice(None), slice(None)), first[:, wide : wide + gates])
    count = got_b.shape[0] - 8
    second = sum_b[0:count, :] + got_b[0:count, :].astype(f32)
    for k in range(experts):
        top = (k // part) * rows
        renew(2, k, second[top : top + rows, (k % part) * out_cols : (k % part + 1) * out_cols])
    for t in range(tasks):
        renew(3, t, second[t * rows : (t + 1) * rows, part * out_cols :])
        renew(4, (slice(t, t + 1), slice(None)), side[0:1, t * LANES : (t + 1) * LANES])
    for copy in copies:
        copy.wait()


class Cube:
    def __init__(self):
        self.rows = lax.axis_size("rows")
        self.fields = lax.axis_size("field")
        bits = int(math.log2(self.rows))
        assert 1 << bits == self.rows and self.fields == 2
        outer = [("row", b) for b in range(bits - 1, 1, -1)]
        self.order = outer + [("mixed", 0), ("mixed", 1)]
        self.other_order = outer + [("mixed", 1), ("mixed", 0)]
        self.core = ("row", 0)

    def pairs(self, step):
        kind, which = step
        pairs = []
        for r in range(self.rows):
            for f in range(self.fields):
                if kind == "row":
                    to = (r ^ (1 << which), f)
                else:
                    to = (r ^ 2, f) if (r & 1) == which else (r, f ^ 1)
                pairs.append((r * self.fields + f, to[0] * self.fields + to[1]))
        return pairs

    def swap(self, values, step):
        return lax.ppermute(values, both, self.pairs(step))

    def place(self, order, rr, ff, r, f):
        dr, df, core = rr ^ r, ff ^ f, r & 1
        out = jnp.zeros_like(dr + df)
        for s, (kind, which) in enumerate(order):
            if kind == "row":
                bit = (dr >> which) & 1
            else:
                bit = jnp.where(core == which, (dr >> 1) & 1, df)
            out = out + (bit << s)
        return out


def gather_two(cube, block_a, make_b, x):
    got_a = cube.swap(block_a, cube.order[0])
    block_a = jnp.concatenate([block_a, got_a], axis=0)
    block_b = make_b(block_a)
    for at in range(1, len(cube.order)):
        got_a = cube.swap(block_a, cube.order[at])
        got_b = cube.swap(block_b, cube.order[at - 1])
        if at + 1 == len(cube.order):
            got_a = after(got_a, x)
        block_a = jnp.concatenate([block_a, after(got_a, got_b)], axis=0)
        block_b = jnp.concatenate([block_b, after(got_b, block_a)], axis=0)
    oth_a = cube.swap(block_a, cube.core)
    return block_a, oth_a, block_b, cube.swap(block_b, cube.order[-1])


def after(values, *earlier):
    return lax.optimization_barrier((values,) + earlier)[0]


def fold(total, got):
    rows = got.shape[0]
    total = total[:rows] + got.astype(f32)
    half = rows // 2
    return total, total[half:].astype(bf16)


def split_two(values):
    high = lax.reduce_precision(values, 8, 7)
    low = lax.reduce_precision(values - high, 8, 7)
    return jnp.concatenate([high, low], axis=0).astype(bf16)


def join_two(rows):
    rows = rows.astype(f32)
    half = rows.shape[0] // 2
    return rows[:half] + rows[half:]


def beside(part, side):
    mine = split_two(side)
    return jnp.concatenate([part, mine], axis=0), join_two(mine)


def fold_beside(total, side, got):
    rows = got.shape[0] - 8
    total, part = fold(total, got[:rows])
    message, side = beside(part, side + join_two(got[rows:]))
    return total, message, side


def shape(dims, dtype):
    return jax.ShapeDtypeStruct(dims, dtype)


def params(limit):
    return pltpu.CompilerParams(vmem_limit_bytes=limit << 20)


vmem = pl.BlockSpec()


def cost(flops):
    return pl.CostEstimate(flops=flops, bytes_accessed=8 << 20, transcendentals=0)


def on_device(
    inputs,
    valid_mask,
    labels,
    domains,
    expert_in,
    gate_in,
    expert_out,
    tower_in,
    tower_out,
    velocity_expert_in,
    velocity_gate_in,
    velocity_expert_out,
    velocity_tower_in,
    velocity_tower_out,
    average_expert_in,
    average_gate_in,
    average_expert_out,
    average_tower_in,
    average_tower_out,
):
    cube = Cube()
    micro, rows_dev, width = inputs.shape
    fields = cube.fields
    tile = rows_dev // fields
    rows_own = micro * tile
    experts, second_rows, out_cols = expert_out.shape
    tasks, tower_cols = tower_out.shape
    wide = expert_in.shape[1]
    hidden = wide // experts
    first_rows = expert_in.shape[0]
    part = experts // 2
    total_rows = micro * rows_dev * cube.rows
    r, f = lax.axis_index("rows"), lax.axis_index("field")

    def own_half(values, which):
        return lax.dynamic_slice_in_dim(values, which * tile, tile, 1)

    block_a = pl.pallas_call(
        pack_a_kernel,
        out_shape=shape((first_rows, wide + LANES), bf16),
        compiler_params=params(4),
        name="pack_a",
    )(expert_in, gate_in)

    def make_b(earlier):
        return pl.pallas_call(
            pack_b_kernel,
            out_shape=shape((2 * second_rows, part * out_cols + 2 * LANES), bf16),
            compiler_params=params(4),
            name="pack_b",
        )(expert_out, tower_in, after(valid_mask, earlier))

    x_send = own_half(after(inputs, block_a), 1 - f).reshape(rows_own, width)
    x_got = lax.ppermute(x_send, "field", [(0, 1), (1, 0)])

    pairs = width // BLOCK
    fit = first_rows == BLOCK
    places = Places(fit, cube.order)
    sent = bf16 if fit else f32

    a_cols, b_cols = wide + LANES, part * out_cols + LANES
    heads = tasks * tower_cols

    x, x_t, flags, by_row = pl.pallas_call(
        rows_kernel,
        out_shape=[
            shape((rows_own, 2 * width), bf16),
            shape((2 * width, rows_own), bf16),
            shape((8, rows_own), f32),
            shape((rows_own, 8), f32),
        ],
        compiler_params=params(8),
        cost_estimate=cost(1 << 20),
        name="rows",
    )(inputs, x_got, valid_mask, labels, domains)

    own_a, oth_a, own_b, got_b = gather_two(cube, block_a, make_b, x)
    if not fit:
        rows_a = first_sorted(cube, cube.order, r, f, width, first_rows)
        own_a, oth_a = jnp.split(jnp.take(jnp.concatenate([own_a, oth_a]), rows_a, axis=0), 2)
    ga, gs, gate, first_w = pl.pallas_call(
        functools.partial(first_kernel, places),
        out_shape=[
            shape((rows_own, wide), bf16),
            shape((rows_own, wide), bf16),
            shape((rows_own, tasks * experts), f32),
            shape((2 * width, a_cols), bf16),
        ],
        compiler_params=params(12),
        cost_estimate=cost(4 * rows_own * 2 * width * a_cols),
        name="first",
    )(own_a, oth_a, x, x_t, flags)

    own_b = jnp.concatenate([own_b, after(got_b, gate)], axis=0)
    oth_b = cube.swap(own_b, cube.core)
    if not fit:
        rows_b = second_sorted(cube, cube.order, r, f, width, second_rows)
        own_b, oth_b = jnp.split(jnp.take(jnp.concatenate([own_b, oth_b]), rows_b, axis=0), 2)
    second_w, dmixed, side, keep_b, send_b = pl.pallas_call(
        functools.partial(second_kernel, places),
        out_shape=[
            shape((wide, out_cols), bf16),
            shape((rows_own, out_cols), bf16),
            shape((8, b_cols), f32),
            shape((width, b_cols), f32),
            shape((width, b_cols), sent),
        ],
        scratch_shapes=[
            pltpu.VMEM((out_cols, heads), bf16),
            pltpu.VMEM((rows_own, out_cols), bf16),
            pltpu.VMEM((experts, hidden, out_cols), f32),
            pltpu.VMEM((out_cols, heads), f32),
        ],
        compiler_params=params(20),
        name="second",
    )(own_b, oth_b, ga, flags, by_row, tower_out)
    if not fit:
        keep_b, send_b = unsorted(keep_b, send_b, rows_b)
    message, side = beside(send_b, side[:4])
    steps = [cube.core] + cube.order[::-1]
    got_b = cube.swap(message, steps[0])

    cut = 7
    low_cols, high_cols = cut * hidden, (experts - cut) * hidden + LANES
    dpre_low, keep_low, send_low, terms = pl.pallas_call(
        functools.partial(back_first_kernel, places, range(cut)),
        out_shape=[
            shape((rows_own, low_cols), bf16),
            shape((width, low_cols), f32),
            shape((width, low_cols), sent),
            shape((rows_own, tasks * experts), f32),
        ],
        scratch_shapes=[pltpu.VMEM((2 * width, low_cols), f32)],
        compiler_params=params(16),
        name="back_first",
    )(after(second_w, message), dmixed, ga, gs, x_t)
    if not fit:
        keep_low, send_low = unsorted(keep_low, send_low, rows_a)
    got_low = cube.swap(send_low, steps[0])
    sum_b, message, side = fold_beside(keep_b, side, after(got_b, send_low))
    got_b = cube.swap(message, steps[1])
    dpre_high, keep_high, send_high, dgate = pl.pallas_call(
        functools.partial(back_last_kernel, places, range(cut, experts)),
        out_shape=[
            shape((rows_own, high_cols - LANES), bf16),
            shape((width, high_cols), f32),
            shape((width, high_cols), sent),
            shape((rows_own, LANES), bf16),
        ],
        scratch_shapes=[
            pltpu.VMEM((2 * width, high_cols), f32),
            pltpu.VMEM((rows_own, tasks * experts), f32),
        ],
        compiler_params=params(16),
        name="back_last",
    )(second_w, dmixed, ga, gs, x_t, after(terms, message), gate, by_row)
    if not fit:
        keep_high, send_high = unsorted(keep_high, send_high, rows_a)
    got_high = cube.swap(send_high, steps[0])
    keep_a = jnp.concatenate([keep_low, keep_high], axis=1)
    got_a = jnp.concatenate([after(got_low, send_high), got_high], axis=1)
    sum_a, next_a = fold(keep_a, got_a)
    grad_keep, grad_send = pl.pallas_call(
        input_kernel,
        grid_spec=pltpu.PrefetchScalarGridSpec(
            num_scalar_prefetch=1,
            grid=(micro,),
            in_specs=[
                pl.BlockSpec((tile, low_cols), lambda i, at: (i, 0)),
            pl.BlockSpec((tile, high_cols - LANES), lambda i, at: (i, 0)),
                pl.BlockSpec((tile, LANES), lambda i, at: (i, 0)),
                pl.BlockSpec((2 * width, a_cols), lambda i, at: (0, 0)),
            ],
            out_specs=[
                pl.BlockSpec((1, tile, width), lambda i, at: (i, at[0], 0)),
                pl.BlockSpec((tile, width), lambda i, at: (i, 0)),
            ],
        ),
        out_shape=[
            shape((micro, rows_dev, width), f32),
            shape((rows_own, width), bf16),
        ],
        compiler_params=params(12),
        cost_estimate=cost(4 * rows_own * 2 * width * a_cols),
        name="input",
    )(f.astype(jnp.int32).reshape(1), dpre_low, dpre_high, after(dgate, next_a), first_w)
    for at in range(1, len(steps)):
        got_a = cube.swap(next_a, steps[at])
        if at + 1 < len(steps):
            sum_b, message, side = fold_beside(sum_b, side, after(got_b, next_a))
            got_b = cube.swap(message, steps[at + 1])
            sum_a, next_a = fold(sum_a, after(got_a, got_b, grad_send))
        if at == 1:
            grad_got = lax.ppermute(after(grad_send, next_a), "field", [(0, 1), (1, 0)])
    side = side + join_two(got_b[got_b.shape[0] - 8 :])
    weights = (expert_in, gate_in, expert_out, tower_in, tower_out)
    velocities = (
        velocity_expert_in,
        velocity_gate_in,
        velocity_expert_out,
        velocity_tower_in,
        velocity_tower_out,
    )
    averages = (
        average_expert_in,
        average_gate_in,
        average_expert_out,
        average_tower_in,
        average_tower_out,
    )
    rates = [base * math.sqrt(total_rows) for base in rate_bases]
    hbm = pl.BlockSpec(memory_space=pl.ANY)
    input_grad, *updated = pl.pallas_call(
        functools.partial(update_kernel, rates),
        in_specs=[vmem] * 6 + [hbm] + [vmem] * 15,
        out_specs=[hbm] + [vmem] * 15,
        out_shape=[shape((micro, rows_dev, width), f32)]
        + [shape(w.shape, f32) for w in weights for _ in range(3)],
        scratch_shapes=[pltpu.VMEM((micro, tile, width), f32), pltpu.SemaphoreType.DMA((micro,))],
        input_output_aliases={6: 0},
        compiler_params=params(8),
        cost_estimate=cost(1 << 20),
        name="update",
    )(sum_a, got_a, sum_b, got_b, side, grad_got, grad_keep, *weights, *velocities, *averages)
    return (side[0, heads], input_grad, *updated)


def owner_rows(cube, order, r, f, rr, ff, inner, size):
    held = cube.rows * cube.fields // 2
    same = (rr & 1) == (r & 1)
    here = cube.place(order, rr, ff, r, f)
    there = cube.place(order, rr, ff, r ^ 1, f)
    return (jnp.where(same, here, held + there) * size + inner).reshape(-1)


def block_grid(width):
    side = np.arange(2)[:, None, None, None]
    j = np.arange(width // (2 * BLOCK))[None, :, None, None]
    ff = np.arange(2)[None, None, :, None]
    inner = np.arange(BLOCK)[None, None, None, :]
    ahead = (2 * j + side) * BLOCK + 0 * ff + 0 * inner
    full = np.zeros(ahead.shape, np.int32)
    return ahead.astype(np.int32), full + ff.astype(np.int32), full + inner.astype(np.int32)


def first_sorted(cube, order, r, f, width, size):
    ahead, ff, inner = block_grid(width)
    at = ahead + inner
    return owner_rows(
        cube, order, r, f, jnp.asarray(at // size), jnp.asarray(ff), jnp.asarray(at % size), size
    )


def second_sorted(cube, order, r, f, width, size):
    ahead, ff, inner = block_grid(width)
    at = ahead + ff * 8 + inner % 8
    owner = at // size
    held = at % size + size * (inner // 8)
    return owner_rows(
        cube, order, r, f, jnp.asarray(owner // 2), jnp.asarray(owner % 2), jnp.asarray(held), 2 * size
    )


def unsorted(keep, send, rows):
    every = jnp.concatenate([keep, send])
    back = jnp.zeros_like(rows).at[rows].set(jnp.arange(rows.shape[0], dtype=rows.dtype))
    keep, send = jnp.split(jnp.take(every, back, axis=0), 2)
    return keep, send.astype(bf16)


def solution(mesh):
    first = P(("field", "rows"), None)
    second = P(None, ("rows", "field"), None)
    by_row = P(None, "rows")
    inputs = P(None, "rows", "field")
    weights = (first, first, second, second, P())
    return jax.shard_map(
        on_device,
        mesh=mesh,
        in_specs=(inputs, by_row, by_row, by_row) + weights * 3,
        out_specs=(P(), inputs) + tuple(spec for spec in weights for _ in range(3)),
        check_vma=False,
    )
```

```python
import functools
import math

import jax
import jax.numpy as jnp
import numpy as np
from jax import lax
from jax.experimental import pallas as pl
from jax.experimental.pallas import tpu as pltpu
from jax.sharding import PartitionSpec as P

momentum_mu = 0.5
average_keep = 0.5
rate_bases = (17.0, 1.0, 24.0, 4.0, 0.25)
both = ("rows", "field")
f32 = jnp.float32
bf16 = jnp.bfloat16
BLOCK = 16
LANES = 128


def dot(a, b):
    return lax.dot_general(a, b, (((1,), (0,)), ((), ())), preferred_element_type=f32)


def dot_t(a, b):
    return lax.dot_general(a, b, (((1,), (1,)), ((), ())), preferred_element_type=f32)


def t_dot(a, b):
    return lax.dot_general(a, b, (((0,), (0,)), ((), ())), preferred_element_type=f32)


def sigmoid(v):
    return 0.5 + 0.5 * jnp.tanh(0.5 * v)


def rows16(start):
    return pl.ds(pl.multiple_of(start, BLOCK), BLOCK)


class Places:
    def __init__(self, fit, order):
        self.fit, self.order = fit, order

    def bits(self, core, rr, ff):
        out = 0
        for s, (kind, which) in enumerate(self.order):
            if kind == "row":
                bit = (rr >> which) & 1
            else:
                bit = (rr >> 1) & 1 if core == which else ff
            out = out | (bit << s)
        return out

    def start(self):
        r, self.field = lax.axis_index("rows"), lax.axis_index("field")
        self.core = r & 1 if self.fit else jnp.int32(0)
        self.bases = [self.bits(core, r, self.field) for core in range(2)]

    def block(self, side, j):
        core = self.core if side == 0 else 1 - self.core
        pair, ff = j // 2, j % 2
        if not self.fit:
            return j, 2 * pair + side, ff
        ways = [base ^ self.bits(c, 2 * pair, ff) for c, base in enumerate(self.bases)]
        return jnp.where(core == 0, ways[0], ways[1]), 2 * pair + core, ff

    def each(self, pairs, body):
        for j in range(pairs):
            for side in range(2):
                body(side, *self.block(side, j))


def pack_a_kernel(expert_ref, gate_ref, out_ref):
    wide, gates = expert_ref.shape[1], gate_ref.shape[1]
    out_ref[:, 0:wide] = expert_ref[...].astype(bf16)
    out_ref[:, wide:] = jnp.zeros((out_ref.shape[0], LANES), bf16)
    out_ref[:, wide : wide + gates] = gate_ref[...].astype(bf16)


def pack_b_kernel(expert_ref, tower_ref, valid_ref, out_ref):
    experts, rows, out_cols = expert_ref.shape
    part = experts // 2
    for k in range(part):
        both_k = jnp.concatenate([expert_ref[k], expert_ref[k + part]], axis=0)
        out_ref[:, k * out_cols : (k + 1) * out_cols] = both_k.astype(bf16)
    at = part * out_cols
    towers = jnp.concatenate([tower_ref[0], tower_ref[1]], axis=0)
    out_ref[:, at : at + LANES] = towers.astype(bf16)
    tile = valid_ref.shape[1] // 2
    own = valid_ref[:, pl.ds(pl.multiple_of(lax.axis_index("field") * tile, tile), tile)].astype(f32)
    ones = jnp.sum(jnp.sum(own, axis=1, keepdims=True), axis=0, keepdims=True).astype(jnp.int32)
    ones = jnp.broadcast_to(ones, (2 * rows, LANES))
    row, lane = (lax.broadcasted_iota(jnp.int32, ones.shape, d) for d in range(2))
    digits = jnp.where(lane == 2, ones >> 16, jnp.where(lane == 1, ones >> 8, ones) & 255)
    digits = jnp.where((row == 0) & (lane < 3), digits, 0).astype(f32)
    out_ref[:, at + LANES :] = digits.astype(bf16)


def rows_kernel(in_ref, got_ref, valid_ref, label_ref, domain_ref, x_ref, xt_ref, flags_ref, by_row_ref):
    micro, rows_dev, width = in_ref.shape
    tile = rows_dev // 2
    start = pl.multiple_of(lax.axis_index("field") * tile, tile)
    for m in range(micro):
        rows = slice(m * tile, (m + 1) * tile)
        x = jnp.concatenate([in_ref[m, pl.ds(start, tile), :], got_ref[rows, :]], axis=1)
        x_ref[rows, :] = x
        xt_ref[:, rows] = x.T
        kinds = [ref[m : m + 1, pl.ds(start, tile)].astype(f32) for ref in (valid_ref, label_ref, domain_ref)]
        flags = jnp.concatenate(kinds + [jnp.zeros((5, tile), f32)], axis=0)
        flags_ref[:, rows] = flags
        by_row_ref[rows, :] = flags.T


def first_kernel(places, own_ref, oth_ref, x_ref, xt_ref, flags_ref, ga_ref, gs_ref, gate_ref, w_ref):
    half = own_ref.shape[0]
    count, wide = ga_ref.shape
    experts = wide // half
    tile = count // 4
    places.start()

    def put(side, place, rr, ff):
        src = own_ref if side == 0 else oth_ref
        row = (ff ^ places.field) * half + rr * BLOCK
        w_ref[rows16(row), :] = src[rows16(place * BLOCK), :]

    places.each(half // BLOCK, put)
    logits = dot(w_ref[:, wide:].T, xt_ref[...])
    logits = jnp.where(flags_ref[2:3, :] == 0.0, logits[0:experts], logits[experts : 2 * experts])
    raised = jnp.exp(logits - jnp.max(logits, axis=0, keepdims=True))
    gate = raised / jnp.sum(raised, axis=0, keepdims=True)
    gate_ref[...] = jnp.concatenate([gate, gate], axis=0).T

    for i in range(4):
        rows = slice(i * tile, (i + 1) * tile)
        x = x_ref[rows, :]
        gate = 0.5 * gate_ref[rows, :]
        for k in range(experts):
            cols = slice(k * half, (k + 1) * half)
            pre = dot(x, w_ref[:, cols])
            low = 0.5 * pre
            up = 1.0 + jnp.tanh(low)
            scaled = gate[:, k : k + 1] * up
            ga_ref[rows, cols] = (scaled * pre).astype(bf16)
            gs_ref[rows, cols] = (scaled * (1.0 + pre - low * up)).astype(bf16)


def second_kernel(
    places,
    own_ref,
    oth_ref,
    ga_ref,
    flags_ref,
    by_row_ref,
    to_ref,
    w_ref,
    dm_ref,
    side_ref,
    keep_ref,
    send_ref,
    ti_ref,
    mix_ref,
    g_ref,
    gti_ref,
):
    half = own_ref.shape[0]
    pairs = half // BLOCK
    count, out_cols = dm_ref.shape
    hidden = half
    wide = ga_ref.shape[1]
    experts = wide // hidden
    part = experts // 2

    places.start()

    digits = jnp.zeros((BLOCK, LANES), f32)
    for side in range(2):
        for j in range(pairs // 2):
            src = own_ref if side == 0 else oth_ref
            (place0, rr, _), (place1, _, _) = places.block(side, 2 * j), places.block(side, 2 * j + 1)
            a0 = src[rows16(place0 * BLOCK), :].astype(f32)
            a1 = src[rows16(place1 * BLOCK), :].astype(f32)
            row = rr * BLOCK
            upper = jnp.concatenate([a0[:8], a1[:8]], axis=0).astype(bf16)
            lower = jnp.concatenate([a0[8:], a1[8:]], axis=0).astype(bf16)
            at = part * out_cols
            for k in range(part):
                cols = slice(k * out_cols, (k + 1) * out_cols)
                w_ref[rows16(k * hidden + row), :] = upper[:, cols]
                w_ref[rows16((k + part) * hidden + row), :] = lower[:, cols]
            ti_ref[rows16(row), 0:LANES] = upper[:, at : at + LANES]
            ti_ref[rows16(row), LANES : 2 * LANES] = lower[:, at : at + LANES]
            digits = digits + (a0 + a1)[:, at + LANES :]
    lane = lax.broadcasted_iota(jnp.int32, digits.shape, 1)
    scale = jnp.where(lane == 0, 1.0, jnp.where(lane == 1, 256.0, jnp.where(lane == 2, 65536.0, 0.0)))
    real = jnp.sum(jnp.sum(digits * scale, axis=1, keepdims=True), axis=0, keepdims=True)

    domain = by_row_ref[:, 2:3]
    heads = to_ref[...].astype(bf16).astype(f32)
    empty = jnp.zeros((6, LANES), f32)
    tile = count // 4
    for i in range(4):
        rows = slice(i * tile, (i + 1) * tile)
        mix_ref[rows, :] = dot(ga_ref[rows, :], w_ref[...]).astype(bf16)
    mixed = mix_ref[...]
    tpre = dot(mixed, ti_ref[...])
    tpre = jnp.where(domain == 0.0, tpre[:, :LANES], tpre[:, LANES:])
    s = sigmoid(tpre)
    act = (tpre * s).astype(bf16)
    logits = dot_t(jnp.concatenate([heads, empty], axis=0).astype(bf16), act)
    valid, label, first = flags_ref[0:1, :], flags_ref[1:2, :], flags_ref[2:3, :] == 0.0
    chosen = jnp.where(first, logits[0:1, :], logits[1:2, :])
    soft = jnp.maximum(chosen, 0.0) + jnp.log1p(jnp.exp(-jnp.abs(chosen)))
    loss = jnp.sum(valid * (soft - label * chosen), axis=1, keepdims=True) / real
    dlogit = valid * (sigmoid(chosen) - label) / real
    dlogit = jnp.concatenate(
        [jnp.where(first, dlogit, 0.0), jnp.where(first, 0.0, dlogit), jnp.zeros((6, count), f32)], axis=0
    ).astype(bf16)
    apart = jnp.concatenate(
        [
            jnp.concatenate([heads[0:1], jnp.zeros((1, LANES), f32)], axis=1),
            jnp.concatenate([jnp.zeros((1, LANES), f32), heads[1:2]], axis=1),
            jnp.concatenate([empty, empty], axis=1),
        ],
        axis=0,
    ).astype(bf16)
    slope = s * (1.0 + tpre * (1.0 - s))
    dtpre = (t_dot(dlogit, apart) * jnp.concatenate([slope, slope], axis=1)).astype(bf16)
    dm_ref[...] = dot_t(dtpre, ti_ref[...]).astype(bf16)
    head_grad = dot(dlogit, act)
    side_ref[...] = jnp.zeros_like(side_ref)
    side_ref[0:1, 0:LANES] = head_grad[0:1]
    side_ref[0:1, LANES : 2 * LANES] = head_grad[1:2]
    side_ref[0:1, 2 * LANES : 3 * LANES] = jnp.broadcast_to(loss, (1, LANES))
    gti_ref[...] = t_dot(mixed, dtpre)

    def pack(above, below, cols):
        def put(side, place, rr, ff):
            dst = keep_ref if side == 0 else send_ref
            row = pl.ds(pl.multiple_of(rr * BLOCK + ff * 8, 8), 8)
            tile = jnp.concatenate([above(row), below(row)], axis=0)
            dst[rows16(place * BLOCK), cols] = tile.astype(dst.dtype)

        places.each(pairs, put)

    for k in range(part):
        g_ref[k] = t_dot(ga_ref[:, k * hidden : (k + 1) * hidden], dm_ref[...])
        g_ref[k + part] = t_dot(ga_ref[:, (k + part) * hidden : (k + part + 1) * hidden], dm_ref[...])
        pack(
            lambda row: g_ref[k, row, :],
            lambda row: g_ref[k + part, row, :],
            slice(k * out_cols, (k + 1) * out_cols),
        )
    at = part * out_cols
    pack(lambda row: gti_ref[row, 0:LANES], lambda row: gti_ref[row, LANES : 2 * LANES], slice(at, at + LANES))


def back_part(places, ks, w_ref, dm_ref, ga_ref, gs_ref, xt_ref, dp_ref, keep_ref, send_ref, g_ref):
    half = keep_ref.shape[0]
    tile = dm_ref.shape[0] // 2
    places.start()

    def weights(at):
        here = slice(at * half, (at + 1) * half)
        g_ref[:, here] = dot(xt_ref[...], dp_ref[:, here])
        back_pack(places, here, keep_ref, send_ref, g_ref)

    terms = []
    for at, k in enumerate(ks):
        cols, here = slice(k * half, (k + 1) * half), slice(at * half, (at + 1) * half)
        sums = []
        for i in range(2):
            rows = slice(i * tile, (i + 1) * tile)
            u = dot_t(dm_ref[rows, :], w_ref[cols, :])
            dp_ref[rows, here] = (u * gs_ref[rows, cols].astype(f32)).astype(bf16)
            sums.append(jnp.sum(u * ga_ref[rows, cols].astype(f32), axis=1, keepdims=True))
        terms.append(sums)
        if at:
            weights(at - 1)
    weights(len(ks) - 1)
    return terms


def back_pack(places, cols, keep_ref, send_ref, g_ref):
    half = keep_ref.shape[0]

    def put(side, place, rr, ff):
        dst = keep_ref if side == 0 else send_ref
        row = (ff ^ places.field) * half + rr * BLOCK
        dst[rows16(place * BLOCK), cols] = g_ref[rows16(row), cols].astype(dst.dtype)

    places.each(half // BLOCK, put)


def set_terms(q_ref, terms, ks):
    tile = q_ref.shape[0] // 2
    experts = q_ref.shape[1] // 2
    lane = lax.broadcasted_iota(jnp.int32, (tile, 2 * experts), 1)
    for i in range(2):
        rows = slice(i * tile, (i + 1) * tile)
        q = q_ref[rows, :]
        for k, sums in zip(ks, terms):
            q = jnp.where((lane == k) | (lane == k + experts), sums[i], q)
        q_ref[rows, :] = q


def back_first_kernel(
    places, ks, w_ref, dm_ref, ga_ref, gs_ref, xt_ref, dp_ref, keep_ref, send_ref, q_ref, g_ref
):
    terms = back_part(places, ks, w_ref, dm_ref, ga_ref, gs_ref, xt_ref, dp_ref, keep_ref, send_ref, g_ref)
    q_ref[...] = jnp.zeros_like(q_ref)
    set_terms(q_ref, terms, ks)


def back_last_kernel(
    places,
    ks,
    w_ref,
    dm_ref,
    ga_ref,
    gs_ref,
    xt_ref,
    before_ref,
    gate_ref,
    by_row_ref,
    dp_ref,
    keep_ref,
    send_ref,
    dg_ref,
    g_ref,
    q_ref,
):
    terms = back_part(places, ks, w_ref, dm_ref, ga_ref, gs_ref, xt_ref, dp_ref, keep_ref, send_ref, g_ref)
    q_ref[...] = before_ref[...]
    set_terms(q_ref, terms, ks)
    q = q_ref[...]
    experts = q.shape[1] // 2
    lane = lax.broadcasted_iota(jnp.int32, q.shape, 1)
    total = 0.5 * jnp.sum(q, axis=1, keepdims=True)
    mine = (lane // experts).astype(f32) == by_row_ref[:, 2:3]
    dg_ref[...] = jnp.zeros_like(dg_ref)
    dg_ref[:, 0 : 2 * experts] = jnp.where(mine, q - gate_ref[...] * total, 0.0).astype(bf16)
    cols = slice(dp_ref.shape[1], dp_ref.shape[1] + LANES)
    g_ref[:, cols] = dot(xt_ref[...], dg_ref[...])
    back_pack(places, cols, keep_ref, send_ref, g_ref)


def input_kernel(at, low_ref, high_ref, dg_ref, w_ref, *refs):
    keep_ref, send_ref = refs[-2:]
    part = low_ref.shape[1]
    wide = part + high_ref.shape[1]
    grad = dot_t(low_ref[...], w_ref[:, 0:part]) + dot_t(high_ref[...], w_ref[:, part:wide])
    grad = grad + dot_t(dg_ref[...], w_ref[:, wide:])
    half = grad.shape[1] // 2
    keep_ref[0] = grad[:, :half]
    send_ref[...] = grad[:, half:].astype(bf16)


def place_kernel(at, early_ref, late_ref, held_ref, out_ref):
    tile = out_ref.shape[1]
    half = pl.num_programs(0) // 2
    m = pl.program_id(0)

    @pl.when(m < half)
    def _():
        out_ref[0] = early_ref[pl.ds(pl.multiple_of(m * tile, tile), tile), :].astype(f32)

    @pl.when(m >= half)
    def _():
        out_ref[0] = late_ref[pl.ds(pl.multiple_of((m - half) * tile, tile), tile), :].astype(f32)


def update_kernel(rates, sum_a, got_a, sum_b, got_b, side, *refs):
    weights, velocities, averages, outs = refs[0:5], refs[5:10], refs[10:15], refs[15:30]
    wide, gates = weights[0].shape[1], weights[1].shape[1]
    experts, rows, out_cols = weights[2].shape
    tasks = weights[3].shape[0]
    part = experts // 2

    def renew(at, place, gradient):
        velocity = momentum_mu * velocities[at][place] + gradient
        weight = weights[at][place] - rates[at] * (gradient + momentum_mu * velocity)
        outs[3 * at][place] = weight
        outs[3 * at + 1][place] = velocity
        outs[3 * at + 2][place] = average_keep * averages[at][place] + (1.0 - average_keep) * weight

    first = sum_a[0 : got_a.shape[0], :] + got_a[...].astype(f32)
    renew(0, (slice(None), slice(None)), first[:, :wide])
    renew(1, (slice(None), slice(None)), first[:, wide : wide + gates])
    count = got_b.shape[0] - 8
    second = sum_b[0:count, :] + got_b[0:count, :].astype(f32)
    for k in range(experts):
        top = (k // part) * rows
        renew(2, k, second[top : top + rows, (k % part) * out_cols : (k % part + 1) * out_cols])
    for t in range(tasks):
        renew(3, t, second[t * rows : (t + 1) * rows, part * out_cols :])
        renew(4, (slice(t, t + 1), slice(None)), side[0:1, t * LANES : (t + 1) * LANES])


class Cube:
    def __init__(self):
        self.rows = lax.axis_size("rows")
        self.fields = lax.axis_size("field")
        bits = int(math.log2(self.rows))
        assert 1 << bits == self.rows and self.fields == 2
        outer = [("row", b) for b in range(bits - 1, 1, -1)]
        self.order = outer + [("mixed", 0), ("mixed", 1)]
        self.other_order = outer + [("mixed", 1), ("mixed", 0)]
        self.core = ("row", 0)

    def pairs(self, step):
        kind, which = step
        pairs = []
        for r in range(self.rows):
            for f in range(self.fields):
                if kind == "row":
                    to = (r ^ (1 << which), f)
                else:
                    to = (r ^ 2, f) if (r & 1) == which else (r, f ^ 1)
                pairs.append((r * self.fields + f, to[0] * self.fields + to[1]))
        return pairs

    def swap(self, values, step):
        return lax.ppermute(values, both, self.pairs(step))

    def place(self, order, rr, ff, r, f):
        dr, df, core = rr ^ r, ff ^ f, r & 1
        out = jnp.zeros_like(dr + df)
        for s, (kind, which) in enumerate(order):
            if kind == "row":
                bit = (dr >> which) & 1
            else:
                bit = jnp.where(core == which, (dr >> 1) & 1, df)
            out = out + (bit << s)
        return out


def gather_two(cube, block_a, make_b, make_x):
    got_a = cube.swap(block_a, cube.order[0])
    x = make_x(block_a)
    block_a = jnp.concatenate([block_a, got_a], axis=0)
    block_b = make_b(block_a)
    for at in range(1, len(cube.order)):
        got_a = cube.swap(block_a, cube.order[at])
        got_b = cube.swap(block_b, cube.order[at - 1])
        if at + 1 == len(cube.order):
            got_a = after(got_a, x[0])
        block_a = jnp.concatenate([block_a, after(got_a, got_b)], axis=0)
        block_b = jnp.concatenate([block_b, after(got_b, block_a)], axis=0)
    oth_a = cube.swap(block_a, cube.core)
    return block_a, oth_a, block_b, cube.swap(block_b, cube.order[-1]), x


def after(values, *earlier):
    return lax.optimization_barrier((values,) + earlier)[0]


def fold(total, got):
    rows = got.shape[0]
    total = total[:rows] + got.astype(f32)
    half = rows // 2
    return total, total[half:].astype(bf16)


def split_two(values):
    high = lax.reduce_precision(values, 8, 7)
    low = lax.reduce_precision(values - high, 8, 7)
    return jnp.concatenate([high, low], axis=0).astype(bf16)


def join_two(rows):
    rows = rows.astype(f32)
    half = rows.shape[0] // 2
    return rows[:half] + rows[half:]


def beside(part, side):
    mine = split_two(side)
    return jnp.concatenate([part, mine], axis=0), join_two(mine)


def fold_beside(total, side, got):
    rows = got.shape[0] - 8
    total, part = fold(total, got[:rows])
    message, side = beside(part, side + join_two(got[rows:]))
    return total, message, side


def shape(dims, dtype):
    return jax.ShapeDtypeStruct(dims, dtype)


def params(limit):
    return pltpu.CompilerParams(vmem_limit_bytes=limit << 20)


vmem = pl.BlockSpec()


def cost(flops):
    return pl.CostEstimate(flops=flops, bytes_accessed=8 << 20, transcendentals=0)


def on_device(
    inputs,
    valid_mask,
    labels,
    domains,
    expert_in,
    gate_in,
    expert_out,
    tower_in,
    tower_out,
    velocity_expert_in,
    velocity_gate_in,
    velocity_expert_out,
    velocity_tower_in,
    velocity_tower_out,
    average_expert_in,
    average_gate_in,
    average_expert_out,
    average_tower_in,
    average_tower_out,
):
    cube = Cube()
    micro, rows_dev, width = inputs.shape
    fields = cube.fields
    tile = rows_dev // fields
    rows_own = micro * tile
    experts, second_rows, out_cols = expert_out.shape
    tasks, tower_cols = tower_out.shape
    wide = expert_in.shape[1]
    hidden = wide // experts
    first_rows = expert_in.shape[0]
    part = experts // 2
    total_rows = micro * rows_dev * cube.rows
    r, f = lax.axis_index("rows"), lax.axis_index("field")

    def swap_field(values):
        return lax.ppermute(values, "field", [(0, 1), (1, 0)])

    def own_half(values, which):
        return lax.dynamic_slice_in_dim(values, which * tile, tile, 1)

    block_a = pl.pallas_call(
        pack_a_kernel,
        out_shape=shape((first_rows, wide + LANES), bf16),
        compiler_params=params(4),
        name="pack_a",
    )(expert_in, gate_in)

    def make_b(earlier):
        return pl.pallas_call(
            pack_b_kernel,
            out_shape=shape((2 * second_rows, part * out_cols + 2 * LANES), bf16),
            compiler_params=params(4),
            name="pack_b",
        )(expert_out, tower_in, after(valid_mask, earlier))


    def send_x(earlier):
        return swap_field(own_half(after(inputs, earlier), 1 - f).reshape(rows_own, width))


    pairs = width // BLOCK
    fit = first_rows == BLOCK
    places = Places(fit, cube.order)
    sent = bf16 if fit else f32

    a_cols, b_cols = wide + LANES, part * out_cols + LANES
    heads = tasks * tower_cols

    def make_x(earlier):
        x_got = send_x(earlier)
        return pl.pallas_call(
            rows_kernel,
            out_shape=[
                shape((rows_own, 2 * width), bf16),
                shape((2 * width, rows_own), bf16),
                shape((8, rows_own), f32),
                shape((rows_own, 8), f32),
            ],
            compiler_params=params(8),
            cost_estimate=cost(1 << 20),
            name="rows",
        )(inputs, x_got, valid_mask, labels, domains)

    own_a, oth_a, own_b, got_b, (x, x_t, flags, by_row) = gather_two(cube, block_a, make_b, make_x)
    if not fit:
        rows_a = first_sorted(cube, cube.order, r, f, width, first_rows)
        own_a, oth_a = jnp.split(jnp.take(jnp.concatenate([own_a, oth_a]), rows_a, axis=0), 2)
    ga, gs, gate, first_w = pl.pallas_call(
        functools.partial(first_kernel, places),
        out_shape=[
            shape((rows_own, wide), bf16),
            shape((rows_own, wide), bf16),
            shape((rows_own, tasks * experts), f32),
            shape((2 * width, a_cols), bf16),
        ],
        compiler_params=params(12),
        cost_estimate=cost(4 * rows_own * 2 * width * a_cols),
        name="first",
    )(own_a, oth_a, x, x_t, flags)

    own_b = jnp.concatenate([own_b, after(got_b, gate)], axis=0)
    oth_b = cube.swap(own_b, cube.core)
    if not fit:
        rows_b = second_sorted(cube, cube.order, r, f, width, second_rows)
        own_b, oth_b = jnp.split(jnp.take(jnp.concatenate([own_b, oth_b]), rows_b, axis=0), 2)
    second_w, dmixed, side, keep_b, send_b = pl.pallas_call(
        functools.partial(second_kernel, places),
        out_shape=[
            shape((wide, out_cols), bf16),
            shape((rows_own, out_cols), bf16),
            shape((8, b_cols), f32),
            shape((width, b_cols), f32),
            shape((width, b_cols), sent),
        ],
        scratch_shapes=[
            pltpu.VMEM((out_cols, heads), bf16),
            pltpu.VMEM((rows_own, out_cols), bf16),
            pltpu.VMEM((experts, hidden, out_cols), f32),
            pltpu.VMEM((out_cols, heads), f32),
        ],
        compiler_params=params(20),
        name="second",
    )(own_b, oth_b, ga, flags, by_row, tower_out)
    if not fit:
        keep_b, send_b = unsorted(keep_b, send_b, rows_b)
    message, side = beside(send_b, side[:4])
    steps = [cube.core] + cube.order[::-1]
    got_b = cube.swap(message, steps[0])

    cut = 7
    low_cols, high_cols = cut * hidden, (experts - cut) * hidden + LANES
    dpre_low, keep_low, send_low, terms = pl.pallas_call(
        functools.partial(back_first_kernel, places, range(cut)),
        out_shape=[
            shape((rows_own, low_cols), bf16),
            shape((width, low_cols), f32),
            shape((width, low_cols), sent),
            shape((rows_own, tasks * experts), f32),
        ],
        scratch_shapes=[pltpu.VMEM((2 * width, low_cols), f32)],
        compiler_params=params(16),
        name="back_first",
    )(after(second_w, message), dmixed, ga, gs, x_t)
    if not fit:
        keep_low, send_low = unsorted(keep_low, send_low, rows_a)
    got_low = cube.swap(send_low, steps[0])
    sum_b, message, side = fold_beside(keep_b, side, after(got_b, send_low))
    got_b = cube.swap(message, steps[1])
    dpre_high, keep_high, send_high, dgate = pl.pallas_call(
        functools.partial(back_last_kernel, places, range(cut, experts)),
        out_shape=[
            shape((rows_own, high_cols - LANES), bf16),
            shape((width, high_cols), f32),
            shape((width, high_cols), sent),
            shape((rows_own, LANES), bf16),
        ],
        scratch_shapes=[
            pltpu.VMEM((2 * width, high_cols), f32),
            pltpu.VMEM((rows_own, tasks * experts), f32),
        ],
        compiler_params=params(16),
        name="back_last",
    )(second_w, dmixed, ga, gs, x_t, after(terms, message), gate, by_row)
    if not fit:
        keep_high, send_high = unsorted(keep_high, send_high, rows_a)
    got_high = cube.swap(send_high, steps[0])
    sum_low, next_low = fold(keep_low, after(got_low, send_high))
    got_low = cube.swap(next_low, steps[1])
    sum_high, next_a = fold(keep_high, after(got_high, next_low))
    got_high = cube.swap(next_a, steps[1])
    def input_part(first, held, gates):
        half = micro // 2
        return pl.pallas_call(
            input_kernel,
            grid_spec=pltpu.PrefetchScalarGridSpec(
                num_scalar_prefetch=1,
                grid=(half,),
                in_specs=[
                    pl.BlockSpec((tile, low_cols), lambda i, at: (i + first, 0)),
                    pl.BlockSpec((tile, high_cols - LANES), lambda i, at: (i + first, 0)),
                    pl.BlockSpec((tile, LANES), lambda i, at: (i + first, 0)),
                    pl.BlockSpec((2 * width, a_cols), lambda i, at: (0, 0)),
                ]
                + [pl.BlockSpec(memory_space=pl.ANY)] * len(held),
                out_specs=[
                    pl.BlockSpec((1, tile, width), lambda i, at: (i + first, at[0], 0)),
                    pl.BlockSpec((tile, width), lambda i, at: (i, 0)),
                ],
            ),
            out_shape=[
                shape((micro, rows_dev, width), f32),
                shape((half * tile, width), bf16),
            ],
            input_output_aliases={5: 0} if held else {},
            compiler_params=params(12),
            name="input",
        )(f.astype(jnp.int32).reshape(1), dpre_low, dpre_high, gates, first_w, *held)

    grad_keep, grad_send = input_part(0, (), after(dgate, next_a))
    grad_got = []
    got_a = jnp.concatenate([got_low, got_high], axis=1)
    sum_a = jnp.concatenate([sum_low, sum_high], axis=1)
    for at in range(1, len(steps)):
        if at > 1:
            got_a = cube.swap(next_a, steps[at])
        if at + 1 < len(steps):
            sum_b, message, side = fold_beside(sum_b, side, after(got_b, next_a))
            got_b = cube.swap(message, steps[at + 1])
            if at == 1:
                early = grad_send
                grad_keep, grad_send = input_part(micro // 2, (grad_keep,), after(dgate, message))
            elif at <= 3:
                grad_got.append(swap_field(after(early if at == 2 else grad_send, message)))
            sum_a, next_a = fold(sum_a, after(got_a, got_b, grad_send))
    side = side + join_two(got_b[got_b.shape[0] - 8 :])
    weights = (expert_in, gate_in, expert_out, tower_in, tower_out)
    velocities = (
        velocity_expert_in,
        velocity_gate_in,
        velocity_expert_out,
        velocity_tower_in,
        velocity_tower_out,
    )
    averages = (
        average_expert_in,
        average_gate_in,
        average_expert_out,
        average_tower_in,
        average_tower_out,
    )
    rates = [base * math.sqrt(total_rows) for base in rate_bases]
    input_grad = pl.pallas_call(
        place_kernel,
        grid_spec=pltpu.PrefetchScalarGridSpec(
            num_scalar_prefetch=1,
            grid=(micro,),
            in_specs=[pl.BlockSpec((rows_own // 2, width), lambda i, at: (0, 0))] * 2
            + [pl.BlockSpec(memory_space=pl.ANY)],
            out_specs=pl.BlockSpec((1, tile, width), lambda i, at: (i, 1 - at[0], 0)),
        ),
        out_shape=shape((micro, rows_dev, width), f32),
        input_output_aliases={3: 0},
        compiler_params=params(8),
        name="place",
    )(f.astype(jnp.int32).reshape(1), *grad_got, after(grad_keep, next_a))
    updated = pl.pallas_call(
        functools.partial(update_kernel, rates),
        out_shape=[shape(w.shape, f32) for w in weights for _ in range(3)],
        compiler_params=params(8),
        name="update",
    )(sum_a, after(got_a, input_grad), sum_b, got_b, side, *weights, *velocities, *averages)
    return (side[0, heads], input_grad, *updated)


def owner_rows(cube, order, r, f, rr, ff, inner, size):
    held = cube.rows * cube.fields // 2
    same = (rr & 1) == (r & 1)
    here = cube.place(order, rr, ff, r, f)
    there = cube.place(order, rr, ff, r ^ 1, f)
    return (jnp.where(same, here, held + there) * size + inner).reshape(-1)


def block_grid(width):
    side = np.arange(2)[:, None, None, None]
    j = np.arange(width // (2 * BLOCK))[None, :, None, None]
    ff = np.arange(2)[None, None, :, None]
    inner = np.arange(BLOCK)[None, None, None, :]
    ahead = (2 * j + side) * BLOCK + 0 * ff + 0 * inner
    full = np.zeros(ahead.shape, np.int32)
    return ahead.astype(np.int32), full + ff.astype(np.int32), full + inner.astype(np.int32)


def first_sorted(cube, order, r, f, width, size):
    ahead, ff, inner = block_grid(width)
    at = ahead + inner
    return owner_rows(
        cube, order, r, f, jnp.asarray(at // size), jnp.asarray(ff), jnp.asarray(at % size), size
    )


def second_sorted(cube, order, r, f, width, size):
    ahead, ff, inner = block_grid(width)
    at = ahead + ff * 8 + inner % 8
    owner = at // size
    held = at % size + size * (inner // 8)
    return owner_rows(
        cube, order, r, f, jnp.asarray(owner // 2), jnp.asarray(owner % 2), jnp.asarray(held), 2 * size
    )


def unsorted(keep, send, rows):
    every = jnp.concatenate([keep, send])
    back = jnp.zeros_like(rows).at[rows].set(jnp.arange(rows.shape[0], dtype=rows.dtype))
    keep, send = jnp.split(jnp.take(every, back, axis=0), 2)
    return keep, send.astype(bf16)


def solution(mesh):
    first = P(("field", "rows"), None)
    second = P(None, ("rows", "field"), None)
    by_row = P(None, "rows")
    inputs = P(None, "rows", "field")
    weights = (first, first, second, second, P())
    return jax.shard_map(
        on_device,
        mesh=mesh,
        in_specs=(inputs, by_row, by_row, by_row) + weights * 3,
        out_specs=(P(), inputs) + tuple(spec for spec in weights for _ in range(3)),
        check_vma=False,
    )
```

```python
import functools
import math

import jax
import jax.numpy as jnp
import numpy as np
from jax import lax
from jax.experimental import pallas as pl
from jax.experimental.pallas import tpu as pltpu
from jax.sharding import PartitionSpec as P

momentum_mu = 0.5
average_keep = 0.5
rate_bases = (17.0, 1.0, 24.0, 4.0, 0.25)
both = ("rows", "field")
f32 = jnp.float32
bf16 = jnp.bfloat16
BLOCK = 16
LANES = 128


def dot(a, b):
    return lax.dot_general(a, b, (((1,), (0,)), ((), ())), preferred_element_type=f32)


def dot_t(a, b):
    return lax.dot_general(a, b, (((1,), (1,)), ((), ())), preferred_element_type=f32)


def t_dot(a, b):
    return lax.dot_general(a, b, (((0,), (0,)), ((), ())), preferred_element_type=f32)


def sigmoid(v):
    return 0.5 + 0.5 * jnp.tanh(0.5 * v)


def rows16(start):
    return pl.ds(pl.multiple_of(start, BLOCK), BLOCK)


class Places:
    def __init__(self, fit, order):
        self.fit, self.order = fit, order

    def bits(self, core, rr, ff):
        out = 0
        for s, (kind, which) in enumerate(self.order):
            if kind == "row":
                bit = (rr >> which) & 1
            else:
                bit = (rr >> 1) & 1 if core == which else ff
            out = out | (bit << s)
        return out

    def start(self):
        r, self.field = lax.axis_index("rows"), lax.axis_index("field")
        self.core = r & 1 if self.fit else jnp.int32(0)
        self.bases = [self.bits(core, r, self.field) for core in range(2)]

    def block(self, side, j):
        core = self.core if side == 0 else 1 - self.core
        pair, ff = j // 2, j % 2
        if not self.fit:
            return j, 2 * pair + side, ff
        ways = [base ^ self.bits(c, 2 * pair, ff) for c, base in enumerate(self.bases)]
        return jnp.where(core == 0, ways[0], ways[1]), 2 * pair + core, ff

    def each(self, pairs, body):
        for j in range(pairs):
            for side in range(2):
                body(side, *self.block(side, j))


def pack_a_kernel(expert_ref, gate_ref, out_ref):
    wide, gates = expert_ref.shape[1], gate_ref.shape[1]
    out_ref[:, 0:wide] = expert_ref[...].astype(bf16)
    out_ref[:, wide:] = jnp.zeros((out_ref.shape[0], LANES), bf16)
    out_ref[:, wide : wide + gates] = gate_ref[...].astype(bf16)


def pack_b_kernel(expert_ref, tower_ref, valid_ref, out_ref):
    experts, rows, out_cols = expert_ref.shape
    part = experts // 2
    for k in range(part):
        both_k = jnp.concatenate([expert_ref[k], expert_ref[k + part]], axis=0)
        out_ref[:, k * out_cols : (k + 1) * out_cols] = both_k.astype(bf16)
    at = part * out_cols
    towers = jnp.concatenate([tower_ref[0], tower_ref[1]], axis=0)
    out_ref[:, at : at + LANES] = towers.astype(bf16)
    tile = valid_ref.shape[1] // 2
    own = valid_ref[:, pl.ds(pl.multiple_of(lax.axis_index("field") * tile, tile), tile)].astype(f32)
    ones = jnp.sum(jnp.sum(own, axis=1, keepdims=True), axis=0, keepdims=True).astype(jnp.int32)
    ones = jnp.broadcast_to(ones, (2 * rows, LANES))
    row, lane = (lax.broadcasted_iota(jnp.int32, ones.shape, d) for d in range(2))
    digits = jnp.where(lane == 2, ones >> 16, jnp.where(lane == 1, ones >> 8, ones) & 255)
    digits = jnp.where((row == 0) & (lane < 3), digits, 0).astype(f32)
    out_ref[:, at + LANES :] = digits.astype(bf16)


def rows_kernel(in_ref, got_ref, valid_ref, label_ref, domain_ref, x_ref, xt_ref, flags_ref, by_row_ref):
    micro, rows_dev, width = in_ref.shape
    tile = rows_dev // 2
    start = pl.multiple_of(lax.axis_index("field") * tile, tile)
    for m in range(micro):
        rows = slice(m * tile, (m + 1) * tile)
        x = jnp.concatenate([in_ref[m, pl.ds(start, tile), :], got_ref[rows, :]], axis=1)
        x_ref[rows, :] = x
        xt_ref[:, rows] = x.T
        kinds = [ref[m : m + 1, pl.ds(start, tile)].astype(f32) for ref in (valid_ref, label_ref, domain_ref)]
        flags = jnp.concatenate(kinds + [jnp.zeros((5, tile), f32)], axis=0)
        flags_ref[:, rows] = flags
        by_row_ref[rows, :] = flags.T


def first_kernel(places, own_ref, oth_ref, x_ref, xt_ref, flags_ref, ga_ref, gs_ref, gate_ref, w_ref):
    half = own_ref.shape[0]
    count, wide = ga_ref.shape
    experts = wide // half
    tile = count // 4
    places.start()

    def put(side, place, rr, ff):
        src = own_ref if side == 0 else oth_ref
        row = (ff ^ places.field) * half + rr * BLOCK
        w_ref[rows16(row), :] = src[rows16(place * BLOCK), :]

    places.each(half // BLOCK, put)
    logits = dot(w_ref[:, wide:].T, xt_ref[...])
    logits = jnp.where(flags_ref[2:3, :] == 0.0, logits[0:experts], logits[experts : 2 * experts])
    raised = jnp.exp(logits - jnp.max(logits, axis=0, keepdims=True))
    gate = raised / jnp.sum(raised, axis=0, keepdims=True)
    gate_ref[...] = jnp.concatenate([gate, gate], axis=0).T

    for i in range(4):
        rows = slice(i * tile, (i + 1) * tile)
        x = x_ref[rows, :]
        gate = 0.5 * gate_ref[rows, :]
        for k in range(experts):
            cols = slice(k * half, (k + 1) * half)
            pre = dot(x, w_ref[:, cols])
            low = 0.5 * pre
            up = 1.0 + jnp.tanh(low)
            scaled = gate[:, k : k + 1] * up
            ga_ref[rows, cols] = (scaled * pre).astype(bf16)
            gs_ref[rows, cols] = (scaled * (1.0 + pre - low * up)).astype(bf16)


def second_kernel(
    places,
    own_ref,
    oth_ref,
    ga_ref,
    flags_ref,
    by_row_ref,
    to_ref,
    w_ref,
    dm_ref,
    side_ref,
    keep_ref,
    send_ref,
    ti_ref,
    mix_ref,
    g_ref,
    gti_ref,
):
    half = own_ref.shape[0]
    pairs = half // BLOCK
    count, out_cols = dm_ref.shape
    hidden = half
    wide = ga_ref.shape[1]
    experts = wide // hidden
    part = experts // 2

    places.start()

    digits = jnp.zeros((BLOCK, LANES), f32)
    for side in range(2):
        for j in range(pairs // 2):
            src = own_ref if side == 0 else oth_ref
            (place0, rr, _), (place1, _, _) = places.block(side, 2 * j), places.block(side, 2 * j + 1)
            a0 = src[rows16(place0 * BLOCK), :].astype(f32)
            a1 = src[rows16(place1 * BLOCK), :].astype(f32)
            row = rr * BLOCK
            upper = jnp.concatenate([a0[:8], a1[:8]], axis=0).astype(bf16)
            lower = jnp.concatenate([a0[8:], a1[8:]], axis=0).astype(bf16)
            at = part * out_cols
            for k in range(part):
                cols = slice(k * out_cols, (k + 1) * out_cols)
                w_ref[rows16(k * hidden + row), :] = upper[:, cols]
                w_ref[rows16((k + part) * hidden + row), :] = lower[:, cols]
            ti_ref[rows16(row), 0:LANES] = upper[:, at : at + LANES]
            ti_ref[rows16(row), LANES : 2 * LANES] = lower[:, at : at + LANES]
            digits = digits + (a0 + a1)[:, at + LANES :]
    lane = lax.broadcasted_iota(jnp.int32, digits.shape, 1)
    scale = jnp.where(lane == 0, 1.0, jnp.where(lane == 1, 256.0, jnp.where(lane == 2, 65536.0, 0.0)))
    real = jnp.sum(jnp.sum(digits * scale, axis=1, keepdims=True), axis=0, keepdims=True)

    domain = by_row_ref[:, 2:3]
    heads = to_ref[...].astype(bf16).astype(f32)
    empty = jnp.zeros((6, LANES), f32)
    tile = count // 4
    for i in range(4):
        rows = slice(i * tile, (i + 1) * tile)
        mix_ref[rows, :] = dot(ga_ref[rows, :], w_ref[...]).astype(bf16)
    mixed = mix_ref[...]
    tpre = dot(mixed, ti_ref[...])
    tpre = jnp.where(domain == 0.0, tpre[:, :LANES], tpre[:, LANES:])
    s = sigmoid(tpre)
    act = (tpre * s).astype(bf16)
    logits = dot_t(jnp.concatenate([heads, empty], axis=0).astype(bf16), act)
    valid, label, first = flags_ref[0:1, :], flags_ref[1:2, :], flags_ref[2:3, :] == 0.0
    chosen = jnp.where(first, logits[0:1, :], logits[1:2, :])
    soft = jnp.maximum(chosen, 0.0) + jnp.log1p(jnp.exp(-jnp.abs(chosen)))
    loss = jnp.sum(valid * (soft - label * chosen), axis=1, keepdims=True) / real
    dlogit = valid * (sigmoid(chosen) - label) / real
    dlogit = jnp.concatenate(
        [jnp.where(first, dlogit, 0.0), jnp.where(first, 0.0, dlogit), jnp.zeros((6, count), f32)], axis=0
    ).astype(bf16)
    apart = jnp.concatenate(
        [
            jnp.concatenate([heads[0:1], jnp.zeros((1, LANES), f32)], axis=1),
            jnp.concatenate([jnp.zeros((1, LANES), f32), heads[1:2]], axis=1),
            jnp.concatenate([empty, empty], axis=1),
        ],
        axis=0,
    ).astype(bf16)
    slope = s * (1.0 + tpre * (1.0 - s))
    dtpre = (t_dot(dlogit, apart) * jnp.concatenate([slope, slope], axis=1)).astype(bf16)
    dm_ref[...] = dot_t(dtpre, ti_ref[...]).astype(bf16)
    head_grad = dot(dlogit, act)
    side_ref[...] = jnp.zeros_like(side_ref)
    side_ref[0:1, 0:LANES] = head_grad[0:1]
    side_ref[0:1, LANES : 2 * LANES] = head_grad[1:2]
    side_ref[0:1, 2 * LANES : 3 * LANES] = jnp.broadcast_to(loss, (1, LANES))
    gti_ref[...] = t_dot(mixed, dtpre)

    def pack(above, below, cols):
        def put(side, place, rr, ff):
            dst = keep_ref if side == 0 else send_ref
            row = pl.ds(pl.multiple_of(rr * BLOCK + ff * 8, 8), 8)
            tile = jnp.concatenate([above(row), below(row)], axis=0)
            dst[rows16(place * BLOCK), cols] = tile.astype(dst.dtype)

        places.each(pairs, put)

    for k in range(part):
        g_ref[k] = t_dot(ga_ref[:, k * hidden : (k + 1) * hidden], dm_ref[...])
        g_ref[k + part] = t_dot(ga_ref[:, (k + part) * hidden : (k + part + 1) * hidden], dm_ref[...])
        pack(
            lambda row: g_ref[k, row, :],
            lambda row: g_ref[k + part, row, :],
            slice(k * out_cols, (k + 1) * out_cols),
        )
    at = part * out_cols
    pack(lambda row: gti_ref[row, 0:LANES], lambda row: gti_ref[row, LANES : 2 * LANES], slice(at, at + LANES))


def back_part(places, ks, w_ref, dm_ref, ga_ref, gs_ref, xt_ref, dp_ref, keep_ref, send_ref, g_ref):
    half = keep_ref.shape[0]
    tile = dm_ref.shape[0] // 2
    places.start()

    def weights(at):
        here = slice(at * half, (at + 1) * half)
        g_ref[:, here] = dot(xt_ref[...], dp_ref[:, here])
        back_pack(places, here, keep_ref, send_ref, g_ref)

    terms = []
    for at, k in enumerate(ks):
        cols, here = slice(k * half, (k + 1) * half), slice(at * half, (at + 1) * half)
        sums = []
        for i in range(2):
            rows = slice(i * tile, (i + 1) * tile)
            u = dot_t(dm_ref[rows, :], w_ref[cols, :])
            dp_ref[rows, here] = (u * gs_ref[rows, cols].astype(f32)).astype(bf16)
            sums.append(jnp.sum(u * ga_ref[rows, cols].astype(f32), axis=1, keepdims=True))
        terms.append(sums)
        if at:
            weights(at - 1)
    weights(len(ks) - 1)
    return terms


def back_pack(places, cols, keep_ref, send_ref, g_ref):
    half = keep_ref.shape[0]

    def put(side, place, rr, ff):
        dst = keep_ref if side == 0 else send_ref
        row = (ff ^ places.field) * half + rr * BLOCK
        dst[rows16(place * BLOCK), cols] = g_ref[rows16(row), cols].astype(dst.dtype)

    places.each(half // BLOCK, put)


def set_terms(q_ref, terms, ks):
    tile = q_ref.shape[0] // 2
    experts = q_ref.shape[1] // 2
    lane = lax.broadcasted_iota(jnp.int32, (tile, 2 * experts), 1)
    for i in range(2):
        rows = slice(i * tile, (i + 1) * tile)
        q = q_ref[rows, :]
        for k, sums in zip(ks, terms):
            q = jnp.where((lane == k) | (lane == k + experts), sums[i], q)
        q_ref[rows, :] = q


def back_first_kernel(
    places, ks, w_ref, dm_ref, ga_ref, gs_ref, xt_ref, dp_ref, keep_ref, send_ref, q_ref, g_ref
):
    terms = back_part(places, ks, w_ref, dm_ref, ga_ref, gs_ref, xt_ref, dp_ref, keep_ref, send_ref, g_ref)
    q_ref[...] = jnp.zeros_like(q_ref)
    set_terms(q_ref, terms, ks)


def back_last_kernel(
    places,
    ks,
    w_ref,
    dm_ref,
    ga_ref,
    gs_ref,
    xt_ref,
    before_ref,
    gate_ref,
    by_row_ref,
    dp_ref,
    keep_ref,
    send_ref,
    dg_ref,
    g_ref,
    q_ref,
):
    terms = back_part(places, ks, w_ref, dm_ref, ga_ref, gs_ref, xt_ref, dp_ref, keep_ref, send_ref, g_ref)
    q_ref[...] = before_ref[...]
    set_terms(q_ref, terms, ks)
    q = q_ref[...]
    experts = q.shape[1] // 2
    lane = lax.broadcasted_iota(jnp.int32, q.shape, 1)
    total = 0.5 * jnp.sum(q, axis=1, keepdims=True)
    mine = (lane // experts).astype(f32) == by_row_ref[:, 2:3]
    dg_ref[...] = jnp.zeros_like(dg_ref)
    dg_ref[:, 0 : 2 * experts] = jnp.where(mine, q - gate_ref[...] * total, 0.0).astype(bf16)
    cols = slice(dp_ref.shape[1], dp_ref.shape[1] + LANES)
    g_ref[:, cols] = dot(xt_ref[...], dg_ref[...])
    back_pack(places, cols, keep_ref, send_ref, g_ref)


def input_kernel(at, low_ref, high_ref, dg_ref, w_ref, *refs):
    keep_ref, send_ref = refs[-2:]
    part = low_ref.shape[1]
    wide = part + high_ref.shape[1]
    grad = dot_t(low_ref[...], w_ref[:, 0:part]) + dot_t(high_ref[...], w_ref[:, part:wide])
    grad = grad + dot_t(dg_ref[...], w_ref[:, wide:])
    half = grad.shape[1] // 2
    keep_ref[0] = grad[:, :half]
    send_ref[...] = grad[:, half:].astype(bf16)


def place_kernel(at, early_ref, late_ref, held_ref, out_ref):
    tile = out_ref.shape[1]
    half = pl.num_programs(0) // 2
    m = pl.program_id(0)

    @pl.when(m < half)
    def _():
        out_ref[0] = early_ref[pl.ds(pl.multiple_of(m * tile, tile), tile), :].astype(f32)

    @pl.when(m >= half)
    def _():
        out_ref[0] = late_ref[pl.ds(pl.multiple_of((m - half) * tile, tile), tile), :].astype(f32)


def update_kernel(rates, sum_a, got_a, sum_b, got_b, side, *refs):
    weights, velocities, averages, outs = refs[0:5], refs[5:10], refs[10:15], refs[15:30]
    wide, gates = weights[0].shape[1], weights[1].shape[1]
    experts, rows, out_cols = weights[2].shape
    tasks = weights[3].shape[0]
    part = experts // 2

    def renew(at, place, gradient):
        velocity = momentum_mu * velocities[at][place] + gradient
        weight = weights[at][place] - rates[at] * (gradient + momentum_mu * velocity)
        outs[3 * at][place] = weight
        outs[3 * at + 1][place] = velocity
        outs[3 * at + 2][place] = average_keep * averages[at][place] + (1.0 - average_keep) * weight

    first = sum_a[0 : got_a.shape[0], :] + got_a[...].astype(f32)
    renew(0, (slice(None), slice(None)), first[:, :wide])
    renew(1, (slice(None), slice(None)), first[:, wide : wide + gates])
    count = got_b.shape[0] - 8
    second = sum_b[0:count, :] + got_b[0:count, :].astype(f32)
    for k in range(experts):
        top = (k // part) * rows
        renew(2, k, second[top : top + rows, (k % part) * out_cols : (k % part + 1) * out_cols])
    for t in range(tasks):
        renew(3, t, second[t * rows : (t + 1) * rows, part * out_cols :])
        renew(4, (slice(t, t + 1), slice(None)), side[0:1, t * LANES : (t + 1) * LANES])


class Cube:
    def __init__(self):
        self.rows = lax.axis_size("rows")
        self.fields = lax.axis_size("field")
        bits = int(math.log2(self.rows))
        assert 1 << bits == self.rows and self.fields == 2
        outer = [("row", b) for b in range(bits - 1, 1, -1)]
        self.order = outer + [("mixed", 0), ("mixed", 1)]
        self.other_order = outer + [("mixed", 1), ("mixed", 0)]
        self.core = ("row", 0)

    def pairs(self, step):
        kind, which = step
        pairs = []
        for r in range(self.rows):
            for f in range(self.fields):
                if kind == "row":
                    to = (r ^ (1 << which), f)
                else:
                    to = (r ^ 2, f) if (r & 1) == which else (r, f ^ 1)
                pairs.append((r * self.fields + f, to[0] * self.fields + to[1]))
        return pairs

    def swap(self, values, step):
        return lax.ppermute(values, both, self.pairs(step))

    def place(self, order, rr, ff, r, f):
        dr, df, core = rr ^ r, ff ^ f, r & 1
        out = jnp.zeros_like(dr + df)
        for s, (kind, which) in enumerate(order):
            if kind == "row":
                bit = (dr >> which) & 1
            else:
                bit = jnp.where(core == which, (dr >> 1) & 1, df)
            out = out + (bit << s)
        return out


def gather_two(cube, block_a, make_b, make_x):
    got_a = cube.swap(block_a, cube.order[0])
    x = make_x(block_a)
    block_a = jnp.concatenate([block_a, got_a], axis=0)
    block_b = make_b(block_a)
    for at in range(1, len(cube.order)):
        got_a = cube.swap(block_a, cube.order[at])
        got_b = cube.swap(block_b, cube.order[at - 1])
        if at + 1 == len(cube.order):
            got_a = after(got_a, x[0])
        block_a = jnp.concatenate([block_a, after(got_a, got_b if at > 1 else block_b)], axis=0)
        block_b = jnp.concatenate([block_b, after(got_b, block_a)], axis=0)
    oth_a = cube.swap(block_a, cube.core)
    return block_a, oth_a, block_b, cube.swap(block_b, cube.order[-1]), x


def after(values, *earlier):
    return lax.optimization_barrier((values,) + earlier)[0]


def fold(total, got):
    rows = got.shape[0]
    total = total[:rows] + got.astype(f32)
    half = rows // 2
    return total, total[half:].astype(bf16)


def split_two(values):
    high = lax.reduce_precision(values, 8, 7)
    low = lax.reduce_precision(values - high, 8, 7)
    return jnp.concatenate([high, low], axis=0).astype(bf16)


def join_two(rows):
    rows = rows.astype(f32)
    half = rows.shape[0] // 2
    return rows[:half] + rows[half:]


def beside(part, side):
    mine = split_two(side)
    return jnp.concatenate([part, mine], axis=0), join_two(mine)


def fold_beside(total, side, got):
    rows = got.shape[0] - 8
    total, part = fold(total, got[:rows])
    message, side = beside(part, side + join_two(got[rows:]))
    return total, message, side


def shape(dims, dtype):
    return jax.ShapeDtypeStruct(dims, dtype)


def params(limit):
    return pltpu.CompilerParams(vmem_limit_bytes=limit << 20)


vmem = pl.BlockSpec()


def cost(flops):
    return pl.CostEstimate(flops=flops, bytes_accessed=8 << 20, transcendentals=0)


def on_device(
    inputs,
    valid_mask,
    labels,
    domains,
    expert_in,
    gate_in,
    expert_out,
    tower_in,
    tower_out,
    velocity_expert_in,
    velocity_gate_in,
    velocity_expert_out,
    velocity_tower_in,
    velocity_tower_out,
    average_expert_in,
    average_gate_in,
    average_expert_out,
    average_tower_in,
    average_tower_out,
):
    cube = Cube()
    micro, rows_dev, width = inputs.shape
    fields = cube.fields
    tile = rows_dev // fields
    rows_own = micro * tile
    experts, second_rows, out_cols = expert_out.shape
    tasks, tower_cols = tower_out.shape
    wide = expert_in.shape[1]
    hidden = wide // experts
    first_rows = expert_in.shape[0]
    part = experts // 2
    total_rows = micro * rows_dev * cube.rows
    r, f = lax.axis_index("rows"), lax.axis_index("field")

    def swap_field(values):
        return lax.ppermute(values, "field", [(0, 1), (1, 0)])

    def own_half(values, which):
        return lax.dynamic_slice_in_dim(values, which * tile, tile, 1)

    block_a = pl.pallas_call(
        pack_a_kernel,
        out_shape=shape((first_rows, wide + LANES), bf16),
        compiler_params=params(4),
        name="pack_a",
    )(expert_in, gate_in)

    def make_b(earlier):
        return pl.pallas_call(
            pack_b_kernel,
            out_shape=shape((2 * second_rows, part * out_cols + 2 * LANES), bf16),
            compiler_params=params(4),
            name="pack_b",
        )(expert_out, tower_in, after(valid_mask, earlier))


    def send_x(earlier):
        return swap_field(own_half(after(inputs, earlier), 1 - f).reshape(rows_own, width))


    pairs = width // BLOCK
    fit = first_rows == BLOCK
    places = Places(fit, cube.order)
    sent = bf16 if fit else f32

    a_cols, b_cols = wide + LANES, part * out_cols + LANES
    heads = tasks * tower_cols

    def make_x(earlier):
        x_got = send_x(earlier)
        return pl.pallas_call(
            rows_kernel,
            out_shape=[
                shape((rows_own, 2 * width), bf16),
                shape((2 * width, rows_own), bf16),
                shape((8, rows_own), f32),
                shape((rows_own, 8), f32),
            ],
            compiler_params=params(8),
            cost_estimate=cost(1 << 20),
            name="rows",
        )(inputs, x_got, valid_mask, labels, domains)

    own_a, oth_a, own_b, got_b, (x, x_t, flags, by_row) = gather_two(cube, block_a, make_b, make_x)
    if not fit:
        rows_a = first_sorted(cube, cube.order, r, f, width, first_rows)
        own_a, oth_a = jnp.split(jnp.take(jnp.concatenate([own_a, oth_a]), rows_a, axis=0), 2)
    ga, gs, gate, first_w = pl.pallas_call(
        functools.partial(first_kernel, places),
        out_shape=[
            shape((rows_own, wide), bf16),
            shape((rows_own, wide), bf16),
            shape((rows_own, tasks * experts), f32),
            shape((2 * width, a_cols), bf16),
        ],
        compiler_params=params(12),
        cost_estimate=cost(4 * rows_own * 2 * width * a_cols),
        name="first",
    )(own_a, oth_a, x, x_t, flags)

    own_b = jnp.concatenate([own_b, after(got_b, gate)], axis=0)
    oth_b = cube.swap(own_b, cube.core)
    if not fit:
        rows_b = second_sorted(cube, cube.order, r, f, width, second_rows)
        own_b, oth_b = jnp.split(jnp.take(jnp.concatenate([own_b, oth_b]), rows_b, axis=0), 2)
    second_w, dmixed, side, keep_b, send_b = pl.pallas_call(
        functools.partial(second_kernel, places),
        out_shape=[
            shape((wide, out_cols), bf16),
            shape((rows_own, out_cols), bf16),
            shape((8, b_cols), f32),
            shape((width, b_cols), f32),
            shape((width, b_cols), sent),
        ],
        scratch_shapes=[
            pltpu.VMEM((out_cols, heads), bf16),
            pltpu.VMEM((rows_own, out_cols), bf16),
            pltpu.VMEM((experts, hidden, out_cols), f32),
            pltpu.VMEM((out_cols, heads), f32),
        ],
        compiler_params=params(20),
        name="second",
    )(own_b, oth_b, ga, flags, by_row, tower_out)
    if not fit:
        keep_b, send_b = unsorted(keep_b, send_b, rows_b)
    message, side = beside(send_b, side[:4])
    steps = [cube.core] + cube.order[::-1]
    got_b = cube.swap(message, steps[0])

    cut = 7
    low_cols, high_cols = cut * hidden, (experts - cut) * hidden + LANES
    dpre_low, keep_low, send_low, terms = pl.pallas_call(
        functools.partial(back_first_kernel, places, range(cut)),
        out_shape=[
            shape((rows_own, low_cols), bf16),
            shape((width, low_cols), f32),
            shape((width, low_cols), sent),
            shape((rows_own, tasks * experts), f32),
        ],
        scratch_shapes=[pltpu.VMEM((2 * width, low_cols), f32)],
        compiler_params=params(16),
        name="back_first",
    )(after(second_w, message), dmixed, ga, gs, x_t)
    if not fit:
        keep_low, send_low = unsorted(keep_low, send_low, rows_a)
    got_low = cube.swap(send_low, steps[0])
    sum_b, message, side = fold_beside(keep_b, side, after(got_b, send_low))
    got_b = cube.swap(message, steps[1])
    dpre_high, keep_high, send_high, dgate = pl.pallas_call(
        functools.partial(back_last_kernel, places, range(cut, experts)),
        out_shape=[
            shape((rows_own, high_cols - LANES), bf16),
            shape((width, high_cols), f32),
            shape((width, high_cols), sent),
            shape((rows_own, LANES), bf16),
        ],
        scratch_shapes=[
            pltpu.VMEM((2 * width, high_cols), f32),
            pltpu.VMEM((rows_own, tasks * experts), f32),
        ],
        compiler_params=params(16),
        name="back_last",
    )(second_w, dmixed, ga, gs, x_t, after(terms, message), gate, by_row)
    if not fit:
        keep_high, send_high = unsorted(keep_high, send_high, rows_a)
    got_high = cube.swap(send_high, steps[0])
    sum_low, next_low = fold(keep_low, after(got_low, send_high))
    got_low = cube.swap(next_low, steps[1])
    sum_high, next_a = fold(keep_high, after(got_high, next_low))
    got_high = cube.swap(next_a, steps[1])
    def input_part(first, held, gates):
        half = micro // 2
        return pl.pallas_call(
            input_kernel,
            grid_spec=pltpu.PrefetchScalarGridSpec(
                num_scalar_prefetch=1,
                grid=(half,),
                in_specs=[
                    pl.BlockSpec((tile, low_cols), lambda i, at: (i + first, 0)),
                    pl.BlockSpec((tile, high_cols - LANES), lambda i, at: (i + first, 0)),
                    pl.BlockSpec((tile, LANES), lambda i, at: (i + first, 0)),
                    pl.BlockSpec((2 * width, a_cols), lambda i, at: (0, 0)),
                ]
                + [pl.BlockSpec(memory_space=pl.ANY)] * len(held),
                out_specs=[
                    pl.BlockSpec((1, tile, width), lambda i, at: (i + first, at[0], 0)),
                    pl.BlockSpec((tile, width), lambda i, at: (i, 0)),
                ],
            ),
            out_shape=[
                shape((micro, rows_dev, width), f32),
                shape((half * tile, width), bf16),
            ],
            input_output_aliases={5: 0} if held else {},
            compiler_params=params(12),
            name="input",
        )(f.astype(jnp.int32).reshape(1), dpre_low, dpre_high, gates, first_w, *held)

    grad_keep, grad_send = input_part(0, (), after(dgate, next_a))
    grad_got = []
    got_a = jnp.concatenate([got_low, got_high], axis=1)
    sum_a = jnp.concatenate([sum_low, sum_high], axis=1)
    for at in range(1, len(steps)):
        if at > 1:
            got_a = cube.swap(next_a, steps[at])
        if at + 1 < len(steps):
            sum_b, message, side = fold_beside(sum_b, side, after(got_b, next_a))
            got_b = cube.swap(message, steps[at + 1])
            if at == 1:
                early = grad_send
                grad_keep, grad_send = input_part(micro // 2, (grad_keep,), after(dgate, message))
            elif at <= 3:
                grad_got.append(swap_field(after(early if at == 2 else grad_send, message)))
            sum_a, next_a = fold(sum_a, after(got_a, got_b, grad_send))
    side = side + join_two(got_b[got_b.shape[0] - 8 :])
    weights = (expert_in, gate_in, expert_out, tower_in, tower_out)
    velocities = (
        velocity_expert_in,
        velocity_gate_in,
        velocity_expert_out,
        velocity_tower_in,
        velocity_tower_out,
    )
    averages = (
        average_expert_in,
        average_gate_in,
        average_expert_out,
        average_tower_in,
        average_tower_out,
    )
    rates = [base * math.sqrt(total_rows) for base in rate_bases]
    input_grad = pl.pallas_call(
        place_kernel,
        grid_spec=pltpu.PrefetchScalarGridSpec(
            num_scalar_prefetch=1,
            grid=(micro,),
            in_specs=[pl.BlockSpec((rows_own // 2, width), lambda i, at: (0, 0))] * 2
            + [pl.BlockSpec(memory_space=pl.ANY)],
            out_specs=pl.BlockSpec((1, tile, width), lambda i, at: (i, 1 - at[0], 0)),
        ),
        out_shape=shape((micro, rows_dev, width), f32),
        input_output_aliases={3: 0},
        compiler_params=params(8),
        name="place",
    )(f.astype(jnp.int32).reshape(1), *grad_got, after(grad_keep, next_a))
    updated = pl.pallas_call(
        functools.partial(update_kernel, rates),
        out_shape=[shape(w.shape, f32) for w in weights for _ in range(3)],
        compiler_params=params(8),
        name="update",
    )(sum_a, after(got_a, input_grad), sum_b, got_b, side, *weights, *velocities, *averages)
    return (side[0, heads], input_grad, *updated)


def owner_rows(cube, order, r, f, rr, ff, inner, size):
    held = cube.rows * cube.fields // 2
    same = (rr & 1) == (r & 1)
    here = cube.place(order, rr, ff, r, f)
    there = cube.place(order, rr, ff, r ^ 1, f)
    return (jnp.where(same, here, held + there) * size + inner).reshape(-1)


def block_grid(width):
    side = np.arange(2)[:, None, None, None]
    j = np.arange(width // (2 * BLOCK))[None, :, None, None]
    ff = np.arange(2)[None, None, :, None]
    inner = np.arange(BLOCK)[None, None, None, :]
    ahead = (2 * j + side) * BLOCK + 0 * ff + 0 * inner
    full = np.zeros(ahead.shape, np.int32)
    return ahead.astype(np.int32), full + ff.astype(np.int32), full + inner.astype(np.int32)


def first_sorted(cube, order, r, f, width, size):
    ahead, ff, inner = block_grid(width)
    at = ahead + inner
    return owner_rows(
        cube, order, r, f, jnp.asarray(at // size), jnp.asarray(ff), jnp.asarray(at % size), size
    )


def second_sorted(cube, order, r, f, width, size):
    ahead, ff, inner = block_grid(width)
    at = ahead + ff * 8 + inner % 8
    owner = at // size
    held = at % size + size * (inner // 8)
    return owner_rows(
        cube, order, r, f, jnp.asarray(owner // 2), jnp.asarray(owner % 2), jnp.asarray(held), 2 * size
    )


def unsorted(keep, send, rows):
    every = jnp.concatenate([keep, send])
    back = jnp.zeros_like(rows).at[rows].set(jnp.arange(rows.shape[0], dtype=rows.dtype))
    keep, send = jnp.split(jnp.take(every, back, axis=0), 2)
    return keep, send.astype(bf16)


def solution(mesh):
    first = P(("field", "rows"), None)
    second = P(None, ("rows", "field"), None)
    by_row = P(None, "rows")
    inputs = P(None, "rows", "field")
    weights = (first, first, second, second, P())
    return jax.shard_map(
        on_device,
        mesh=mesh,
        in_specs=(inputs, by_row, by_row, by_row) + weights * 3,
        out_specs=(P(), inputs) + tuple(spec for spec in weights for _ in range(3)),
        check_vma=False,
    )
```

```python
import functools
import math

import jax
import jax.numpy as jnp
import numpy as np
from jax import lax
from jax.experimental import pallas as pl
from jax.experimental.pallas import tpu as pltpu
from jax.sharding import PartitionSpec as P

momentum_mu = 0.5
average_keep = 0.5
rate_bases = (17.0, 1.0, 24.0, 4.0, 0.25)
both = ("rows", "field")
f32 = jnp.float32
bf16 = jnp.bfloat16
BLOCK = 16
LANES = 128


def dot(a, b):
    return lax.dot_general(a, b, (((1,), (0,)), ((), ())), preferred_element_type=f32)


def dot_t(a, b):
    return lax.dot_general(a, b, (((1,), (1,)), ((), ())), preferred_element_type=f32)


def t_dot(a, b):
    return lax.dot_general(a, b, (((0,), (0,)), ((), ())), preferred_element_type=f32)


def sigmoid(v):
    return 0.5 + 0.5 * jnp.tanh(0.5 * v)


def rows16(start):
    return pl.ds(pl.multiple_of(start, BLOCK), BLOCK)


class Places:
    def __init__(self, fit, order):
        self.fit, self.order = fit, order

    def bits(self, core, rr, ff):
        out = 0
        for s, (kind, which) in enumerate(self.order):
            if kind == "row":
                bit = (rr >> which) & 1
            else:
                bit = (rr >> 1) & 1 if core == which else ff
            out = out | (bit << s)
        return out

    def start(self):
        r, self.field = lax.axis_index("rows"), lax.axis_index("field")
        self.core = r & 1 if self.fit else jnp.int32(0)
        self.bases = [self.bits(core, r, self.field) for core in range(2)]

    def block(self, side, j):
        core = self.core if side == 0 else 1 - self.core
        pair, ff = j // 2, j % 2
        if not self.fit:
            return j, 2 * pair + side, ff
        ways = [base ^ self.bits(c, 2 * pair, ff) for c, base in enumerate(self.bases)]
        return jnp.where(core == 0, ways[0], ways[1]), 2 * pair + core, ff

    def each(self, pairs, body):
        for j in range(pairs):
            for side in range(2):
                body(side, *self.block(side, j))


def pack_a_kernel(expert_ref, gate_ref, out_ref):
    wide, gates = expert_ref.shape[1], gate_ref.shape[1]
    out_ref[:, 0:wide] = expert_ref[...].astype(bf16)
    out_ref[:, wide:] = jnp.zeros((out_ref.shape[0], LANES), bf16)
    out_ref[:, wide : wide + gates] = gate_ref[...].astype(bf16)


def pack_b_kernel(expert_ref, tower_ref, valid_ref, out_ref):
    experts, rows, out_cols = expert_ref.shape
    part = experts // 2
    for k in range(part):
        both_k = jnp.concatenate([expert_ref[k], expert_ref[k + part]], axis=0)
        out_ref[:, k * out_cols : (k + 1) * out_cols] = both_k.astype(bf16)
    at = part * out_cols
    towers = jnp.concatenate([tower_ref[0], tower_ref[1]], axis=0)
    out_ref[:, at : at + LANES] = towers.astype(bf16)
    tile = valid_ref.shape[1] // 2
    own = valid_ref[:, pl.ds(pl.multiple_of(lax.axis_index("field") * tile, tile), tile)].astype(f32)
    ones = jnp.sum(jnp.sum(own, axis=1, keepdims=True), axis=0, keepdims=True).astype(jnp.int32)
    ones = jnp.broadcast_to(ones, (2 * rows, LANES))
    row, lane = (lax.broadcasted_iota(jnp.int32, ones.shape, d) for d in range(2))
    digits = jnp.where(lane == 2, ones >> 16, jnp.where(lane == 1, ones >> 8, ones) & 255)
    digits = jnp.where((row == 0) & (lane < 3), digits, 0).astype(f32)
    out_ref[:, at + LANES :] = digits.astype(bf16)


def rows_kernel(in_ref, got_ref, valid_ref, label_ref, domain_ref, x_ref, xt_ref, flags_ref, by_row_ref):
    micro, rows_dev, width = in_ref.shape
    tile = rows_dev // 2
    start = pl.multiple_of(lax.axis_index("field") * tile, tile)
    for m in range(micro):
        rows = slice(m * tile, (m + 1) * tile)
        x = jnp.concatenate([in_ref[m, pl.ds(start, tile), :], got_ref[rows, :]], axis=1)
        x_ref[rows, :] = x
        xt_ref[:, rows] = x.T
        kinds = [ref[m : m + 1, pl.ds(start, tile)].astype(f32) for ref in (valid_ref, label_ref, domain_ref)]
        flags = jnp.concatenate(kinds + [jnp.zeros((5, tile), f32)], axis=0)
        flags_ref[:, rows] = flags
        by_row_ref[rows, :] = flags.T


def first_kernel(places, own_ref, oth_ref, x_ref, xt_ref, flags_ref, ga_ref, gs_ref, gate_ref, w_ref):
    half = own_ref.shape[0]
    count, wide = ga_ref.shape
    experts = wide // half
    tile = count // 4
    places.start()

    def put(side, place, rr, ff):
        src = own_ref if side == 0 else oth_ref
        row = (ff ^ places.field) * half + rr * BLOCK
        w_ref[rows16(row), :] = src[rows16(place * BLOCK), :]

    places.each(half // BLOCK, put)
    logits = dot(w_ref[:, wide:].T, xt_ref[...])
    logits = jnp.where(flags_ref[2:3, :] == 0.0, logits[0:experts], logits[experts : 2 * experts])
    raised = jnp.exp(logits - jnp.max(logits, axis=0, keepdims=True))
    gate = raised / jnp.sum(raised, axis=0, keepdims=True)
    gate_ref[...] = jnp.concatenate([gate, gate], axis=0).T

    for i in range(4):
        rows = slice(i * tile, (i + 1) * tile)
        x = x_ref[rows, :]
        gate = 0.5 * gate_ref[rows, :]
        for k in range(experts):
            cols = slice(k * half, (k + 1) * half)
            pre = dot(x, w_ref[:, cols])
            low = 0.5 * pre
            up = 1.0 + jnp.tanh(low)
            scaled = gate[:, k : k + 1] * up
            ga_ref[rows, cols] = (scaled * pre).astype(bf16)
            gs_ref[rows, cols] = (scaled * (1.0 + pre - low * up)).astype(bf16)


def second_kernel(
    places,
    own_ref,
    oth_ref,
    ga_ref,
    flags_ref,
    by_row_ref,
    to_ref,
    w_ref,
    dm_ref,
    side_ref,
    keep_ref,
    send_ref,
    ti_ref,
    mix_ref,
    g_ref,
    gti_ref,
):
    half = own_ref.shape[0]
    pairs = half // BLOCK
    count, out_cols = dm_ref.shape
    hidden = half
    wide = ga_ref.shape[1]
    experts = wide // hidden
    part = experts // 2

    places.start()

    digits = jnp.zeros((BLOCK, LANES), f32)
    for side in range(2):
        for j in range(pairs // 2):
            src = own_ref if side == 0 else oth_ref
            (place0, rr, _), (place1, _, _) = places.block(side, 2 * j), places.block(side, 2 * j + 1)
            a0 = src[rows16(place0 * BLOCK), :].astype(f32)
            a1 = src[rows16(place1 * BLOCK), :].astype(f32)
            row = rr * BLOCK
            upper = jnp.concatenate([a0[:8], a1[:8]], axis=0).astype(bf16)
            lower = jnp.concatenate([a0[8:], a1[8:]], axis=0).astype(bf16)
            at = part * out_cols
            for k in range(part):
                cols = slice(k * out_cols, (k + 1) * out_cols)
                w_ref[rows16(k * hidden + row), :] = upper[:, cols]
                w_ref[rows16((k + part) * hidden + row), :] = lower[:, cols]
            ti_ref[rows16(row), 0:LANES] = upper[:, at : at + LANES]
            ti_ref[rows16(row), LANES : 2 * LANES] = lower[:, at : at + LANES]
            digits = digits + (a0 + a1)[:, at + LANES :]
    lane = lax.broadcasted_iota(jnp.int32, digits.shape, 1)
    scale = jnp.where(lane == 0, 1.0, jnp.where(lane == 1, 256.0, jnp.where(lane == 2, 65536.0, 0.0)))
    real = jnp.sum(jnp.sum(digits * scale, axis=1, keepdims=True), axis=0, keepdims=True)

    domain = by_row_ref[:, 2:3]
    heads = to_ref[...].astype(bf16).astype(f32)
    empty = jnp.zeros((6, LANES), f32)
    tile = count // 4
    for i in range(4):
        rows = slice(i * tile, (i + 1) * tile)
        mix_ref[rows, :] = dot(ga_ref[rows, :], w_ref[...]).astype(bf16)
    mixed = mix_ref[...]
    tpre = dot(mixed, ti_ref[...])
    tpre = jnp.where(domain == 0.0, tpre[:, :LANES], tpre[:, LANES:])
    s = sigmoid(tpre)
    act = (tpre * s).astype(bf16)
    logits = dot_t(jnp.concatenate([heads, empty], axis=0).astype(bf16), act)
    valid, label, first = flags_ref[0:1, :], flags_ref[1:2, :], flags_ref[2:3, :] == 0.0
    chosen = jnp.where(first, logits[0:1, :], logits[1:2, :])
    soft = jnp.maximum(chosen, 0.0) + jnp.log1p(jnp.exp(-jnp.abs(chosen)))
    loss = jnp.sum(valid * (soft - label * chosen), axis=1, keepdims=True) / real
    dlogit = valid * (sigmoid(chosen) - label) / real
    dlogit = jnp.concatenate(
        [jnp.where(first, dlogit, 0.0), jnp.where(first, 0.0, dlogit), jnp.zeros((6, count), f32)], axis=0
    ).astype(bf16)
    apart = jnp.concatenate(
        [
            jnp.concatenate([heads[0:1], jnp.zeros((1, LANES), f32)], axis=1),
            jnp.concatenate([jnp.zeros((1, LANES), f32), heads[1:2]], axis=1),
            jnp.concatenate([empty, empty], axis=1),
        ],
        axis=0,
    ).astype(bf16)
    slope = s * (1.0 + tpre * (1.0 - s))
    dtpre = (t_dot(dlogit, apart) * jnp.concatenate([slope, slope], axis=1)).astype(bf16)
    dm_ref[...] = dot_t(dtpre, ti_ref[...]).astype(bf16)
    head_grad = dot(dlogit, act)
    side_ref[...] = jnp.zeros_like(side_ref)
    side_ref[0:1, 0:LANES] = head_grad[0:1]
    side_ref[0:1, LANES : 2 * LANES] = head_grad[1:2]
    side_ref[0:1, 2 * LANES : 3 * LANES] = jnp.broadcast_to(loss, (1, LANES))
    gti_ref[...] = t_dot(mixed, dtpre)

    def pack(above, below, cols):
        def put(side, place, rr, ff):
            dst = keep_ref if side == 0 else send_ref
            row = pl.ds(pl.multiple_of(rr * BLOCK + ff * 8, 8), 8)
            tile = jnp.concatenate([above(row), below(row)], axis=0)
            dst[rows16(place * BLOCK), cols] = tile.astype(dst.dtype)

        places.each(pairs, put)

    for k in range(part):
        g_ref[k] = t_dot(ga_ref[:, k * hidden : (k + 1) * hidden], dm_ref[...])
        g_ref[k + part] = t_dot(ga_ref[:, (k + part) * hidden : (k + part + 1) * hidden], dm_ref[...])
        pack(
            lambda row: g_ref[k, row, :],
            lambda row: g_ref[k + part, row, :],
            slice(k * out_cols, (k + 1) * out_cols),
        )
    at = part * out_cols
    pack(lambda row: gti_ref[row, 0:LANES], lambda row: gti_ref[row, LANES : 2 * LANES], slice(at, at + LANES))


def back_part(places, ks, w_ref, dm_ref, ga_ref, gs_ref, xt_ref, dp_ref, keep_ref, send_ref, g_ref):
    half = keep_ref.shape[0]
    tile = dm_ref.shape[0] // 2
    places.start()

    def weights(at):
        here = slice(at * half, (at + 1) * half)
        g_ref[:, here] = dot(xt_ref[...], dp_ref[:, here])
        back_pack(places, here, keep_ref, send_ref, g_ref)

    terms = []
    for at, k in enumerate(ks):
        cols, here = slice(k * half, (k + 1) * half), slice(at * half, (at + 1) * half)
        sums = []
        for i in range(2):
            rows = slice(i * tile, (i + 1) * tile)
            u = dot_t(dm_ref[rows, :], w_ref[cols, :])
            dp_ref[rows, here] = (u * gs_ref[rows, cols].astype(f32)).astype(bf16)
            sums.append(jnp.sum(u * ga_ref[rows, cols].astype(f32), axis=1, keepdims=True))
        terms.append(sums)
        if at:
            weights(at - 1)
    weights(len(ks) - 1)
    return terms


def back_pack(places, cols, keep_ref, send_ref, g_ref):
    half = keep_ref.shape[0]

    def put(side, place, rr, ff):
        dst = keep_ref if side == 0 else send_ref
        row = (ff ^ places.field) * half + rr * BLOCK
        dst[rows16(place * BLOCK), cols] = g_ref[rows16(row), cols].astype(dst.dtype)

    places.each(half // BLOCK, put)


def set_terms(q_ref, terms, ks):
    tile = q_ref.shape[0] // 2
    experts = q_ref.shape[1] // 2
    lane = lax.broadcasted_iota(jnp.int32, (tile, 2 * experts), 1)
    for i in range(2):
        rows = slice(i * tile, (i + 1) * tile)
        q = q_ref[rows, :]
        for k, sums in zip(ks, terms):
            q = jnp.where((lane == k) | (lane == k + experts), sums[i], q)
        q_ref[rows, :] = q


def back_first_kernel(
    places, ks, w_ref, dm_ref, ga_ref, gs_ref, xt_ref, dp_ref, keep_ref, send_ref, q_ref, g_ref
):
    terms = back_part(places, ks, w_ref, dm_ref, ga_ref, gs_ref, xt_ref, dp_ref, keep_ref, send_ref, g_ref)
    q_ref[...] = jnp.zeros_like(q_ref)
    set_terms(q_ref, terms, ks)


def back_last_kernel(
    places,
    ks,
    w_ref,
    dm_ref,
    ga_ref,
    gs_ref,
    xt_ref,
    before_ref,
    gate_ref,
    by_row_ref,
    dp_ref,
    keep_ref,
    send_ref,
    dg_ref,
    g_ref,
    q_ref,
):
    terms = back_part(places, ks, w_ref, dm_ref, ga_ref, gs_ref, xt_ref, dp_ref, keep_ref, send_ref, g_ref)
    q_ref[...] = before_ref[...]
    set_terms(q_ref, terms, ks)
    q = q_ref[...]
    experts = q.shape[1] // 2
    lane = lax.broadcasted_iota(jnp.int32, q.shape, 1)
    total = 0.5 * jnp.sum(q, axis=1, keepdims=True)
    mine = (lane // experts).astype(f32) == by_row_ref[:, 2:3]
    dg_ref[...] = jnp.zeros_like(dg_ref)
    dg_ref[:, 0 : 2 * experts] = jnp.where(mine, q - gate_ref[...] * total, 0.0).astype(bf16)
    cols = slice(dp_ref.shape[1], dp_ref.shape[1] + LANES)
    g_ref[:, cols] = dot(xt_ref[...], dg_ref[...])
    back_pack(places, cols, keep_ref, send_ref, g_ref)


def input_kernel(at, low_ref, high_ref, dg_ref, w_ref, *refs):
    keep_ref, send_ref = refs[-2:]
    part = low_ref.shape[1]
    wide = part + high_ref.shape[1]
    grad = dot_t(low_ref[...], w_ref[:, 0:part]) + dot_t(high_ref[...], w_ref[:, part:wide])
    grad = grad + dot_t(dg_ref[...], w_ref[:, wide:])
    half = grad.shape[1] // 2
    keep_ref[0] = grad[:, :half]
    send_ref[...] = grad[:, half:].astype(bf16)


def place_kernel(at, early_ref, late_ref, held_ref, out_ref):
    tile = out_ref.shape[1]
    half = pl.num_programs(0) // 2
    m = pl.program_id(0)

    @pl.when(m < half)
    def _():
        out_ref[0] = early_ref[pl.ds(pl.multiple_of(m * tile, tile), tile), :].astype(f32)

    @pl.when(m >= half)
    def _():
        out_ref[0] = late_ref[pl.ds(pl.multiple_of((m - half) * tile, tile), tile), :].astype(f32)


def update_kernel(rates, sum_a, got_a, sum_b, got_b, side, *refs):
    weights, velocities, averages, outs = refs[0:5], refs[5:10], refs[10:15], refs[15:30]
    wide, gates = weights[0].shape[1], weights[1].shape[1]
    experts, rows, out_cols = weights[2].shape
    tasks = weights[3].shape[0]
    part = experts // 2

    def renew(at, place, gradient):
        velocity = momentum_mu * velocities[at][place] + gradient
        weight = weights[at][place] - rates[at] * (gradient + momentum_mu * velocity)
        outs[3 * at][place] = weight
        outs[3 * at + 1][place] = velocity
        outs[3 * at + 2][place] = average_keep * averages[at][place] + (1.0 - average_keep) * weight

    first = sum_a[0 : got_a.shape[0], :] + got_a[...].astype(f32)
    renew(0, (slice(None), slice(None)), first[:, :wide])
    renew(1, (slice(None), slice(None)), first[:, wide : wide + gates])
    count = got_b.shape[0] - 8
    second = sum_b[0:count, :] + got_b[0:count, :].astype(f32)
    for k in range(experts):
        top = (k // part) * rows
        renew(2, k, second[top : top + rows, (k % part) * out_cols : (k % part + 1) * out_cols])
    for t in range(tasks):
        renew(3, t, second[t * rows : (t + 1) * rows, part * out_cols :])
        renew(4, (slice(t, t + 1), slice(None)), side[0:1, t * LANES : (t + 1) * LANES])


class Cube:
    def __init__(self):
        self.rows = lax.axis_size("rows")
        self.fields = lax.axis_size("field")
        bits = int(math.log2(self.rows))
        assert 1 << bits == self.rows and self.fields == 2
        outer = [("row", b) for b in range(bits - 1, 1, -1)]
        self.order = outer + [("mixed", 0), ("mixed", 1)]
        self.other_order = outer + [("mixed", 1), ("mixed", 0)]
        self.core = ("row", 0)

    def pairs(self, step):
        kind, which = step
        pairs = []
        for r in range(self.rows):
            for f in range(self.fields):
                if kind == "row":
                    to = (r ^ (1 << which), f)
                else:
                    to = (r ^ 2, f) if (r & 1) == which else (r, f ^ 1)
                pairs.append((r * self.fields + f, to[0] * self.fields + to[1]))
        return pairs

    def swap(self, values, step):
        return lax.ppermute(values, both, self.pairs(step))

    def place(self, order, rr, ff, r, f):
        dr, df, core = rr ^ r, ff ^ f, r & 1
        out = jnp.zeros_like(dr + df)
        for s, (kind, which) in enumerate(order):
            if kind == "row":
                bit = (dr >> which) & 1
            else:
                bit = jnp.where(core == which, (dr >> 1) & 1, df)
            out = out + (bit << s)
        return out


def gather_two(cube, block_a, make_b, make_x):
    got_a = cube.swap(block_a, cube.order[0])
    x = make_x(block_a)
    block_a = jnp.concatenate([block_a, got_a], axis=0)
    block_b = make_b(block_a)
    for at in range(1, len(cube.order)):
        got_a = cube.swap(block_a, cube.order[at])
        got_b = cube.swap(block_b, cube.order[at - 1])
        if at + 1 == len(cube.order):
            got_a = after(got_a, x[0])
        block_a = jnp.concatenate([block_a, after(got_a, got_b if at > 1 else block_b)], axis=0)
        block_b = jnp.concatenate([block_b, after(got_b, block_a)], axis=0)
    oth_a = cube.swap(block_a, cube.core)
    return block_a, oth_a, block_b, cube.swap(block_b, cube.order[-1]), x


def after(values, *earlier):
    return lax.optimization_barrier((values,) + earlier)[0]


def fold(total, got):
    rows = got.shape[0]
    total = total[:rows] + got.astype(f32)
    half = rows // 2
    return total, total[half:].astype(bf16)


def split_two(values):
    high = lax.reduce_precision(values, 8, 7)
    low = lax.reduce_precision(values - high, 8, 7)
    return jnp.concatenate([high, low], axis=0).astype(bf16)


def join_two(rows):
    rows = rows.astype(f32)
    half = rows.shape[0] // 2
    return rows[:half] + rows[half:]


def beside(part, side):
    mine = split_two(side)
    return jnp.concatenate([part, mine], axis=0), join_two(mine)


def fold_beside(total, side, got):
    rows = got.shape[0] - 8
    total, part = fold(total, got[:rows])
    message, side = beside(part, side + join_two(got[rows:]))
    return total, message, side


def shape(dims, dtype):
    return jax.ShapeDtypeStruct(dims, dtype)


def params(limit):
    return pltpu.CompilerParams(vmem_limit_bytes=limit << 20)


vmem = pl.BlockSpec()


def cost(flops):
    return pl.CostEstimate(flops=flops, bytes_accessed=8 << 20, transcendentals=0)


def on_device(
    inputs,
    valid_mask,
    labels,
    domains,
    expert_in,
    gate_in,
    expert_out,
    tower_in,
    tower_out,
    velocity_expert_in,
    velocity_gate_in,
    velocity_expert_out,
    velocity_tower_in,
    velocity_tower_out,
    average_expert_in,
    average_gate_in,
    average_expert_out,
    average_tower_in,
    average_tower_out,
):
    cube = Cube()
    micro, rows_dev, width = inputs.shape
    fields = cube.fields
    tile = rows_dev // fields
    rows_own = micro * tile
    experts, second_rows, out_cols = expert_out.shape
    tasks, tower_cols = tower_out.shape
    wide = expert_in.shape[1]
    hidden = wide // experts
    first_rows = expert_in.shape[0]
    part = experts // 2
    total_rows = micro * rows_dev * cube.rows
    r, f = lax.axis_index("rows"), lax.axis_index("field")

    def swap_field(values):
        return lax.ppermute(values, "field", [(0, 1), (1, 0)])

    def own_half(values, which):
        return lax.dynamic_slice_in_dim(values, which * tile, tile, 1)

    block_a = pl.pallas_call(
        pack_a_kernel,
        out_shape=shape((first_rows, wide + LANES), bf16),
        compiler_params=params(4),
        name="pack_a",
    )(expert_in, gate_in)

    def make_b(earlier):
        return pl.pallas_call(
            pack_b_kernel,
            out_shape=shape((2 * second_rows, part * out_cols + 2 * LANES), bf16),
            compiler_params=params(4),
            name="pack_b",
        )(expert_out, tower_in, after(valid_mask, earlier))


    def send_x(earlier):
        return swap_field(own_half(after(inputs, earlier), 1 - f).reshape(rows_own, width))


    pairs = width // BLOCK
    fit = first_rows == BLOCK
    places = Places(fit, cube.order)
    sent = bf16 if fit else f32

    a_cols, b_cols = wide + LANES, part * out_cols + LANES
    heads = tasks * tower_cols

    def make_x(earlier):
        x_got = send_x(earlier)
        return pl.pallas_call(
            rows_kernel,
            out_shape=[
                shape((rows_own, 2 * width), bf16),
                shape((2 * width, rows_own), bf16),
                shape((8, rows_own), f32),
                shape((rows_own, 8), f32),
            ],
            compiler_params=params(8),
            cost_estimate=cost(1 << 20),
            name="rows",
        )(inputs, x_got, valid_mask, labels, domains)

    own_a, oth_a, own_b, got_b, (x, x_t, flags, by_row) = gather_two(cube, block_a, make_b, make_x)
    if not fit:
        rows_a = first_sorted(cube, cube.order, r, f, width, first_rows)
        own_a, oth_a = jnp.split(jnp.take(jnp.concatenate([own_a, oth_a]), rows_a, axis=0), 2)
    ga, gs, gate, first_w = pl.pallas_call(
        functools.partial(first_kernel, places),
        out_shape=[
            shape((rows_own, wide), bf16),
            shape((rows_own, wide), bf16),
            shape((rows_own, tasks * experts), f32),
            shape((2 * width, a_cols), bf16),
        ],
        compiler_params=params(12),
        cost_estimate=cost(4 * rows_own * 2 * width * a_cols),
        name="first",
    )(own_a, oth_a, x, x_t, flags)

    own_b = jnp.concatenate([own_b, after(got_b, gate)], axis=0)
    oth_b = cube.swap(own_b, cube.core)
    if not fit:
        rows_b = second_sorted(cube, cube.order, r, f, width, second_rows)
        own_b, oth_b = jnp.split(jnp.take(jnp.concatenate([own_b, oth_b]), rows_b, axis=0), 2)
    second_w, dmixed, side, keep_b, send_b = pl.pallas_call(
        functools.partial(second_kernel, places),
        out_shape=[
            shape((wide, out_cols), bf16),
            shape((rows_own, out_cols), bf16),
            shape((8, b_cols), f32),
            shape((width, b_cols), f32),
            shape((width, b_cols), sent),
        ],
        scratch_shapes=[
            pltpu.VMEM((out_cols, heads), bf16),
            pltpu.VMEM((rows_own, out_cols), bf16),
            pltpu.VMEM((experts, hidden, out_cols), f32),
            pltpu.VMEM((out_cols, heads), f32),
        ],
        compiler_params=params(20),
        name="second",
    )(own_b, oth_b, ga, flags, by_row, tower_out)
    if not fit:
        keep_b, send_b = unsorted(keep_b, send_b, rows_b)
    message, side = beside(send_b, side[:4])
    steps = [cube.core] + cube.order[::-1]
    got_b = cube.swap(message, steps[0])

    cut = 6
    low_cols, high_cols = cut * hidden, (experts - cut) * hidden + LANES
    dpre_low, keep_low, send_low, terms = pl.pallas_call(
        functools.partial(back_first_kernel, places, range(cut)),
        out_shape=[
            shape((rows_own, low_cols), bf16),
            shape((width, low_cols), f32),
            shape((width, low_cols), sent),
            shape((rows_own, tasks * experts), f32),
        ],
        scratch_shapes=[pltpu.VMEM((2 * width, low_cols), f32)],
        compiler_params=params(16),
        name="back_first",
    )(after(second_w, message), dmixed, ga, gs, x_t)
    if not fit:
        keep_low, send_low = unsorted(keep_low, send_low, rows_a)
    got_low = cube.swap(send_low, steps[0])
    sum_b, message, side = fold_beside(keep_b, side, after(got_b, send_low))
    got_b = cube.swap(message, steps[1])
    dpre_high, keep_high, send_high, dgate = pl.pallas_call(
        functools.partial(back_last_kernel, places, range(cut, experts)),
        out_shape=[
            shape((rows_own, high_cols - LANES), bf16),
            shape((width, high_cols), f32),
            shape((width, high_cols), sent),
            shape((rows_own, LANES), bf16),
        ],
        scratch_shapes=[
            pltpu.VMEM((2 * width, high_cols), f32),
            pltpu.VMEM((rows_own, tasks * experts), f32),
        ],
        compiler_params=params(16),
        name="back_last",
    )(second_w, dmixed, ga, gs, x_t, after(terms, message), gate, by_row)
    if not fit:
        keep_high, send_high = unsorted(keep_high, send_high, rows_a)
    got_high = cube.swap(send_high, steps[0])
    sum_low, next_low = fold(keep_low, after(got_low, send_high))
    got_low = cube.swap(next_low, steps[1])
    sum_high, next_a = fold(keep_high, after(got_high, next_low))
    got_high = cube.swap(next_a, steps[1])
    def input_part(first, held, gates):
        half = micro // 2
        return pl.pallas_call(
            input_kernel,
            grid_spec=pltpu.PrefetchScalarGridSpec(
                num_scalar_prefetch=1,
                grid=(half,),
                in_specs=[
                    pl.BlockSpec((tile, low_cols), lambda i, at: (i + first, 0)),
                    pl.BlockSpec((tile, high_cols - LANES), lambda i, at: (i + first, 0)),
                    pl.BlockSpec((tile, LANES), lambda i, at: (i + first, 0)),
                    pl.BlockSpec((2 * width, a_cols), lambda i, at: (0, 0)),
                ]
                + [pl.BlockSpec(memory_space=pl.ANY)] * len(held),
                out_specs=[
                    pl.BlockSpec((1, tile, width), lambda i, at: (i + first, at[0], 0)),
                    pl.BlockSpec((tile, width), lambda i, at: (i, 0)),
                ],
            ),
            out_shape=[
                shape((micro, rows_dev, width), f32),
                shape((half * tile, width), bf16),
            ],
            input_output_aliases={5: 0} if held else {},
            compiler_params=params(12),
            name="input",
        )(f.astype(jnp.int32).reshape(1), dpre_low, dpre_high, gates, first_w, *held)

    grad_keep, grad_send = input_part(0, (), after(dgate, next_a))
    grad_got = []
    got_a = jnp.concatenate([got_low, got_high], axis=1)
    sum_a = jnp.concatenate([sum_low, sum_high], axis=1)
    for at in range(1, len(steps)):
        if at > 1:
            got_a = cube.swap(next_a, steps[at])
        if at + 1 < len(steps):
            sum_b, message, side = fold_beside(sum_b, side, after(got_b, next_a))
            got_b = cube.swap(message, steps[at + 1])
            if at == 1:
                early = grad_send
                grad_keep, grad_send = input_part(micro // 2, (grad_keep,), after(dgate, message))
            elif at <= 3:
                grad_got.append(swap_field(after(early if at == 2 else grad_send, message)))
            sum_a, next_a = fold(sum_a, after(got_a, got_b, grad_send))
    side = side + join_two(got_b[got_b.shape[0] - 8 :])
    weights = (expert_in, gate_in, expert_out, tower_in, tower_out)
    velocities = (
        velocity_expert_in,
        velocity_gate_in,
        velocity_expert_out,
        velocity_tower_in,
        velocity_tower_out,
    )
    averages = (
        average_expert_in,
        average_gate_in,
        average_expert_out,
        average_tower_in,
        average_tower_out,
    )
    rates = [base * math.sqrt(total_rows) for base in rate_bases]
    input_grad = pl.pallas_call(
        place_kernel,
        grid_spec=pltpu.PrefetchScalarGridSpec(
            num_scalar_prefetch=1,
            grid=(micro,),
            in_specs=[pl.BlockSpec((rows_own // 2, width), lambda i, at: (0, 0))] * 2
            + [pl.BlockSpec(memory_space=pl.ANY)],
            out_specs=pl.BlockSpec((1, tile, width), lambda i, at: (i, 1 - at[0], 0)),
        ),
        out_shape=shape((micro, rows_dev, width), f32),
        input_output_aliases={3: 0},
        compiler_params=params(8),
        name="place",
    )(f.astype(jnp.int32).reshape(1), *grad_got, after(grad_keep, next_a))
    updated = pl.pallas_call(
        functools.partial(update_kernel, rates),
        out_shape=[shape(w.shape, f32) for w in weights for _ in range(3)],
        compiler_params=params(8),
        name="update",
    )(sum_a, after(got_a, input_grad), sum_b, got_b, side, *weights, *velocities, *averages)
    return (side[0, heads], input_grad, *updated)


def owner_rows(cube, order, r, f, rr, ff, inner, size):
    held = cube.rows * cube.fields // 2
    same = (rr & 1) == (r & 1)
    here = cube.place(order, rr, ff, r, f)
    there = cube.place(order, rr, ff, r ^ 1, f)
    return (jnp.where(same, here, held + there) * size + inner).reshape(-1)


def block_grid(width):
    side = np.arange(2)[:, None, None, None]
    j = np.arange(width // (2 * BLOCK))[None, :, None, None]
    ff = np.arange(2)[None, None, :, None]
    inner = np.arange(BLOCK)[None, None, None, :]
    ahead = (2 * j + side) * BLOCK + 0 * ff + 0 * inner
    full = np.zeros(ahead.shape, np.int32)
    return ahead.astype(np.int32), full + ff.astype(np.int32), full + inner.astype(np.int32)


def first_sorted(cube, order, r, f, width, size):
    ahead, ff, inner = block_grid(width)
    at = ahead + inner
    return owner_rows(
        cube, order, r, f, jnp.asarray(at // size), jnp.asarray(ff), jnp.asarray(at % size), size
    )


def second_sorted(cube, order, r, f, width, size):
    ahead, ff, inner = block_grid(width)
    at = ahead + ff * 8 + inner % 8
    owner = at // size
    held = at % size + size * (inner // 8)
    return owner_rows(
        cube, order, r, f, jnp.asarray(owner // 2), jnp.asarray(owner % 2), jnp.asarray(held), 2 * size
    )


def unsorted(keep, send, rows):
    every = jnp.concatenate([keep, send])
    back = jnp.zeros_like(rows).at[rows].set(jnp.arange(rows.shape[0], dtype=rows.dtype))
    keep, send = jnp.split(jnp.take(every, back, axis=0), 2)
    return keep, send.astype(bf16)


def solution(mesh):
    first = P(("field", "rows"), None)
    second = P(None, ("rows", "field"), None)
    by_row = P(None, "rows")
    inputs = P(None, "rows", "field")
    weights = (first, first, second, second, P())
    return jax.shard_map(
        on_device,
        mesh=mesh,
        in_specs=(inputs, by_row, by_row, by_row) + weights * 3,
        out_specs=(P(), inputs) + tuple(spec for spec in weights for _ in range(3)),
        check_vma=False,
    )
```
